32 devices in a mesh: sub: 8 (over z, core), row: 4 (over y, x).
Axes of the slice: x: 2, y: 2, z: 4, core: 2. Of those that a mesh axis runs over, the one named last changes fastest.
Arguments:
- modes: float32 [24576, 64], P(('sub', 'row')), may hold values from -6 to 6
- search: float32 [24576, 64], P(('sub', 'row')), may hold values from -6 to 6
- precond: float32 [24576], P(('sub', 'row')), may hold values from 0.05 to 0.25
- in_row: int32 [8, 4, 96], P('sub', 'row'), may hold values from 0 to 11, as said below
- in_col: int32 [8, 4, 96], P('sub', 'row'), may hold values from 0 to 47, as said below
- in_val: bfloat16 [8, 4, 96, 64, 64], P('sub', 'row'), as said below
- bnd_rows: int32 [8, 4, 3], P('sub', 'row'), may hold values from 0 to 11, as said below
- if_row: int32 [8, 4, 12], P('sub', 'row'), may hold values from 0 to 11, as said below
- if_src: int32 [8, 4, 12], P('sub', 'row'), may hold values from 0 to 23, as said below
- if_val: bfloat16 [8, 4, 12, 64, 64], P('sub', 'row')
Outputs:
- modes_out: float32 [24576, 64], P(('sub', 'row'))
- search_out: float32 [24576, 64], P(('sub', 'row'))
The draws below stay inside these ranges and needn't reach their ends.
Inputs may be any that keep to these rules, and one draw needn't show every extreme that they name: `in_row`: entry k < 12 is k; each later group of 12 entries names each of the device's block-rows once. `in_col`: entry k < 12 is r * 12 + k on device (s, r); in each later group of 12 entries the devices of a subdomain together name each of its 48 block-rows once, and no entry names its own block-row. `in_val`: the first 12 blocks of every device are symmetric; the operator A is symmetric positive definite. `bnd_rows`: distinct within a device. `if_row`: each of the device's 12 block-rows once. `if_src`: t * 3 + q with t never the device's own subdomain; among the devices with one index of row, each boundary slot of each subdomain is named exactly 4 times.
All inputs are finite; a program needn't handle non-finite values.
Results may differ from the reference program's by a relative error of at most 0.0006.
Values may be sent and summed in bfloat16 or wider, within the bound.
No kernel may reach another device: no remote copies, remote signals or barrier semaphores. Data moves between devices by JAX's collectives and lax.ppermute only.
A program may use at most 128 MiB of HBM per device.

```python
import math
import jax
import jax.numpy as jnp
from jax import lax

NMODE = 64
KB = 64
LB = 12
ITERS = 2
NIN = 96
IFR = 3
NIF = 12
SUBB = 48
ROWS = 24576
N_SUB = 8
N_ROW = 4


def intra_pattern(key):
    base = jax.random.fold_in(key, 11)
    first_key, second_key = jax.random.split(base)
    groups = NIN // LB - 1
    ladder = jnp.broadcast_to(jnp.arange(LB, dtype=jnp.int32), (N_SUB, N_ROW, groups, LB))
    rows_extra = jax.random.permutation(first_key, ladder, axis=-1, independent=True).astype(jnp.int32)
    shifts = jax.random.randint(second_key, (N_SUB, 1, groups, 1), 1, SUBB).astype(jnp.int32)
    owner = jnp.arange(N_ROW, dtype=jnp.int32)[None, :, None, None] * LB
    cols_extra = ((owner + rows_extra + shifts) % SUBB).astype(jnp.int32)
    diagonal_rows = jnp.broadcast_to(jnp.arange(LB, dtype=jnp.int32)[None, None, :], (N_SUB, N_ROW, LB))
    rows_all = jnp.concatenate([diagonal_rows, rows_extra.reshape(N_SUB, N_ROW, groups * LB)], -1)
    cols_all = jnp.concatenate([owner[..., 0] + diagonal_rows, cols_extra.reshape(N_SUB, N_ROW, groups * LB)], -1)
    return (rows_all.astype(jnp.int32), cols_all.astype(jnp.int32))


def draw_in_row(key, part):
    return intra_pattern(key)[0]


def draw_in_col(key, part):
    return intra_pattern(key)[1]


def draw_in_val(key, part):
    base = jax.random.fold_in(key, 23)
    first_key, second_key, third_key = jax.random.split(base, 3)
    spread = 0.5 / KB
    raw = jax.random.uniform(first_key, (N_SUB, N_ROW, NIN, KB, KB), jnp.float32, -spread, spread)
    level = jax.random.uniform(second_key, (N_SUB, N_ROW, NIN, KB), jnp.float32, 2.0, 6.0)
    coupling = jnp.exp(jax.random.uniform(third_key, (N_SUB, N_ROW, NIN, 1, 1), jnp.float32, math.log(0.25), math.log(1.0)))
    identity = (jnp.arange(KB)[:, None] == jnp.arange(KB)[None, :]).astype(jnp.float32)
    symmetric = 0.5 * (raw + jnp.swapaxes(raw, -1, -2)) + identity * (36.0 + level[..., None])
    off_block = raw - identity * coupling
    is_diag = (jnp.arange(NIN) < LB)[None, None, :, None, None]
    return jnp.where(is_diag, symmetric, off_block).astype(jnp.bfloat16)


def draw_bnd_rows(key, part):
    base = jax.random.fold_in(key, 37)
    scores = jax.random.randint(base, (N_SUB, N_ROW, LB), 0, 1 << 20) * LB + jnp.arange(LB, dtype=jnp.int32)
    order = jnp.argsort(scores, axis=-1)
    return order[..., :IFR].astype(jnp.int32)


def draw_if_row(key, part):
    base = jax.random.fold_in(key, 47)
    ladder = jnp.broadcast_to(jnp.arange(LB, dtype=jnp.int32), (N_SUB, N_ROW, NIF))
    return jax.random.permutation(base, ladder, axis=-1, independent=True).astype(jnp.int32)


def draw_if_src(key, part):
    base = jax.random.fold_in(key, 41)
    first_key, second_key = jax.random.split(base)
    quarters = NIF // IFR
    shift_by = jax.random.randint(first_key, (1, N_ROW, quarters, IFR), 1, N_SUB).astype(jnp.int32)
    own_sub = jnp.arange(N_SUB, dtype=jnp.int32)[:, None, None, None]
    target = (own_sub + shift_by) % N_SUB
    ladder = jnp.broadcast_to(jnp.arange(IFR, dtype=jnp.int32), (1, N_ROW, quarters, IFR))
    slot_ids = jax.random.permutation(second_key, ladder, axis=-1, independent=True).astype(jnp.int32)
    return (target * IFR + slot_ids).reshape(N_SUB, N_ROW, NIF).astype(jnp.int32)


def draw_if_val(key, part):
    base = jax.random.fold_in(key, 53)
    first_key, second_key = jax.random.split(base)
    spread = 0.5 / KB
    raw = jax.random.uniform(first_key, (N_SUB, N_ROW, NIF, KB, KB), jnp.float32, -spread, spread)
    coupling = jnp.exp(jax.random.uniform(second_key, (N_SUB, N_ROW, NIF, 1, 1), jnp.float32, math.log(0.75), math.log(2.0)))
    identity = (jnp.arange(KB)[:, None] == jnp.arange(KB)[None, :]).astype(jnp.float32)
    return (raw - identity * coupling).astype(jnp.bfloat16)


def level_of(key, extent, cuts, low, top_value):
    loudness = 1.0
    for position, parts in cuts:
        draws = jax.random.uniform(jax.random.fold_in(jax.random.fold_in(key, 6), position), (parts,), jnp.float32, low / len(cuts), top_value / len(cuts))
        loudness = loudness * jnp.repeat(jnp.exp(draws), extent[position] // parts).reshape((-1,) + (1,) * (len(extent) - 1 - position))
    return loudness


def normal_values(key, shape, scale, most, shards=(), kind=jnp.bfloat16):
    values = jax.random.normal(key, shape, jnp.float32) * scale
    if len(shards) > 0:
        values = level_of(key, shape, shards, -0.22, 0.18) * values
    return jnp.clip(values, min=-most, max=most).astype(kind)


def setup_inputs(seed: int = 0) -> dict:
    key_list = jax.random.split(jax.random.key(seed), 11)
    return {
        "modes": normal_values(key_list[0], (ROWS, NMODE), 1.0, 6.0, ((0, 32),), jnp.float32),
        "search": normal_values(key_list[1], (ROWS, NMODE), 1.0, 6.0, ((0, 32),), jnp.float32),
        "precond": jnp.clip(jnp.exp(math.log(0.25) - 1.609438 * jax.random.uniform(key_list[2], (ROWS,), jnp.float32) ** level_of(key_list[2], (ROWS,), ((0, 32),), -0.2, 0.2)), 0.05, 0.25),
        "in_row": draw_in_row(jax.random.fold_in(key_list[10], 71), 0),
        "in_col": draw_in_col(jax.random.fold_in(key_list[10], 71), 0),
        "in_val": draw_in_val(jax.random.fold_in(key_list[10], 71), 0),
        "bnd_rows": draw_bnd_rows(jax.random.fold_in(key_list[10], 71), 0),
        "if_row": draw_if_row(jax.random.fold_in(key_list[10], 71), 0),
        "if_src": draw_if_src(jax.random.fold_in(key_list[10], 71), 0),
        "if_val": draw_if_val(jax.random.fold_in(key_list[10], 71), 0),
    }


precise_mode = lax.Precision.HIGHEST

def gram_product(left, right):
    return jnp.dot(left.T.astype(jnp.float32), right.astype(jnp.float32), precision=precise_mode, preferred_element_type=jnp.float32)

def full_dot(left, right):
    return jnp.dot(left.astype(jnp.float32), right.astype(jnp.float32), precision=precise_mode, preferred_element_type=jnp.float32)

def chol_solve(matrix, rhs):
    factor = jnp.linalg.cholesky(matrix)
    halfway = lax.linalg.triangular_solve(factor, rhs, left_side=True, lower=True)
    return lax.linalg.triangular_solve(factor, halfway, left_side=True, lower=True, transpose_a=True)

def rescale(factor, moved):
    return lax.linalg.triangular_solve(factor, moved, left_side=False, lower=True, transpose_a=True)

def apply_blocks(vector, in_row, in_col, in_val, bnd_rows, if_row, if_src, if_val):
    width = vector.shape[1]
    pieces = vector.reshape(N_SUB, N_ROW, LB, KB, width)
    row_ids = jnp.arange(N_ROW, dtype=jnp.int32)
    local_ids = jnp.arange(LB, dtype=jnp.int32)

    def subdomain(items):
        group, rows_here, cols_here, vals_here = items
        flat = group.reshape(SUBB, KB, width)
        fetched = flat[cols_here]
        vals_wide = vals_here.astype(jnp.float32)
        forward = jnp.einsum('rkij,rkjw->rkiw', vals_wide, fetched, precision=precise_mode)
        owned = group[row_ids[:, None], rows_here]
        backward = jnp.einsum('rkji,rkjw->rkiw', vals_wide, owned, precision=precise_mode)
        keeper = (cols_here != row_ids[:, None] * LB + rows_here).astype(jnp.float32)
        backward = backward * keeper[:, :, None, None]
        select = (rows_here[:, :, None] == local_ids).astype(jnp.float32)
        result = jnp.einsum('rka,rkiw->raiw', select, forward, precision=precise_mode)
        spread = jax.ops.segment_sum(backward.reshape(N_ROW * NIN, KB, width), cols_here.reshape(-1), num_segments=SUBB)
        return result + spread.reshape(N_ROW, LB, KB, width)
    result = lax.map(subdomain, (pieces, in_row, in_col, in_val))
    sub_ids = jnp.arange(N_SUB, dtype=jnp.int32)[:, None, None]
    row_grid = row_ids[None, :, None]
    boundary = pieces[sub_ids, row_grid, bnd_rows]
    target = (if_src // IFR).astype(jnp.int32)
    slot_ids = (if_src % IFR).astype(jnp.int32)
    remote = boundary[target, row_grid, slot_ids]
    face_wide = if_val.astype(jnp.float32)
    forward = jnp.einsum('srkij,srkjw->srkiw', face_wide, remote, precision=precise_mode)
    owned = pieces[sub_ids, row_grid, if_row]
    backward = jnp.einsum('srkji,srkjw->srkiw', face_wide, owned, precision=precise_mode)
    select = (if_row[..., None] == local_ids).astype(jnp.float32)
    result = result + jnp.einsum('srka,srkiw->sraiw', select, forward, precision=precise_mode)
    destination = ((target * N_ROW + row_grid) * IFR + slot_ids).astype(jnp.int32)
    landed = jax.ops.segment_sum(backward.reshape(-1, KB, width), destination.reshape(-1), num_segments=N_SUB * N_ROW * IFR)
    landed = landed.reshape(N_SUB, N_ROW, IFR, KB, width)
    placed = (bnd_rows[..., None] == local_ids).astype(jnp.float32)
    result = result + jnp.einsum('srqa,srqiw->sraiw', placed, landed, precision=precise_mode)
    return result.reshape(-1, width)

def reference(modes, search, precond, in_row, in_col, in_val, bnd_rows, if_row, if_src, if_val):

    def operator(vector):
        return apply_blocks(vector, in_row, in_col, in_val, bnd_rows, if_row, if_src, if_val)
    nmode = modes.shape[1]
    images = operator(jnp.concatenate([modes, search], 1))
    current, direction = (modes, search)
    image_x, image_p = (images[:, :nmode], images[:, nmode:])
    for sweep in range(ITERS):
        correlation = gram_product(current, current)
        energy = gram_product(current, image_x)
        ritz = chol_solve(correlation, energy)
        residue = image_x - full_dot(current, ritz)
        update = precond[:, None] * residue
        image_w = operator(update)
        basis = jnp.concatenate([update, direction], 1)
        image_b = jnp.concatenate([image_w, image_p], 1)
        coupled = gram_product(basis, image_b)
        driving = gram_product(basis, image_x)
        coeffs = -chol_solve(coupled, driving)
        step_x = full_dot(basis, coeffs)
        step_a = full_dot(image_b, coeffs)
        moved = current + step_x
        moved_image = image_x + step_a
        factor = jnp.linalg.cholesky(gram_product(moved, moved) / ROWS)
        current = rescale(factor, moved)
        image_x = rescale(factor, moved_image)
        direction = rescale(factor, step_x)
        image_p = rescale(factor, step_a)
    return (current, direction)
```

```python
import functools

import jax
import jax.numpy as jnp
from jax import lax
from jax.experimental import pallas as pl
from jax.experimental.pallas import tpu as pltpu
from jax.sharding import PartitionSpec as P

f32 = jnp.float32
bf16 = jnp.bfloat16
precise_mode = lax.Precision.HIGHEST
ITERS = 2
VMEM = pltpu.VMEM
SMEM = pltpu.SMEM


def nn(a, b):
    return lax.dot_general(a, b, (((1,), (0,)), ((), ())), precision=precise_mode, preferred_element_type=f32)


def nt(a, b):
    return lax.dot_general(a, b, (((1,), (1,)), ((), ())), precision=precise_mode, preferred_element_type=f32)


def two_parts(block):
    high = block.astype(bf16).astype(f32)
    return jnp.concatenate([high, block - high], axis=1).astype(bf16)


def write_wire(vector, bnd, wire, edge):
    blocks, kb = wire.shape[0], wire.shape[2] // 2
    for i in range(blocks):
        wire[i] = two_parts(vector[:, i * kb : (i + 1) * kb])
    for q in range(edge.shape[0]):
        edge[q] = wire[bnd[q]]


def write_pieces(table, pos, pieces):
    height = pieces[0].shape[0]
    for k, piece in enumerate(pieces):
        start = pl.multiple_of((pos[2] ^ k) * height, 8)
        piece[...] = table[pl.ds(start, height), :]


def read_pieces(pieces, pos, table):
    height = pieces[0].shape[0]
    for k, piece in enumerate(pieces):
        start = pl.multiple_of((pos[2] ^ k) * height, 8)
        table[pl.ds(start, height), :] = piece[...]


def fill_halo(wires, edges, pos, halo):
    lb = wires[0].shape[0]
    n_row = len(wires)
    ifr = edges[0].shape[0]
    for k, wire in enumerate(wires):
        start = (pos[0] ^ k) * lb
        for i in range(lb):
            halo[start + i] = wire[i]
    for k, edge in enumerate(edges):
        start = n_row * lb + (pos[1] ^ (k + 1)) * ifr
        for q in range(ifr):
            halo[start + q] = edge[q]
    own = n_row * lb + pos[1] * ifr
    for q in range(ifr):
        halo[own + q] = jnp.zeros(halo.shape[1:], bf16)


def forward(halo, wire, stored, diagonal, where, out, diag_out):
    lb, kb = wire.shape[0], wire.shape[2] // 2
    groups = stored.shape[2] // (2 * kb)
    for i in range(0, lb, 2):
        sums, diags = [], []
        for m in (i, i + 1):
            row = jnp.concatenate([halo[where[m * groups + g]] for g in range(groups)], axis=1)
            sums.append(lax.dot_general(row, stored[m], (((1,), (1,)), ((), ())), preferred_element_type=f32))
            diags.append(lax.dot_general(wire[m], diagonal[m], (((1,), (1,)), ((), ())), preferred_element_type=f32))
        out[:, i * kb : (i + 2) * kb] = jnp.concatenate(sums, axis=1)
        diag_out[:, i * kb : (i + 2) * kb] = jnp.concatenate(diags, axis=1)


def returned(own, rows, edges, bnd, back):
    lb, kb = own.shape[0], own.shape[2]
    for i in range(lb):
        total = rows[0][i].astype(f32)
        for row in rows[1:]:
            total = total + row[i].astype(f32)
        back[i] = own[i] + (total[:, :kb] + total[:, kb:])
    for q in range(edges[0].shape[0]):
        total = edges[0][q].astype(f32)
        for edge in edges[1:]:
            total = total + edge[q].astype(f32)
        back[bnd[q]] = back[bnd[q]] + (total[:, :kb] + total[:, kb:])


def add_returned(back, target):
    lb, kb = back.shape[0], back.shape[2]
    for i in range(0, lb, 2):
        span = slice(i * kb, (i + 2) * kb)
        target[:, span] = target[:, span] + jnp.concatenate([back[i], back[i + 1]], axis=1)


def eliminate(table, full):
    order = table.shape[0]
    rows = lax.broadcasted_iota(jnp.int32, table.shape, 0)
    for j in range(order):
        pivot_row = table[j : j + 1, :]
        scaled = pivot_row * (1.0 / table[j : j + 1, j : j + 1])
        moved = table - table[:, j : j + 1] * scaled
        if full:
            table = jnp.where(rows == j, scaled, moved)
        else:
            table = jnp.where(rows > j, moved, table)
    return table


def unit(order):
    return (
        lax.broadcasted_iota(jnp.int32, (order, order), 0) == lax.broadcasted_iota(jnp.int32, (order, order), 1)
    ).astype(f32)


def inverse(matrix):
    order = matrix.shape[0]
    return eliminate(jnp.concatenate([matrix, unit(order)], axis=1), True)[:, order:]


def cholesky_inverse(matrix):
    order = matrix.shape[0]
    done = eliminate(jnp.concatenate([matrix, unit(order)], axis=1), False)
    pivots = jnp.sum(done[:, :order] * unit(order), axis=1, keepdims=True)
    return done[:, order:] * (1.0 / jnp.sqrt(pivots))


def coefficients(table, gram, xp, pp, pax, pap_inverse, total_rows):
    n = gram.shape[0]
    waw, wap = table[0:n, :n], table[0:n, n:]
    wax, wx = table[n : 2 * n, :n], table[n : 2 * n, n:]
    wp, ww = table[2 * n : 3 * n, :n], table[2 * n : 3 * n, n:]
    waw = waw + waw.T
    first = nn(pap_inverse, wap.T)
    if pax is None:
        rhs = -wax
    else:
        second = nn(pap_inverse, pax)
        rhs = nn(wap, second) - wax
    schur = waw - nn(wap, first)
    zw = eliminate(jnp.concatenate([schur, rhs], axis=1), True)[:, n:]
    zp = -nn(first, zw)
    if pax is not None:
        zp = zp - second
    cross = nn(wx.T, zw) + nn(xp, zp)
    inner = nn(zw.T, nn(ww, zw) + nn(wp, zp)) + nn(zp.T, nn(wp.T, zw) + nn(pp, zp))
    lengths = (gram + cross + cross.T + inner) / total_rows
    return zw, zp, cross, inner, wax, cholesky_inverse(lengths)


def prepare_kernel(groups, base, vals, faces, rows, cols, face_rows, face_src, stored, joined, diagonal, where):
    lb, kb = faces.shape[0], faces.shape[1]
    for k in range(lb):
        diagonal[k] = vals[k]
    for g in range(groups):
        half = (g % 2) * kb
        for m in range(lb):
            if g < groups - 1:
                k = (g + 1) * lb + m
                i, target, block = rows[k], cols[k], vals[k]
            else:
                i, target, block = face_rows[m], base + face_src[m], faces[m]
            stored[i, :, 2 * kb * g : 2 * kb * (g + 1)] = block
            joined[i, :, kb * g : kb * (g + 1)] = block[:, half : half + kb]
            where[i * groups + g] = target


def wire_kernel(vector, bnd, wire, edge):
    write_wire(vector, bnd, wire, edge)


def start_gram_kernel(x, p, pos, *rest):
    pieces, table = rest[:-1], rest[-1]
    n = x.shape[0]
    table[...] = jnp.zeros(table.shape, f32)
    table[0:n, :] = nt(x[...], jnp.concatenate([x[...], p[...]], axis=0))
    table[n : 2 * n, 0:n] = nt(p[...], p[...])
    write_pieces(table, pos, pieces)


def partial_kernel(n_row, n_sub, wire, joined, where, pos, own, *rest):
    row_outs, edge_outs, acc = rest[: n_row - 1], rest[n_row - 1 : -1], rest[-1]
    lb, kb = wire.shape[0], wire.shape[2] // 2
    ifr = edge_outs[0].shape[0]
    groups = joined.shape[2] // kb
    acc[...] = jnp.zeros(acc.shape, f32)
    low = lax.broadcasted_iota(jnp.int32, (kb, 2 * kb), 1) < kb
    for i in range(lb):
        blocks = jnp.concatenate([joined[i], joined[i]], axis=0)
        out = jnp.dot(wire[i], blocks, preferred_element_type=f32)
        for t in range(groups // 2):
            tile = out[:, 2 * kb * t : 2 * kb * (t + 1)]
            one = where[i * groups + 2 * t]
            two = where[i * groups + 2 * t + 1]
            acc[one] = acc[one] + jnp.where(low, tile, 0.0)
            acc[two] = acc[two] + jnp.where(low, 0.0, tile)

    def folded(index):
        block = acc[index]
        return block[:, :kb] + block[:, kb:]

    for k in range(n_row):
        start = (pos[0] ^ k) * lb
        for i in range(lb):
            if k == 0:
                own[i] = folded(start + i)
            else:
                row_outs[k - 1][i] = two_parts(folded(start + i))
    for k in range(1, n_sub):
        start = n_row * lb + (pos[1] ^ k) * ifr
        for q in range(ifr):
            edge_outs[k - 1][q] = two_parts(folded(start + q))


def image_kernel(n_row, n_sub, is_x, *refs):
    refs = list(refs)
    take = lambda count: [refs.pop(0) for _ in range(count)]
    wires, edges = take(n_row), take(n_sub - 1)
    own, = take(1)
    rows, back_edges = take(n_row - 1), take(n_sub - 1)
    stored, diagonal, where, bnd, pos = take(5)
    x, p = take(2) if is_x else (None, take(1)[0])
    image, = take(1)
    halo, back, diag, table = refs[-4:]
    pieces = refs[:-4]
    n = p.shape[0]
    fill_halo(wires, edges, pos, halo)
    forward(halo, wires[0], stored, diagonal, where, image, diag)
    returned(own, rows, back_edges, bnd, back)
    image[...] = image[...] + diag[...]
    add_returned(back, image)
    table[...] = jnp.zeros(table.shape, f32)
    if is_x:
        table[0:n, 0:n] = nt(image[...], x[...])
        table[0:n, n : 2 * n] = nt(p[...], image[...])
    else:
        table[0:n, 0:n] = nt(p[...], image[...])
    write_pieces(table, pos, pieces)


def update_image_kernel(n_row, n_sub, *refs):
    refs = list(refs)
    take = lambda count: [refs.pop(0) for _ in range(count)]
    wires, edges = take(n_row), take(n_sub - 1)
    stored, diagonal, where, pos, w, x, p, ax, ap, near = take(10)
    halo, diag, table = refs[-3:]
    pieces = refs[:-3]
    n = w.shape[0]
    fill_halo(wires, edges, pos, halo)
    forward(halo, wires[0], stored, diagonal, where, near, diag)
    table[...] = jnp.zeros(table.shape, f32)
    w_here = w[...]
    half = near[...] + 0.5 * diag[...]
    table[0:n, :] = nt(w_here, jnp.concatenate([half, ap[...]], axis=0))
    table[n : 2 * n, :] = nt(w_here, jnp.concatenate([ax[...], x[...]], axis=0))
    table[2 * n : 3 * n, :] = nt(w_here, jnp.concatenate([p[...], w_here], axis=0))
    near[...] = near[...] + diag[...]
    write_pieces(table, pos, pieces)


def gram_inverse_kernel(n_plane, *refs):
    pieces = refs[:n_plane]
    pos, table, solved = refs[n_plane:]
    n = solved.shape[0]
    read_pieces(pieces, pos, table)
    matrix = table[0:n, 0:n]
    solved[...] = inverse(0.5 * (matrix + matrix.T))


def inverse_kernel(matrix, solved):
    solved[...] = inverse(matrix[...])


def update_kernel(n_plane, *refs):
    pieces = refs[:n_plane]
    pos, bnd, gram_inverse, x, ax, precond, table, w, wire, edge = refs[n_plane:]
    n = x.shape[0]
    read_pieces(pieces, pos, table)
    ritz = nn(table[0:n, 0:n], gram_inverse[...])
    w[...] = precond[...] * (ax[...] - nn(ritz, x[...]))
    write_wire(w, bnd, wire, edge)


def move_kernel(n_plane, n_row, n_sub, total_rows, *refs):
    refs = list(refs)
    take = lambda count: [refs.pop(0) for _ in range(count)]
    pieces = take(n_plane)
    own, = take(1)
    rows, back_edges = take(n_row - 1), take(n_sub - 1)
    pos, bnd, start, energy, pap_inverse, x, p, ax, ap, w, near, precond = take(12)
    x_out, p_out, ax_out, ap_out, w_out, wire, edge, state, table, back = refs
    n = x.shape[0]
    read_pieces(pieces, pos, table)
    gram, xp, pp = start[0:n, 0:n], start[0:n, n:], start[n : 2 * n, 0:n]
    ht, pax = energy[0:n, 0:n], energy[0:n, n:]
    zw, zp, cross, inner, wax, scale = coefficients(
        table[...], 0.5 * (gram + gram.T), xp, pp, pax, pap_inverse[...], total_rows
    )
    returned(own, rows, back_edges, bnd, back)
    add_returned(back, near)
    zwt, zpt = zw.T, zp.T
    step_x = nn(zwt, w[...]) + nn(zpt, p[...])
    step_a = nn(zwt, near[...]) + nn(zpt, ap[...])
    x_out[...] = nn(scale, x[...] + step_x)
    p_out[...] = nn(scale, step_x)
    ax_out[...] = nn(scale, ax[...] + step_a)
    ap_out[...] = nn(scale, step_a)
    gain = nn(wax.T, zw) + nn(pax.T, zp)
    gain = 0.5 * (gain + gain.T)
    scale_t = scale.T
    ritz = nn(scale, nn(0.5 * (ht + ht.T) + gain, scale_t)) / total_rows
    w_out[...] = precond[...] * (ax_out[...] - nn(ritz, x_out[...]))
    write_wire(w_out, bnd, wire, edge)
    state[0:n, :] = nn(scale, nn(-gain, scale_t))
    state[n : 2 * n, :] = nn(scale, nn(cross + inner, scale_t))
    state[2 * n : 3 * n, :] = nn(scale, nn(inner, scale_t))


def finish_kernel(n_plane, total_rows, *refs):
    pieces = refs[:n_plane]
    pos, state, pap_inverse, x, p, w, x_out, p_out, table = refs[n_plane:]
    n = x.shape[0]
    read_pieces(pieces, pos, table)
    zw, zp, _, _, _, scale = coefficients(
        table[...],
        unit(n) * total_rows,
        state[n : 2 * n, :],
        state[2 * n : 3 * n, :],
        None,
        pap_inverse[...],
        total_rows,
    )
    step = nn(zw.T, w[...]) + nn(zp.T, p[...])
    x_out[...] = nn(scale, x[...] + step)
    p_out[...] = nn(scale, step)


def run(kernel, name, outs, ins, scratch=(), smem=(), smem_outs=(), flops=1000000):
    in_specs = [pl.BlockSpec(memory_space=SMEM if i in smem else VMEM) for i in range(len(ins))]
    out_specs = [pl.BlockSpec(memory_space=SMEM if i in smem_outs else VMEM) for i in range(len(outs))]
    moved = sum(a.size * a.dtype.itemsize for a in ins) + sum(o.size * o.dtype.itemsize for o in outs)
    return pl.pallas_call(
        kernel,
        name=name,
        out_shape=outs,
        in_specs=in_specs,
        out_specs=out_specs,
        scratch_shapes=list(scratch),
        compiler_params=pltpu.CompilerParams(vmem_limit_bytes=48 * 1024 * 1024),
        cost_estimate=pl.CostEstimate(flops=flops, bytes_accessed=moved, transcendentals=0),
    )(*ins)


def shaped(*shape, dtype=f32):
    return jax.ShapeDtypeStruct(shape, dtype)


def local(n_sub, n_row, modes, search, precond, in_row, in_col, in_val, bnd_rows, if_row, if_src, if_val):
    nin, kb = in_val.shape[2], in_val.shape[3]
    rows, n = modes.shape
    lb = rows // kb
    ifr = bnd_rows.shape[2]
    groups = nin // lb
    n_core = 2
    n_z = n_sub // n_core
    n_plane = n_core * n_row
    total_rows = float(rows * n_sub * n_row)
    halo_blocks = n_row * lb + n_sub * ifr
    bnd = bnd_rows[0, 0]
    me_row, me_sub = lax.axis_index("row"), lax.axis_index("sub")
    pos = jnp.stack([me_row, me_sub, (me_sub % n_core) * n_row + me_row]).astype(jnp.int32)

    def to_row(k):
        return [(r, r ^ k) for r in range(n_row)]

    def to_sub(k):
        return [(s, s ^ k) for s in range(n_sub)]

    def to_plane(k):
        kc, kr = divmod(k, n_row)
        return [(s * n_row + r, (s ^ kc) * n_row + (r ^ kr)) for s in range(n_sub) for r in range(n_row)]

    def halo_of(wire, edge):
        wires = [wire] + [lax.ppermute(wire, "row", to_row(k)) for k in range(1, n_row)]
        edges = [lax.ppermute(edge, "sub", to_sub(k)) for k in range(1, n_sub)]
        return wires, edges

    def tree(parts):
        while len(parts) > 1:
            parts = [parts[i] + parts[i + 1] for i in range(0, len(parts), 2)]
        return parts[0]

    def all_sum(pieces):
        got = [pieces[0]] + [lax.ppermute(pieces[k], ("sub", "row"), to_plane(k)) for k in range(1, n_plane)]
        mine = tree(got)
        got = [mine] + [lax.ppermute(mine, "sub", to_sub(k * n_core)) for k in range(1, n_z)]
        mine = tree(got)
        return [mine] + [lax.ppermute(mine, ("sub", "row"), to_plane(k)) for k in range(1, n_plane)]

    def table_rows(blocks):
        unit_rows = 8 * n_plane
        return -(-blocks * n // unit_rows) * unit_rows

    def piece_shapes(blocks):
        return [shaped(table_rows(blocks) // n_plane, 2 * n)] * n_plane

    def send_partials(wire):
        outs = [shaped(lb, n, kb)] + [shaped(lb, n, 2 * kb, dtype=bf16)] * (n_row - 1)
        outs += [shaped(ifr, n, 2 * kb, dtype=bf16)] * (n_sub - 1)
        parts = run(
            functools.partial(partial_kernel, n_row, n_sub),
            "partials",
            outs,
            [wire, joined, where, pos],
            [VMEM((halo_blocks, n, 2 * kb), f32)],
            smem=(2, 3),
        )
        back = [lax.ppermute(parts[k], "row", to_row(k)) for k in range(1, n_row)]
        back += [lax.ppermute(parts[n_row + k - 1], "sub", to_sub(k)) for k in range(1, n_sub)]
        return [parts[0]] + back

    x, p = modes.T, search.T
    scaling = precond.reshape(1, rows)
    wire_shapes = [shaped(lb, n, 2 * kb, dtype=bf16), shaped(ifr, n, 2 * kb, dtype=bf16)]
    x_wire, x_edge = run(wire_kernel, "wire", wire_shapes, [x, bnd], smem=(1,))
    x_halo = halo_of(x_wire, x_edge)
    p_wire, p_edge = run(wire_kernel, "wire", wire_shapes, [p, bnd], smem=(1,))
    start_pieces = run(
        start_gram_kernel, "start_gram", piece_shapes(2), [x, p, pos], [VMEM((table_rows(2), 2 * n), f32)], smem=(2,)
    )
    twice = jnp.concatenate([in_val[0, 0], in_val[0, 0]], axis=-1)
    twice_face = jnp.concatenate([if_val[0, 0], if_val[0, 0]], axis=-1)
    stored, joined, diagonal, where = run(
        functools.partial(prepare_kernel, groups, n_row * lb),
        "prepare",
        [
            shaped(lb, kb, groups * 2 * kb, dtype=bf16),
            shaped(lb, kb, groups * kb, dtype=bf16),
            shaped(lb, kb, 2 * kb, dtype=bf16),
            shaped(lb * groups, dtype=jnp.int32),
        ],
        [twice, twice_face, in_row[0, 0], in_col[0, 0], if_row[0, 0], if_src[0, 0]],
        smem=(2, 3, 4, 5),
        smem_outs=(3,),
    )
    x_back = send_partials(x_wire)
    p_halo = halo_of(p_wire, p_edge)
    p_back = send_partials(p_wire)

    def image_of(halo, back, vectors, is_x):
        ins = halo[0] + halo[1] + back + [stored, diagonal, where, bnd, pos] + vectors
        first = n_row + n_sub - 1 + len(back) + 2
        return run(
            functools.partial(image_kernel, n_row, n_sub, is_x),
            "image",
            [shaped(n, rows)] + piece_shapes(1),
            ins,
            [
                VMEM((halo_blocks, n, 2 * kb), bf16),
                VMEM((lb, n, kb), f32),
                VMEM((n, rows), f32),
                VMEM((table_rows(1), 2 * n), f32),
            ],
            smem=(first, first + 1, first + 2),
        )

    def update_image(halo, w, x, p, ax, ap):
        ins = halo[0] + halo[1] + [stored, diagonal, where, pos, w, x, p, ax, ap]
        first = n_row + n_sub - 1 + 2
        near, *pieces = run(
            functools.partial(update_image_kernel, n_row, n_sub),
            "update_image",
            [shaped(n, rows)] + piece_shapes(3),
            ins,
            [VMEM((halo_blocks, n, 2 * kb), bf16), VMEM((n, rows), f32), VMEM((table_rows(3), 2 * n), f32)],
            smem=(first, first + 1),
        )
        return near, pieces

    start_sums = all_sum(start_pieces)
    start_table, gram_inverse = run(
        functools.partial(gram_inverse_kernel, n_plane),
        "gram_inverse",
        [shaped(table_rows(2), 2 * n), shaped(n, n)],
        start_sums + [pos],
        smem=(n_plane,),
    )
    ax, *energy_pieces = image_of(x_halo, x_back, [x, p], True)
    energy_sums = all_sum(energy_pieces)
    ap, *pap_pieces = image_of(p_halo, p_back, [p], False)
    energy, w, w_wire, w_edge = run(
        functools.partial(update_kernel, n_plane),
        "update",
        [shaped(table_rows(1), 2 * n), shaped(n, rows)] + wire_shapes,
        energy_sums + [pos, bnd, gram_inverse, x, ax, scaling],
        smem=(n_plane, n_plane + 1),
    )
    w_halo = halo_of(w_wire, w_edge)
    pap_sums = all_sum(pap_pieces)
    _, pap_inverse = run(
        functools.partial(gram_inverse_kernel, n_plane),
        "pap_inverse",
        [shaped(table_rows(1), 2 * n), shaped(n, n)],
        pap_sums + [pos],
        smem=(n_plane,),
    )
    w_near, w_pieces = update_image(w_halo, w, x, p, ax, ap)
    w_sums = all_sum(w_pieces)
    w_back = send_partials(w_wire)
    ins = list(w_sums) + w_back
    x, p, ax, ap, w, w_wire, w_edge, state = run(
        functools.partial(move_kernel, n_plane, n_row, n_sub, total_rows),
        "move",
        [shaped(n, rows)] * 5 + wire_shapes + [shaped(3 * n, n)],
        ins + [pos, bnd, start_table, energy, pap_inverse, x, p, ax, ap, w, w_near, scaling],
        [VMEM((table_rows(3), 2 * n), f32), VMEM((lb, n, kb), f32)],
        smem=(len(ins), len(ins) + 1),
    )
    w_halo = halo_of(w_wire, w_edge)
    pap_inverse, = run(inverse_kernel, "next_inverse", [shaped(n, n)], [state[:n]])
    _, w_pieces = update_image(w_halo, w, x, p, ax, ap)
    w_sums = all_sum(w_pieces)
    x, p = run(
        functools.partial(finish_kernel, n_plane, total_rows),
        "finish",
        [shaped(n, rows)] * 2,
        list(w_sums) + [pos, state, pap_inverse, x, p, w],
        [VMEM((table_rows(3), 2 * n), f32)],
        smem=(n_plane,),
    )
    return (x.T, p.T)


def solution(mesh):
    return jax.shard_map(
        functools.partial(local, mesh.shape["sub"], mesh.shape["row"]),
        mesh=mesh,
        in_specs=(
            P(("sub", "row"), None),
            P(("sub", "row"), None),
            P(("sub", "row")),
            P("sub", "row", None),
            P("sub", "row", None),
            P("sub", "row", None, None, None),
            P("sub", "row", None),
            P("sub", "row", None),
            P("sub", "row", None),
            P("sub", "row", None, None, None),
        ),
        out_specs=(P(("sub", "row"), None), P(("sub", "row"), None)),
        check_vma=False,
    )
```

```python
import functools

import jax
import jax.numpy as jnp
from jax import lax
from jax.experimental import pallas as pl
from jax.experimental.pallas import tpu as pltpu
from jax.sharding import PartitionSpec as P

f32 = jnp.float32
bf16 = jnp.bfloat16
precise_mode = lax.Precision.HIGHEST
VMEM = pltpu.VMEM
SMEM = pltpu.SMEM


def nn(a, b):
    return lax.dot_general(a, b, (((1,), (0,)), ((), ())), precision=precise_mode, preferred_element_type=f32)


def nt(a, b):
    return lax.dot_general(a, b, (((1,), (1,)), ((), ())), precision=precise_mode, preferred_element_type=f32)


def two_parts(block):
    high = block.astype(bf16).astype(f32)
    return jnp.concatenate([high, block - high], axis=1).astype(bf16)


def write_wire(vector, bnd, wire, edge):
    blocks, kb = wire.shape[0], wire.shape[2] // 2
    for i in range(blocks):
        wire[i] = two_parts(vector[:, i * kb : (i + 1) * kb])
    for q in range(edge.shape[0]):
        edge[q] = wire[bnd[q]]


def loop(count, body):
    def step(i, carry):
        body(i)
        return carry

    lax.fori_loop(0, count, step, 0)


def fill_halo(wires, edges, pos, halo):
    n_row, n_z = len(wires), len(edges)
    lb, ifr = wires[0][2], edges[0][0][2]
    for k, (wire, offset, count) in enumerate(wires):
        start = (pos[0] ^ k) * lb

        def copy(i, wire=wire, offset=offset, start=start):
            halo[start + i] = wire[offset + i]

        loop(count, copy)
    for k, pair in enumerate(edges):
        for other, (edge, offset, count) in enumerate(pair):
            start = n_row * lb + (((pos[1] // 2) ^ k) * 2 + ((pos[1] % 2) ^ other)) * ifr
            for q in range(count):
                halo[start + q] = edge[offset + q]


def write_halves(table, pos, keep, send):
    height = keep.shape[0]
    core = pos[1] % 2
    keep[...] = table[pl.ds(pl.multiple_of(core * height, 8), height), :]
    send[...] = table[pl.ds(pl.multiple_of((1 - core) * height, 8), height), :]


def read_halves(mine, other, pos, table):
    height = mine.shape[0]
    core = pos[1] % 2
    table[pl.ds(pl.multiple_of(core * height, 8), height), :] = mine[...]
    table[pl.ds(pl.multiple_of((1 - core) * height, 8), height), :] = other[...]


def forward(halo, wire, stored, diagonal, where, out, diag_out):
    lb, kb = wire.shape[0], wire.shape[2] // 2
    groups = stored.shape[2] // (2 * kb)
    for i in range(0, lb, 2):
        sums, diags = [], []
        for m in (i, i + 1):
            row = jnp.concatenate([halo[where[m * groups + g]] for g in range(groups)], axis=1)
            sums.append(lax.dot_general(row, stored[m], (((1,), (1,)), ((), ())), preferred_element_type=f32))
            diags.append(lax.dot_general(wire[m], diagonal[m], (((1,), (1,)), ((), ())), preferred_element_type=f32))
        out[:, i * kb : (i + 2) * kb] = jnp.concatenate(sums, axis=1)
        diag_out[:, i * kb : (i + 2) * kb] = jnp.concatenate(diags, axis=1)


def returned(index, own, rows, edge_own, edges, bnd, back):
    lb, kb = back.shape[0], back.shape[2]
    ifr = bnd.shape[0]
    for i in range(lb):
        total = rows[0][index * lb + i].astype(f32)
        for row in rows[1:]:
            total = total + row[index * lb + i].astype(f32)
        back[i] = own[index * lb + i] + (total[:, :kb] + total[:, kb:])
    for q in range(ifr):
        total = edges[0][index * ifr + q].astype(f32)
        for edge in edges[1:]:
            total = total + edge[index * ifr + q].astype(f32)
        back[bnd[q]] = back[bnd[q]] + edge_own[index * ifr + q] + (total[:, :kb] + total[:, kb:])


def add_returned(back, target):
    lb, kb = back.shape[0], back.shape[2]
    for i in range(0, lb, 2):
        span = slice(i * kb, (i + 2) * kb)
        target[:, span] = target[:, span] + jnp.concatenate([back[i], back[i + 1]], axis=1)


def eliminate(table, full):
    order = table.shape[0]
    rows = lax.broadcasted_iota(jnp.int32, table.shape, 0)
    for j in range(0, order, 2):
        one, two = table[j : j + 1, :], table[j + 1 : j + 2, :]
        a, b = one[:, j : j + 1], one[:, j + 1 : j + 2]
        c, d = two[:, j : j + 1], two[:, j + 1 : j + 2]
        scale = 1.0 / (a * d - b * c)
        first = (d * scale) * one - (b * scale) * two
        second = (a * scale) * two - (c * scale) * one
        moved = table - table[:, j : j + 1] * first - table[:, j + 1 : j + 2] * second
        if full:
            table = jnp.where(rows == j, first, jnp.where(rows == j + 1, second, moved))
        else:
            table = jnp.where(rows > j + 1, moved, jnp.where(rows == j + 1, two - (c / a) * one, table))
    return table


def unit(order):
    return (
        lax.broadcasted_iota(jnp.int32, (order, order), 0) == lax.broadcasted_iota(jnp.int32, (order, order), 1)
    ).astype(f32)


def inverse(matrix):
    order = matrix.shape[0]
    return eliminate(jnp.concatenate([matrix, unit(order)], axis=1), True)[:, order:]


def cholesky_inverse(matrix):
    order = matrix.shape[0]
    done = eliminate(jnp.concatenate([matrix, unit(order)], axis=1), False)
    pivots = jnp.sum(done[:, :order] * unit(order), axis=1, keepdims=True)
    return done[:, order:] * (1.0 / jnp.sqrt(pivots))


def coefficients(table, gram, xp, pp, pax, pap_inverse, total_rows):
    n = gram.shape[0]
    waw, wap = table[0:n, :n], table[0:n, n:]
    wax, wx = table[n : 2 * n, :n], table[n : 2 * n, n:]
    wp, ww = table[2 * n : 3 * n, :n], table[2 * n : 3 * n, n:]
    waw = waw + waw.T
    first = nn(pap_inverse, wap.T)
    if pax is None:
        rhs = -wax
    else:
        second = nn(pap_inverse, pax)
        rhs = nn(wap, second) - wax
    schur = waw - nn(wap, first)
    zw = eliminate(jnp.concatenate([schur, rhs], axis=1), True)[:, n:]
    zp = -nn(first, zw)
    if pax is not None:
        zp = zp - second
    cross = nn(wx.T, zw) + nn(xp, zp)
    zwt, zpt = zw.T, zp.T
    inner = nn(zwt, nn(ww, zw) + nn(wp, zp)) + nn(zpt, nn(wp.T, zw) + nn(pp, zp))
    lengths = (gram + cross + cross.T + inner) / total_rows
    return zw, zp, zwt, zpt, cross, inner, wax, cholesky_inverse(lengths)


def prepare_kernel(groups, base, vals, faces, rows, cols, face_rows, face_src, stored, joined, diagonal, where):
    lb, kb = faces.shape[0], faces.shape[1]
    for k in range(lb):
        diagonal[k] = vals[k]
    for g in range(groups):
        half = (g % 2) * kb
        for m in range(lb):
            if g < groups - 1:
                k = (g + 1) * lb + m
                i, target, block = rows[k], cols[k], vals[k]
            else:
                i, target, block = face_rows[m], base + face_src[m], faces[m]
            stored[i, :, 2 * kb * g : 2 * kb * (g + 1)] = block
            joined[i, :, kb * g : kb * (g + 1)] = block[:, half : half + kb]
            where[i * groups + g] = target


def wire_kernel(vector, bnd, wire, edge):
    write_wire(vector, bnd, wire, edge)


def partial_kernel(n_row, n_z, count, extra, *refs):
    refs = list(refs)
    take = lambda number: [refs.pop(0) for _ in range(number)]
    wires = take(count)
    joined, where, pos = take(3)
    more_wire, more_edge = take(2) if extra else (None, None)
    own, core_keep, core_send = take(3)
    row_outs, acc = refs[:-1], refs[-1]
    lb, kb = wires[0].shape[0], wires[0].shape[2] // 2
    ifr = core_keep.shape[0] // (count * n_z)
    groups = joined.shape[2] // kb
    low = lax.broadcasted_iota(jnp.int32, (kb, 2 * kb), 1) < kb
    core = pos[1] % 2
    for v, wire in enumerate(wires):
        acc[...] = jnp.zeros(acc.shape, f32)

        def step(i):
            blocks = jnp.concatenate([joined[i], joined[i]], axis=0)
            out = jnp.dot(wire[i], blocks, preferred_element_type=f32)
            for t in range(groups // 2):
                tile = out[:, 2 * kb * t : 2 * kb * (t + 1)]
                one = where[i * groups + 2 * t]
                two = where[i * groups + 2 * t + 1]
                acc[one] = acc[one] + jnp.where(low, tile, 0.0)
                acc[two] = acc[two] + jnp.where(low, 0.0, tile)

        loop(lb, step)

        def folded(index):
            block = acc[index]
            return block[:, :kb] + block[:, kb:]

        for k in range(n_row):
            start = (pos[0] ^ k) * lb

            def emit(i, k=k, start=start):
                if k == 0:
                    own[v * lb + i] = folded(start + i)
                else:
                    row_outs[k - 1][v * lb + i] = two_parts(folded(start + i))

            loop(lb, emit)

        def emit_edge(z):
            for q in range(ifr):
                spot = (v * n_z + z) * ifr + q
                core_keep[spot] = folded(n_row * lb + (z * 2 + core) * ifr + q)
                core_send[spot] = two_parts(folded(n_row * lb + (z * 2 + 1 - core) * ifr + q))

        loop(n_z, emit_edge)
    if extra:
        for k in range(1, n_row):
            row_outs[k - 1][pl.ds(count * lb, lb)] = more_wire[...]
        core_send[pl.ds(count * n_z * ifr, ifr)] = more_edge[...]


def pair_kernel(n_z, count, extra, keep, got, pos, *refs):
    refs = list(refs)
    more_edge = refs.pop(0) if extra else None
    own, outs = refs[0], refs[1:]
    ifr, kb = own.shape[0] // count, own.shape[2]
    for k in range(n_z):
        z = (pos[1] // 2) ^ k
        for v in range(count):
            for q in range(ifr):
                spot = (v * n_z + z) * ifr + q
                there = got[spot].astype(f32)
                total = keep[spot] + (there[:, :kb] + there[:, kb:])
                if k == 0:
                    own[v * ifr + q] = total
                else:
                    outs[k - 1][v * ifr + q] = two_parts(total)
        if extra and k > 0:
            outs[k - 1][pl.ds(count * ifr, ifr)] = more_edge[...]
            outs[k - 1][pl.ds((count + 1) * ifr, ifr)] = got[pl.ds(count * n_z * ifr, ifr)]


def split_halo(refs, n_row, n_z):
    wires = [refs.pop(0) for _ in range(n_row)]
    same, other = refs.pop(0), refs.pop(0)
    lb, ifr = wires[0].shape[0], same.shape[0] // n_z
    return [(wire, 0, lb) for wire in wires], [((same, k * ifr, ifr), (other, k * ifr, ifr)) for k in range(n_z)]


def x_image_kernel(n_row, n_z, *refs):
    refs = list(refs)
    wires, edges = split_halo(refs, n_row, n_z)
    stored, diagonal, where, pos, x, half, diag, table, halo = refs
    n = x.shape[0]
    fill_halo(wires, edges, pos, halo)
    forward(halo, wires[0][0], stored, diagonal, where, half, diag)
    half[...] = half[...] + 0.5 * diag[...]
    table[...] = nt(x[...], jnp.concatenate([half[...], x[...]], axis=0))


def p_image_kernel(n_row, n_z, ifr, *refs):
    refs = list(refs)
    wire, edge, core_got = refs[:3]
    rows, edges = refs[3 : 2 + n_row], refs[2 + n_row : 1 + n_row + n_z]
    stored, diagonal, where, pos, half, diag, halo = refs[1 + n_row + n_z :]
    lb = wire.shape[0]
    wires = [(wire, 0, lb)] + [(row, lb, lb) for row in rows]
    pairs = [((edge, 0, ifr), (core_got, n_z * ifr, ifr))]
    pairs += [((got, ifr, ifr), (got, 2 * ifr, ifr)) for got in edges]
    fill_halo(wires, pairs, pos, halo)
    forward(halo, wire, stored, diagonal, where, half, diag)
    half[...] = half[...] + 0.5 * diag[...]


def take_returned(refs, n_row, n_z):
    own = refs.pop(0)
    rows = [refs.pop(0) for _ in range(n_row - 1)]
    edge_own = refs.pop(0)
    return own, rows, edge_own, [refs.pop(0) for _ in range(n_z - 1)]


def update_kernel(n_row, n_z, *refs):
    refs = list(refs)
    back_parts = take_returned(refs, n_row, n_z)
    bnd, table, x, half, diag, precond, ax, energy, w, wire, edge, back = refs
    n = x.shape[0]
    returned(0, *back_parts, bnd, back)
    ax[...] = half[...] + 0.5 * diag[...]
    add_returned(back, ax)
    stored, gram = table[:, 0:n], table[:, n:]
    total = stored + stored.T
    energy[...] = total
    ritz = nn(total, inverse(0.5 * (gram + gram.T)))
    w[...] = precond[...] * (ax[...] - nn(ritz, x[...]))
    write_wire(w, bnd, wire, edge)


def update_image_kernel(n_row, n_z, first, *refs):
    refs = list(refs)
    wires, edges = split_halo(refs, n_row, n_z)
    stored, diagonal, where, pos, w, x, p, ax, ap, half, diag, keep, send, halo, table = refs
    n = w.shape[0]
    fill_halo(wires, edges, pos, halo)
    forward(halo, wires[0][0], stored, diagonal, where, half, diag)
    half[...] = half[...] + 0.5 * diag[...]
    here = w[...]
    table[0:n, :] = nt(here, jnp.concatenate([half[...], ap[...]], axis=0))
    table[n : 2 * n, :] = nt(here, jnp.concatenate([ax[...], x[...]], axis=0))
    table[2 * n : 3 * n, :] = nt(here, jnp.concatenate([p[...], here], axis=0))
    if first:
        table[0:n, n:] = table[0:n, n:] + nt(half[...], p[...])
        table[3 * n : 4 * n, :] = nt(p[...], jnp.concatenate([ax[...], ap[...]], axis=0))
        table[4 * n : 5 * n, :] = nt(p[...], jnp.concatenate([x[...], p[...]], axis=0))
    write_halves(table, pos, keep, send)


def move_kernel(n_row, n_z, total_rows, *refs):
    refs = list(refs)
    back_parts = take_returned(refs, n_row, n_z)
    mine, other, pos, bnd, gram, energy, x, p, ax, ap, ap_diag, w, aw, aw_diag, precond = refs[:15]
    x_out, ax_out, w_out, wire, edge, step_x, step_a, small, table, back = refs[15:]
    n = x.shape[0]
    read_halves(mine, other, pos, table)
    gram_here = gram[:, n:]
    pax, pap = table[3 * n : 4 * n, 0:n], table[3 * n : 4 * n, n:]
    px, pp = table[4 * n : 5 * n, 0:n], table[4 * n : 5 * n, n:]
    zw, zp, zwt, zpt, cross, inner, wax, scale = coefficients(
        table, 0.5 * (gram_here + gram_here.T), px.T, pp, pax, inverse(pap + pap.T), total_rows
    )
    step_a[...] = nn(zpt, ap[...] + 0.5 * ap_diag[...]) + nn(zwt, aw[...] + 0.5 * aw_diag[...])
    returned(0, *back_parts, bnd, back)
    for i in range(0, back.shape[0], 2):
        pair = jnp.concatenate([back[i], back[i + 1]], axis=1)
        span = slice(i * back.shape[2], (i + 2) * back.shape[2])
        step_a[:, span] = step_a[:, span] + nn(zpt, pair)
    returned(1, *back_parts, bnd, back)
    for i in range(0, back.shape[0], 2):
        pair = jnp.concatenate([back[i], back[i + 1]], axis=1)
        span = slice(i * back.shape[2], (i + 2) * back.shape[2])
        step_a[:, span] = step_a[:, span] + nn(zwt, pair)
    step_x[...] = nn(zwt, w[...]) + nn(zpt, p[...])
    x_out[...] = nn(scale, x[...] + step_x[...])
    ax_out[...] = nn(scale, ax[...] + step_a[...])
    gain = nn(wax.T, zw) + nn(pax.T, zp)
    gain = 0.5 * (gain + gain.T)
    ritz = nn(scale, nn(energy[...] + gain, scale.T)) / total_rows
    w_out[...] = precond[...] * (ax_out[...] - nn(ritz, x_out[...]))
    write_wire(w_out, bnd, wire, edge)
    small[0:n, :] = -gain
    small[n : 2 * n, :] = cross + inner
    small[2 * n : 3 * n, :] = inner
    small[3 * n : 4 * n, :] = scale


def settle_kernel(small, step_x, step_a, p_out, ap_out, state):
    n = small.shape[1]
    scale = small[3 * n : 4 * n, :]
    scale_t = scale.T
    p_out[...] = nn(scale, step_x[...])
    ap_out[...] = nn(scale, step_a[...])
    state[0:n, :] = inverse(nn(scale, nn(small[0:n, :], scale_t)))
    state[n : 2 * n, :] = nn(scale, nn(small[n : 2 * n, :], scale_t))
    state[2 * n : 3 * n, :] = nn(scale, nn(small[2 * n : 3 * n, :], scale_t))


def finish_kernel(total_rows, mine, other, pos, state, x, p, w, x_out, p_out, table):
    n = x.shape[0]
    read_halves(mine, other, pos, table)
    zw, zp, zwt, zpt, _, _, _, scale = coefficients(
        table,
        unit(n) * total_rows,
        state[n : 2 * n, :],
        state[2 * n : 3 * n, :],
        None,
        state[0:n, :],
        total_rows,
    )
    step = nn(zwt, w[...]) + nn(zpt, p[...])
    x_out[...] = nn(scale, x[...] + step)
    p_out[...] = nn(scale, step)


def run(kernel, name, outs, ins, scratch=(), smem=(), smem_outs=(), flops=1000000):
    in_specs = [pl.BlockSpec(memory_space=SMEM if i in smem else VMEM) for i in range(len(ins))]
    out_specs = [pl.BlockSpec(memory_space=SMEM if i in smem_outs else VMEM) for i in range(len(outs))]
    moved = sum(a.size * a.dtype.itemsize for a in ins) + sum(o.size * o.dtype.itemsize for o in outs)
    return pl.pallas_call(
        kernel,
        name=name,
        out_shape=outs,
        in_specs=in_specs,
        out_specs=out_specs,
        scratch_shapes=list(scratch),
        compiler_params=pltpu.CompilerParams(vmem_limit_bytes=48 * 1024 * 1024),
        cost_estimate=pl.CostEstimate(flops=flops, bytes_accessed=moved, transcendentals=0),
    )(*ins)


def shaped(*shape, dtype=f32):
    return jax.ShapeDtypeStruct(shape, dtype)


def local(n_sub, n_row, modes, search, precond, in_row, in_col, in_val, bnd_rows, if_row, if_src, if_val):
    nin, kb = in_val.shape[2], in_val.shape[3]
    rows, n = modes.shape
    lb = rows // kb
    ifr = bnd_rows.shape[2]
    groups = nin // lb
    n_z = n_sub // 2
    total_rows = float(rows * n_sub * n_row)
    halo_blocks = n_row * lb + n_sub * ifr
    bnd = bnd_rows[0, 0]
    me_row, me_sub = lax.axis_index("row"), lax.axis_index("sub")
    pos = jnp.stack([me_row, me_sub]).astype(jnp.int32)
    after = lax.optimization_barrier

    def row_send(value, k):
        return lax.ppermute(value, "row", [(r, r ^ k) for r in range(n_row)])

    def sub_send(value, k):
        return lax.ppermute(value, "sub", [(s, s ^ k) for s in range(n_sub)])

    def wire(*shape):
        return shaped(*shape, n, 2 * kb, dtype=bf16)

    def halo_of(own, edge):
        rows_got = [row_send(own, k) for k in range(1, n_row)]
        same = jnp.concatenate([edge] + [sub_send(edge, 2 * k) for k in range(1, n_z)], axis=0)
        return [own] + rows_got + [same, sub_send(same, 1)]

    def doubled(value):
        k = 1
        while k < n_row:
            value = value + row_send(value, k)
            k *= 2
        k = 2
        while k < n_sub:
            value = value + sub_send(value, k)
            k *= 2
        return value

    def sum_halves(keep, send):
        mine = doubled(keep + sub_send(send, 1))
        return [mine, sub_send(mine, 1)]

    def partials(wires, more):
        m, e = len(wires), 1 if more else 0
        outs = [shaped(m * lb, n, kb), shaped(m * n_z * ifr, n, kb), wire((m * n_z + e) * ifr)]
        outs += [wire((m + e) * lb)] * (n_row - 1)
        return run(
            functools.partial(partial_kernel, n_row, n_z, m, e > 0),
            "partials",
            outs,
            wires + [joined, where, pos] + more,
            [VMEM((halo_blocks, n, 2 * kb), f32)],
            smem=(m + 1, m + 2),
        )

    def send_partials(parts, m, more):
        own, keep, send, *row_parts = parts
        e = 1 if more else 0
        rows_got = [row_send(row_parts[k - 1], k) for k in range(1, n_row)]
        got = sub_send(send, 1)
        edge_own, *outs = run(
            functools.partial(pair_kernel, n_z, m, e > 0),
            "pair",
            [shaped(m * ifr, n, kb)] + [wire((m + 2 * e) * ifr)] * (n_z - 1),
            [keep, got, pos] + more,
            smem=(2,),
        )
        edges_got = [sub_send(outs[k - 1], 2 * k) for k in range(1, n_z)]
        return [own] + rows_got + [edge_own] + edges_got, got

    x, p = modes.T, search.T
    scaling = precond.reshape(1, rows)
    wire_shapes = [wire(lb), wire(ifr)]
    x_wire, x_edge = run(wire_kernel, "wire", wire_shapes, [x, bnd], smem=(1,))
    x_halo = halo_of(x_wire, x_edge)
    p_wire, p_edge = run(wire_kernel, "wire", wire_shapes, [p, bnd], smem=(1,))
    twice = jnp.concatenate([in_val[0, 0], in_val[0, 0]], axis=-1)
    twice_face = jnp.concatenate([if_val[0, 0], if_val[0, 0]], axis=-1)
    stored, joined, diagonal, where = run(
        functools.partial(prepare_kernel, groups, n_row * lb),
        "prepare",
        [
            shaped(lb, kb, groups * 2 * kb, dtype=bf16),
            shaped(lb, kb, groups * kb, dtype=bf16),
            shaped(lb, kb, 2 * kb, dtype=bf16),
            shaped(lb * groups, dtype=jnp.int32),
        ],
        [twice, twice_face, in_row[0, 0], in_col[0, 0], if_row[0, 0], if_src[0, 0]],
        smem=(2, 3, 4, 5),
        smem_outs=(3,),
    )
    x_parts = partials([x_wire], [p_wire, p_edge])
    blocks = [stored, diagonal, where, pos]
    halo_scratch = VMEM((halo_blocks, n, 2 * kb), bf16)
    back_scratch = VMEM((lb, n, kb), f32)
    whole = shaped(n, rows)

    count = len(x_halo)
    half_x, diag_x, table = run(
        functools.partial(x_image_kernel, n_row, n_z),
        "x_image",
        [whole, whole, shaped(n, 2 * n)],
        x_halo + blocks + [x],
        [halo_scratch],
        smem=(count + 2, count + 3),
    )
    table, x_parts = after((table, x_parts))
    table = doubled(table)
    table = table + sub_send(table, 1)
    x_back, core_got = send_partials(x_parts, 1, [p_edge])
    p_rows, p_edges = x_back[1:n_row], x_back[n_row + 1 :]
    count = len(x_back)
    ax, energy, w, w_wire, w_edge = run(
        functools.partial(update_kernel, n_row, n_z),
        "update",
        [whole, shaped(n, n), whole] + wire_shapes,
        x_back + [bnd, table, x, half_x, diag_x, scaling],
        [back_scratch],
        smem=(count,),
    )
    w_halo = halo_of(w_wire, w_edge)
    count = 1 + n_row + n_z
    half_p, diag_p = run(
        functools.partial(p_image_kernel, n_row, n_z, ifr),
        "p_image",
        [whole, whole],
        [p_wire, p_edge, core_got] + p_rows + p_edges + blocks,
        [halo_scratch],
        smem=(count + 2, count + 3),
    )
    w_parts = partials([p_wire, w_wire], [])

    def update_image(first, halo, w, x, p, ax, ap):
        count = len(halo)
        height = (5 if first else 3) * n
        return run(
            functools.partial(update_image_kernel, n_row, n_z, first),
            "update_image",
            [whole, whole, shaped(height // 2, 2 * n), shaped(height // 2, 2 * n)],
            halo + blocks + [w, x, p, ax, ap],
            [halo_scratch, VMEM((height, 2 * n), f32)],
            smem=(count + 2, count + 3),
        )

    half_w, diag_w, keep, send = update_image(True, w_halo, w, x, p, ax, half_p)
    keep, send, w_parts = after((keep, send, w_parts))
    halves = sum_halves(keep, send)
    w_back, _ = send_partials(w_parts, 2, [])
    count = len(w_back)
    x, ax, w, w_wire, w_edge, step_x, step_a, small = run(
        functools.partial(move_kernel, n_row, n_z, total_rows),
        "move",
        [whole] * 3 + wire_shapes + [whole, whole, shaped(4 * n, n)],
        w_back + halves + [pos, bnd, table, energy, x, p, ax, half_p, diag_p, w, half_w, diag_w, scaling],
        [VMEM((5 * n, 2 * n), f32), back_scratch],
        smem=(count + 2, count + 3),
    )
    w_halo = halo_of(w_wire, w_edge)
    p, ap, state = run(settle_kernel, "settle", [whole, whole, shaped(3 * n, n)], [small, step_x, step_a])
    _, _, keep, send = update_image(False, w_halo, w, x, p, ax, ap)
    halves = sum_halves(keep, send)
    x, p = run(
        functools.partial(finish_kernel, total_rows),
        "finish",
        [whole, whole],
        halves + [pos, state, x, p, w],
        [VMEM((3 * n, 2 * n), f32)],
        smem=(2,),
    )
    return (x.T, p.T)


def solution(mesh):
    return jax.shard_map(
        functools.partial(local, mesh.shape["sub"], mesh.shape["row"]),
        mesh=mesh,
        in_specs=(
            P(("sub", "row"), None),
            P(("sub", "row"), None),
            P(("sub", "row")),
            P("sub", "row", None),
            P("sub", "row", None),
            P("sub", "row", None, None, None),
            P("sub", "row", None),
            P("sub", "row", None),
            P("sub", "row", None),
            P("sub", "row", None, None, None),
        ),
        out_specs=(P(("sub", "row"), None), P(("sub", "row"), None)),
        check_vma=False,
    )
```

```python
import functools

import jax
import jax.numpy as jnp
from jax import lax
from jax.experimental import pallas as pl
from jax.experimental.pallas import tpu as pltpu
from jax.sharding import PartitionSpec as P

f32 = jnp.float32
bf16 = jnp.bfloat16
precise_mode = lax.Precision.HIGHEST
VMEM = pltpu.VMEM
SMEM = pltpu.SMEM


def nn(a, b):
    return lax.dot_general(a, b, (((1,), (0,)), ((), ())), precision=precise_mode, preferred_element_type=f32)


def nt(a, b):
    return lax.dot_general(a, b, (((1,), (1,)), ((), ())), precision=precise_mode, preferred_element_type=f32)


def two_parts(block):
    high = block.astype(bf16).astype(f32)
    return jnp.concatenate([high, block - high], axis=1).astype(bf16)


def write_wire(vector, bnd, wire, edge):
    blocks, kb = wire.shape[0], wire.shape[2] // 2
    for i in range(blocks):
        wire[i] = two_parts(vector[:, i * kb : (i + 1) * kb])
    for q in range(edge.shape[0]):
        edge[q] = wire[bnd[q]]


def fill_halo(wires, edges, pos, halo):
    n_row = len(wires)
    lb = wires[0].shape[0]
    for k, wire in enumerate(wires):
        start = (pos[0] ^ k) * lb
        for i in range(lb):
            halo[start + i] = wire[i]
    for k, pair in enumerate(edges):
        for other, (edge, offset, count) in enumerate(pair):
            start = n_row * lb + (((pos[1] // 2) ^ k) * 2 + ((pos[1] % 2) ^ other)) * count
            for q in range(count):
                halo[start + q] = edge[offset + q]


def write_halves(table, pos, keep, send):
    height = keep.shape[0]
    core = pos[1] % 2
    keep[...] = table[pl.ds(pl.multiple_of(core * height, 8), height), :]
    send[...] = table[pl.ds(pl.multiple_of((1 - core) * height, 8), height), :]


def read_halves(mine, other, pos, table):
    height = mine.shape[0]
    core = pos[1] % 2
    table[pl.ds(pl.multiple_of(core * height, 8), height), :] = mine[...]
    table[pl.ds(pl.multiple_of((1 - core) * height, 8), height), :] = other[...]


def forward(halo, wire, stored, diagonal, where, out, diag_out):
    lb, kb = wire.shape[0], wire.shape[2] // 2
    groups = stored.shape[2] // (2 * kb)
    for i in range(0, lb, 2):
        sums, diags = [], []
        for m in (i, i + 1):
            row = jnp.concatenate([halo[where[m * groups + g]] for g in range(groups)], axis=1)
            sums.append(lax.dot_general(row, stored[m], (((1,), (1,)), ((), ())), preferred_element_type=f32))
            diags.append(lax.dot_general(wire[m], diagonal[m], (((1,), (1,)), ((), ())), preferred_element_type=f32))
        out[:, i * kb : (i + 2) * kb] = jnp.concatenate(sums, axis=1)
        diag_out[:, i * kb : (i + 2) * kb] = jnp.concatenate(diags, axis=1)


def returned(index, own, rows, edge_own, edges, bnd, back):
    lb, kb = back.shape[0], back.shape[2]
    ifr = bnd.shape[0]
    for i in range(lb):
        total = rows[0][index * lb + i].astype(f32)
        for row in rows[1:]:
            total = total + row[index * lb + i].astype(f32)
        back[i] = own[index * lb + i] + (total[:, :kb] + total[:, kb:])
    for q in range(ifr):
        total = edges[0][index * ifr + q].astype(f32)
        for edge in edges[1:]:
            total = total + edge[index * ifr + q].astype(f32)
        back[bnd[q]] = back[bnd[q]] + edge_own[index * ifr + q] + (total[:, :kb] + total[:, kb:])


def add_returned(back, target):
    lb, kb = back.shape[0], back.shape[2]
    for i in range(0, lb, 2):
        span = slice(i * kb, (i + 2) * kb)
        target[:, span] = target[:, span] + jnp.concatenate([back[i], back[i + 1]], axis=1)


def eliminate(table, full):
    order = table.shape[0]
    rows = lax.broadcasted_iota(jnp.int32, table.shape, 0)
    for j in range(0, order, 2):
        left = jnp.broadcast_to(table[:, j : j + 1], table.shape)
        right = jnp.broadcast_to(table[:, j + 1 : j + 2], table.shape)
        one, two = table[j : j + 1, :], table[j + 1 : j + 2, :]
        over = 1.0 / left[j : j + 1, :]
        ratio = left[j + 1 : j + 2, :] * over
        beside = right[j : j + 1, :]
        two = two - ratio * one
        second = two * (1.0 / (right[j + 1 : j + 2, :] - ratio * beside))
        first = (one - beside * second) * over
        moved = table - left * first - right * second
        if full:
            table = jnp.where(rows == j, first, jnp.where(rows == j + 1, second, moved))
        else:
            table = jnp.where(rows > j + 1, moved, jnp.where(rows == j + 1, two, table))
    return table


def unit(order):
    return (
        lax.broadcasted_iota(jnp.int32, (order, order), 0) == lax.broadcasted_iota(jnp.int32, (order, order), 1)
    ).astype(f32)


def inverse(matrix):
    order = matrix.shape[0]
    return eliminate(jnp.concatenate([matrix, unit(order)], axis=1), True)[:, order:]


def cholesky_inverse(matrix):
    order = matrix.shape[0]
    done = eliminate(jnp.concatenate([matrix, unit(order)], axis=1), False)
    pivots = jnp.sum(done[:, :order] * unit(order), axis=1, keepdims=True)
    return done[:, order:] * (1.0 / jnp.sqrt(pivots))


def coefficients(table, gram, xp, pp, pax, pap_inverse, total_rows):
    n = gram.shape[0]
    waw, wap = table[0:n, :n], table[0:n, n:]
    wax, wx = table[n : 2 * n, :n], table[n : 2 * n, n:]
    wp, ww = table[2 * n : 3 * n, :n], table[2 * n : 3 * n, n:]
    waw = waw + waw.T
    first = nn(pap_inverse, wap.T)
    if pax is None:
        rhs = -wax
    else:
        second = nn(pap_inverse, pax)
        rhs = nn(wap, second) - wax
    schur = waw - nn(wap, first)
    zw = eliminate(jnp.concatenate([schur, rhs], axis=1), True)[:, n:]
    zp = -nn(first, zw)
    if pax is not None:
        zp = zp - second
    cross = nn(wx.T, zw) + nn(xp, zp)
    zwt, zpt = zw.T, zp.T
    inner = nn(zwt, nn(ww, zw) + nn(wp, zp)) + nn(zpt, nn(wp.T, zw) + nn(pp, zp))
    lengths = (gram + cross + cross.T + inner) / total_rows
    return zw, zp, zwt, zpt, cross, inner, wax, cholesky_inverse(lengths)


def prepare_kernel(groups, base, vals, faces, rows, cols, face_rows, face_src, stored, joined, diagonal, where):
    lb, kb = faces.shape[0], faces.shape[1]

    def twice(block):
        wide = block.astype(f32)
        return jnp.concatenate([wide, wide], axis=1).astype(bf16)

    for k in range(lb):
        diagonal[k] = twice(vals[k])
    for g in range(groups):
        half = (g % 2) * kb
        for m in range(lb):
            if g < groups - 1:
                k = (g + 1) * lb + m
                i, target, block = rows[k], cols[k], twice(vals[k])
            else:
                i, target, block = face_rows[m], base + face_src[m], twice(faces[m])
            stored[i, :, 2 * kb * g : 2 * kb * (g + 1)] = block
            joined[i, :, kb * g : kb * (g + 1)] = block[:, half : half + kb]
            where[i * groups + g] = target


def wire_kernel(vector, bnd, wire, edge):
    write_wire(vector, bnd, wire, edge)


def partial_kernel(n_row, n_z, count, *refs):
    refs = list(refs)
    take = lambda number: [refs.pop(0) for _ in range(number)]
    wires = take(count)
    joined, where, pos = take(3)
    own, core_keep, core_send = take(3)
    row_outs, acc = refs[:-1], refs[-1]
    lb, kb = wires[0].shape[0], wires[0].shape[2] // 2
    ifr = core_keep.shape[0] // (count * n_z)
    groups = joined.shape[2] // kb
    low = lax.broadcasted_iota(jnp.int32, (kb, 2 * kb), 1) < kb
    core = pos[1] % 2
    for v, wire in enumerate(wires):
        acc[...] = jnp.zeros(acc.shape, f32)
        for i in range(lb):
            blocks = jnp.concatenate([joined[i], joined[i]], axis=0)
            out = jnp.dot(wire[i], blocks, preferred_element_type=f32)
            for t in range(groups // 2):
                tile = out[:, 2 * kb * t : 2 * kb * (t + 1)]
                one = where[i * groups + 2 * t]
                two = where[i * groups + 2 * t + 1]
                acc[one] = acc[one] + jnp.where(low, tile, 0.0)
                acc[two] = acc[two] + jnp.where(low, 0.0, tile)

        def folded(index):
            block = acc[index]
            return block[:, :kb] + block[:, kb:]

        for k in range(n_row):
            start = (pos[0] ^ k) * lb
            for i in range(lb):
                if k == 0:
                    own[v * lb + i] = folded(start + i)
                else:
                    row_outs[k - 1][v * lb + i] = two_parts(folded(start + i))
        for z in range(n_z):
            for q in range(ifr):
                spot = (v * n_z + z) * ifr + q
                core_keep[spot] = folded(n_row * lb + (z * 2 + core) * ifr + q)
                core_send[spot] = two_parts(folded(n_row * lb + (z * 2 + 1 - core) * ifr + q))


def pair_kernel(n_z, count, keep, got, pos, own, *outs):
    ifr, kb = own.shape[0] // count, own.shape[2]
    for k in range(n_z):
        z = (pos[1] // 2) ^ k
        for v in range(count):
            for q in range(ifr):
                spot = (v * n_z + z) * ifr + q
                there = got[spot].astype(f32)
                total = keep[spot] + (there[:, :kb] + there[:, kb:])
                if k == 0:
                    own[v * ifr + q] = total
                else:
                    outs[k - 1][v * ifr + q] = two_parts(total)


def split_halo(refs, n_row, n_z):
    wires = [refs.pop(0) for _ in range(n_row)]
    same, other = refs.pop(0), refs.pop(0)
    ifr = same.shape[0] // n_z
    return wires, [((same, k * ifr, ifr), (other, k * ifr, ifr)) for k in range(n_z)]


def x_image_kernel(n_row, n_z, *refs):
    refs = list(refs)
    wires, edges = split_halo(refs, n_row, n_z)
    stored, diagonal, where, pos, x, p, half, diag, table, halo = refs
    n = x.shape[0]
    fill_halo(wires, edges, pos, halo)
    forward(halo, wires[0], stored, diagonal, where, half, diag)
    half[...] = half[...] + 0.5 * diag[...]
    table[0:n, :] = nt(x[...], jnp.concatenate([half[...], x[...]], axis=0))
    table[n : 2 * n, :] = nt(p[...], jnp.concatenate([x[...], p[...]], axis=0))


def p_image_kernel(n_row, n_z, *refs):
    refs = list(refs)
    wires, edges = split_halo(refs, n_row, n_z)
    stored, diagonal, where, pos, x, half_x, p, before, half, diag, keep, send, halo, table = refs
    n = x.shape[0]
    fill_halo(wires, edges, pos, halo)
    forward(halo, wires[0], stored, diagonal, where, half, diag)
    half[...] = half[...] + 0.5 * diag[...]
    table[0 : 2 * n, :] = before[...]
    table[2 * n : 3 * n, :] = nt(p[...], jnp.concatenate([half[...], half_x[...]], axis=0))
    table[2 * n : 3 * n, n:] = table[2 * n : 3 * n, n:] + nt(half[...], x[...])
    write_halves(table, pos, keep, send)


def take_returned(refs, n_row, n_z):
    own = refs.pop(0)
    rows = [refs.pop(0) for _ in range(n_row - 1)]
    edge_own = refs.pop(0)
    return own, rows, edge_own, [refs.pop(0) for _ in range(n_z - 1)]


def update_kernel(n_row, n_z, *refs):
    refs = list(refs)
    back_parts = take_returned(refs, n_row, n_z)
    mine, other, pos, bnd, x, half, diag, precond, table, ax, energy, w, wire, edge, back = refs
    n = x.shape[0]
    read_halves(mine, other, pos, table)
    returned(0, *back_parts, bnd, back)
    ax[...] = half[...] + 0.5 * diag[...]
    add_returned(back, ax)
    stored, gram = table[0:n, 0:n], table[0:n, n:]
    total = stored + stored.T
    energy[...] = total
    ritz = nn(total, inverse(0.5 * (gram + gram.T)))
    w[...] = precond[...] * (ax[...] - nn(ritz, x[...]))
    write_wire(w, bnd, wire, edge)


def inverse_kernel(table, solved):
    n = solved.shape[0]
    stored = table[2 * n : 3 * n, 0:n]
    solved[...] = inverse(stored + stored.T)


def update_image_kernel(n_row, n_z, first, *refs):
    refs = list(refs)
    wires, edges = split_halo(refs, n_row, n_z)
    stored, diagonal, where, pos, w, x, p, ax, ap, half, diag, keep, send, halo, table = refs
    n = w.shape[0]
    fill_halo(wires, edges, pos, halo)
    forward(halo, wires[0], stored, diagonal, where, half, diag)
    half[...] = half[...] + 0.5 * diag[...]
    here = w[...]
    table[0:n, :] = nt(here, jnp.concatenate([half[...], ap[...]], axis=0))
    table[n : 2 * n, :] = nt(here, jnp.concatenate([ax[...], x[...]], axis=0))
    table[2 * n : 3 * n, :] = nt(here, jnp.concatenate([p[...], here], axis=0))
    if first:
        table[0:n, n:] = table[0:n, n:] + nt(half[...], p[...])
    write_halves(table, pos, keep, send)


def move_kernel(n_row, n_z, total_rows, *refs):
    refs = list(refs)
    back_parts = take_returned(refs, n_row, n_z)
    mine, other, pos, bnd, start, energy, pap_inverse, x, p, ax, ap, ap_diag, w, aw, aw_diag, precond = refs[:16]
    x_out, ax_out, w_out, wire, edge, step_x, step_a, small, table, back = refs[16:]
    n = x.shape[0]
    read_halves(mine, other, pos, table)
    gram = start[0:n, n:]
    px, pp = start[n : 2 * n, 0:n], start[n : 2 * n, n:]
    pax = start[2 * n : 3 * n, n:]
    zw, zp, zwt, zpt, cross, inner, wax, scale = coefficients(
        table, 0.5 * (gram + gram.T), px.T, pp, pax, pap_inverse[...], total_rows
    )
    step_a[...] = nn(zpt, ap[...] + 0.5 * ap_diag[...]) + nn(zwt, aw[...] + 0.5 * aw_diag[...])
    returned(0, *back_parts, bnd, back)
    for i in range(0, back.shape[0], 2):
        pair = jnp.concatenate([back[i], back[i + 1]], axis=1)
        span = slice(i * back.shape[2], (i + 2) * back.shape[2])
        step_a[:, span] = step_a[:, span] + nn(zpt, pair)
    returned(1, *back_parts, bnd, back)
    for i in range(0, back.shape[0], 2):
        pair = jnp.concatenate([back[i], back[i + 1]], axis=1)
        span = slice(i * back.shape[2], (i + 2) * back.shape[2])
        step_a[:, span] = step_a[:, span] + nn(zwt, pair)
    step_x[...] = nn(zwt, w[...]) + nn(zpt, p[...])
    x_out[...] = nn(scale, x[...] + step_x[...])
    ax_out[...] = nn(scale, ax[...] + step_a[...])
    gain = nn(wax.T, zw) + nn(pax.T, zp)
    gain = 0.5 * (gain + gain.T)
    ritz = nn(scale, nn(energy[...] + gain, scale.T)) / total_rows
    w_out[...] = precond[...] * (ax_out[...] - nn(ritz, x_out[...]))
    write_wire(w_out, bnd, wire, edge)
    small[0:n, :] = -gain
    small[n : 2 * n, :] = cross + inner
    small[2 * n : 3 * n, :] = inner
    small[3 * n : 4 * n, :] = scale


def settle_kernel(small, step_x, step_a, p_out, ap_out, state):
    n = small.shape[1]
    scale = small[3 * n : 4 * n, :]
    scale_t = scale.T
    p_out[...] = nn(scale, step_x[...])
    ap_out[...] = nn(scale, step_a[...])
    state[0:n, :] = inverse(nn(scale, nn(small[0:n, :], scale_t)))
    state[n : 2 * n, :] = nn(scale, nn(small[n : 2 * n, :], scale_t))
    state[2 * n : 3 * n, :] = nn(scale, nn(small[2 * n : 3 * n, :], scale_t))


def finish_kernel(total_rows, mine, other, pos, state, x, p, w, x_out, p_out, table):
    n = x.shape[0]
    read_halves(mine, other, pos, table)
    zw, zp, zwt, zpt, _, _, _, scale = coefficients(
        table,
        unit(n) * total_rows,
        state[n : 2 * n, :],
        state[2 * n : 3 * n, :],
        None,
        state[0:n, :],
        total_rows,
    )
    step = nn(zwt, w[...]) + nn(zpt, p[...])
    x_out[...] = nn(scale, x[...] + step)
    p_out[...] = nn(scale, step)


def run(kernel, name, outs, ins, scratch=(), smem=(), smem_outs=(), flops=1000000):
    in_specs = [pl.BlockSpec(memory_space=SMEM if i in smem else VMEM) for i in range(len(ins))]
    out_specs = [pl.BlockSpec(memory_space=SMEM if i in smem_outs else VMEM) for i in range(len(outs))]
    moved = sum(a.size * a.dtype.itemsize for a in ins) + sum(o.size * o.dtype.itemsize for o in outs)
    return pl.pallas_call(
        kernel,
        name=name,
        out_shape=outs,
        in_specs=in_specs,
        out_specs=out_specs,
        scratch_shapes=list(scratch),
        compiler_params=pltpu.CompilerParams(vmem_limit_bytes=48 * 1024 * 1024),
        cost_estimate=pl.CostEstimate(flops=flops, bytes_accessed=moved, transcendentals=0),
    )(*ins)


def shaped(*shape, dtype=f32):
    return jax.ShapeDtypeStruct(shape, dtype)


def local(n_sub, n_row, modes, search, precond, in_row, in_col, in_val, bnd_rows, if_row, if_src, if_val):
    nin, kb = in_val.shape[2], in_val.shape[3]
    rows, n = modes.shape
    lb = rows // kb
    ifr = bnd_rows.shape[2]
    groups = nin // lb
    n_z = n_sub // 2
    total_rows = float(rows * n_sub * n_row)
    halo_blocks = n_row * lb + n_sub * ifr
    bnd = bnd_rows[0, 0]
    me_row, me_sub = lax.axis_index("row"), lax.axis_index("sub")
    pos = jnp.stack([me_row, me_sub]).astype(jnp.int32)
    after = lax.optimization_barrier

    def row_send(value, k):
        return lax.ppermute(value, "row", [(r, r ^ k) for r in range(n_row)])

    def sub_send(value, k):
        return lax.ppermute(value, "sub", [(s, s ^ k) for s in range(n_sub)])

    def wire(*shape):
        return shaped(*shape, n, 2 * kb, dtype=bf16)

    def halo_of(own, edge):
        rows_got = [row_send(own, k) for k in range(1, n_row)]
        same = jnp.concatenate([edge] + [sub_send(edge, 2 * k) for k in range(1, n_z)], axis=0)
        return [own] + rows_got + [same, sub_send(same, 1)]

    def sum_halves(keep, send):
        total = keep + sub_send(send, 1)
        k = 1
        while k < n_row:
            total = total + row_send(total, k)
            k *= 2
        k = 2
        while k < n_sub:
            total = total + sub_send(total, k)
            k *= 2
        return [total, sub_send(total, 1)]

    def partials(wires):
        m = len(wires)
        outs = [shaped(m * lb, n, kb), shaped(m * n_z * ifr, n, kb), wire(m * n_z * ifr)]
        outs += [wire(m * lb)] * (n_row - 1)
        return run(
            functools.partial(partial_kernel, n_row, n_z, m),
            "partials",
            outs,
            wires + [joined, where, pos],
            [VMEM((halo_blocks, n, 2 * kb), f32)],
            smem=(m + 1, m + 2),
        )

    def sum_with_partials(keep, send, parts, m):
        own, edge_keep, edge_send, *row_parts = parts
        total = keep + sub_send(send, 1)
        edge_got = sub_send(edge_send, 1)
        rows_got = [row_send(row_parts[k - 1], k) for k in range(1, n_row)]
        edge_own, *outs = run(
            functools.partial(pair_kernel, n_z, m),
            "pair",
            [shaped(m * ifr, n, kb)] + [wire(m * ifr)] * (n_z - 1),
            [edge_keep, edge_got, pos],
            smem=(2,),
        )
        k = 2
        while k < n_sub:
            total = total + sub_send(total, k)
            k *= 2
        total, *outs = after((total, *outs))
        edges_got = [sub_send(outs[k - 1], 2 * k) for k in range(1, n_z)]
        k = 1
        while k < n_row:
            total = total + row_send(total, k)
            k *= 2
        return [total, sub_send(total, 1)], [own] + rows_got + [edge_own] + edges_got

    x, p = modes.T, search.T
    scaling = precond.reshape(1, rows)
    wire_shapes = [wire(lb), wire(ifr)]
    x_wire, x_edge = run(wire_kernel, "wire", wire_shapes, [x, bnd], smem=(1,))
    x_halo = halo_of(x_wire, x_edge)
    p_wire, p_edge = run(wire_kernel, "wire", wire_shapes, [p, bnd], smem=(1,))
    stored, joined, diagonal, where = run(
        functools.partial(prepare_kernel, groups, n_row * lb),
        "prepare",
        [
            shaped(lb, kb, groups * 2 * kb, dtype=bf16),
            shaped(lb, kb, groups * kb, dtype=bf16),
            shaped(lb, kb, 2 * kb, dtype=bf16),
            shaped(lb * groups, dtype=jnp.int32),
        ],
        [in_val[0, 0], if_val[0, 0], in_row[0, 0], in_col[0, 0], if_row[0, 0], if_src[0, 0]],
        smem=(2, 3, 4, 5),
        smem_outs=(3,),
    )
    p_wire, p_edge, *x_got = after((p_wire, p_edge, *x_halo[1:]))
    x_halo = [x_wire] + x_got
    p_halo = halo_of(p_wire, p_edge)
    x_parts = partials([x_wire])
    blocks = [stored, diagonal, where, pos]
    halo_scratch = VMEM((halo_blocks, n, 2 * kb), bf16)
    back_scratch = VMEM((lb, n, kb), f32)
    whole = shaped(n, rows)

    count = len(x_halo)
    half_x, diag_x, table = run(
        functools.partial(x_image_kernel, n_row, n_z),
        "x_image",
        [whole, whole, shaped(2 * n, 2 * n)],
        x_halo + blocks + [x, p],
        [halo_scratch],
        smem=(count + 2, count + 3),
    )
    table_shape = shaped(3 * n, 2 * n)
    halves_shape = [shaped(3 * n // 2, 2 * n)] * 2
    table_scratch = VMEM((3 * n, 2 * n), f32)
    half_p, diag_p, keep, send = run(
        functools.partial(p_image_kernel, n_row, n_z),
        "p_image",
        [whole, whole] + halves_shape,
        p_halo + blocks + [x, half_x, p, table],
        [halo_scratch, table_scratch],
        smem=(count + 2, count + 3),
    )
    keep, send, x_parts = after((keep, send, x_parts))
    halves, x_back = sum_with_partials(keep, send, x_parts, 1)
    count = len(x_back)
    table, ax, energy, w, w_wire, w_edge = run(
        functools.partial(update_kernel, n_row, n_z),
        "update",
        [table_shape, whole, shaped(n, n), whole] + wire_shapes,
        x_back + halves + [pos, bnd, x, half_x, diag_x, scaling],
        [back_scratch],
        smem=(count + 2, count + 3),
    )
    w_halo = halo_of(w_wire, w_edge)
    (pap_inverse,) = run(inverse_kernel, "pap_inverse", [shaped(n, n)], [table])
    w_parts = partials([p_wire, w_wire])

    def update_image(first, halo, w, x, p, ax, ap):
        count = len(halo)
        return run(
            functools.partial(update_image_kernel, n_row, n_z, first),
            "update_image",
            [whole, whole] + halves_shape,
            halo + blocks + [w, x, p, ax, ap],
            [halo_scratch, table_scratch],
            smem=(count + 2, count + 3),
        )

    half_w, diag_w, keep, send = update_image(True, w_halo, w, x, p, ax, half_p)
    keep, send, w_parts = after((keep, send, w_parts))
    halves, w_back = sum_with_partials(keep, send, w_parts, 2)
    count = len(w_back)
    x, ax, w, w_wire, w_edge, step_x, step_a, small = run(
        functools.partial(move_kernel, n_row, n_z, total_rows),
        "move",
        [whole] * 3 + wire_shapes + [whole, whole, shaped(4 * n, n)],
        w_back + halves + [pos, bnd, table, energy, pap_inverse, x, p, ax, half_p, diag_p, w, half_w, diag_w, scaling],
        [table_scratch, back_scratch],
        smem=(count + 2, count + 3),
    )
    w_halo = halo_of(w_wire, w_edge)
    p, ap, state = run(settle_kernel, "settle", [whole, whole, shaped(3 * n, n)], [small, step_x, step_a])
    _, _, keep, send = update_image(False, w_halo, w, x, p, ax, ap)
    halves = sum_halves(keep, send)
    x, p = run(
        functools.partial(finish_kernel, total_rows),
        "finish",
        [whole, whole],
        halves + [pos, state, x, p, w],
        [table_scratch],
        smem=(2,),
    )
    return (x.T, p.T)


def solution(mesh):
    return jax.shard_map(
        functools.partial(local, mesh.shape["sub"], mesh.shape["row"]),
        mesh=mesh,
        in_specs=(
            P(("sub", "row"), None),
            P(("sub", "row"), None),
            P(("sub", "row")),
            P("sub", "row", None),
            P("sub", "row", None),
            P("sub", "row", None, None, None),
            P("sub", "row", None),
            P("sub", "row", None),
            P("sub", "row", None),
            P("sub", "row", None, None, None),
        ),
        out_specs=(P(("sub", "row"), None), P(("sub", "row"), None)),
        check_vma=False,
    )
```

```python
import functools

import jax
import jax.numpy as jnp
from jax import lax
from jax.experimental import pallas as pl
from jax.experimental.pallas import tpu as pltpu
from jax.sharding import PartitionSpec as P

f32 = jnp.float32
bf16 = jnp.bfloat16
precise_mode = lax.Precision.HIGHEST
VMEM = pltpu.VMEM
SMEM = pltpu.SMEM


def nn(a, b):
    return lax.dot_general(a, b, (((1,), (0,)), ((), ())), precision=precise_mode, preferred_element_type=f32)


def nt(a, b):
    return lax.dot_general(a, b, (((1,), (1,)), ((), ())), precision=precise_mode, preferred_element_type=f32)


def two_parts(block):
    high = block.astype(bf16).astype(f32)
    return jnp.concatenate([high, block - high], axis=1).astype(bf16)


def write_wire(vector, bnd, wire, edge):
    blocks, kb = wire.shape[0], wire.shape[2] // 2
    for i in range(blocks):
        wire[i] = two_parts(vector[:, i * kb : (i + 1) * kb])
    for q in range(edge.shape[0]):
        edge[q] = wire[bnd[q]]


def fill_halo(wires, edges, pos, halo):
    n_row = len(wires)
    lb = wires[0].shape[0]
    for k, wire in enumerate(wires):
        start = (pos[0] ^ k) * lb
        for i in range(lb):
            halo[start + i] = wire[i]
    for k, pair in enumerate(edges):
        for other, (edge, offset, count) in enumerate(pair):
            start = n_row * lb + (((pos[1] // 2) ^ k) * 2 + ((pos[1] % 2) ^ other)) * count
            for q in range(count):
                halo[start + q] = edge[offset + q]


def write_halves(table, pos, keep, send):
    height = keep.shape[0]
    core = pos[1] % 2
    keep[...] = table[pl.ds(pl.multiple_of(core * height, 8), height), :]
    send[...] = table[pl.ds(pl.multiple_of((1 - core) * height, 8), height), :]


def read_halves(mine, other, pos, table):
    height = mine.shape[0]
    core = pos[1] % 2
    table[pl.ds(pl.multiple_of(core * height, 8), height), :] = mine[...]
    table[pl.ds(pl.multiple_of((1 - core) * height, 8), height), :] = other[...]


def forward(halo, wire, stored, diagonal, where, out, diag_out):
    lb, kb = wire.shape[0], wire.shape[2] // 2
    groups = stored.shape[2] // (2 * kb)
    for i in range(0, lb, 2):
        sums, diags = [], []
        for m in (i, i + 1):
            row = jnp.concatenate([halo[where[m * groups + g]] for g in range(groups)], axis=1)
            sums.append(lax.dot_general(row, stored[m], (((1,), (1,)), ((), ())), preferred_element_type=f32))
            diags.append(lax.dot_general(wire[m], diagonal[m], (((1,), (1,)), ((), ())), preferred_element_type=f32))
        out[:, i * kb : (i + 2) * kb] = jnp.concatenate(sums, axis=1)
        diag_out[:, i * kb : (i + 2) * kb] = jnp.concatenate(diags, axis=1)


def returned(index, own, rows, edge_own, edges, bnd, back):
    lb, kb = back.shape[0], back.shape[2]
    ifr = bnd.shape[0]
    for i in range(lb):
        total = rows[0][index * lb + i].astype(f32)
        for row in rows[1:]:
            total = total + row[index * lb + i].astype(f32)
        back[i] = own[index * lb + i] + (total[:, :kb] + total[:, kb:])
    for q in range(ifr):
        total = edges[0][index * ifr + q].astype(f32)
        for edge in edges[1:]:
            total = total + edge[index * ifr + q].astype(f32)
        back[bnd[q]] = back[bnd[q]] + edge_own[index * ifr + q] + (total[:, :kb] + total[:, kb:])


def add_returned(back, target):
    lb, kb = back.shape[0], back.shape[2]
    for i in range(0, lb, 2):
        span = slice(i * kb, (i + 2) * kb)
        target[:, span] = target[:, span] + jnp.concatenate([back[i], back[i + 1]], axis=1)


def eliminate(table, full):
    order = table.shape[0]
    rows = lax.broadcasted_iota(jnp.int32, table.shape, 0)
    for j in range(0, order, 2):
        left = jnp.broadcast_to(table[:, j : j + 1], table.shape)
        right = jnp.broadcast_to(table[:, j + 1 : j + 2], table.shape)
        one, two = table[j : j + 1, :], table[j + 1 : j + 2, :]
        over = 1.0 / left[j : j + 1, :]
        ratio = left[j + 1 : j + 2, :] * over
        beside = right[j : j + 1, :]
        two = two - ratio * one
        second = two * (1.0 / (right[j + 1 : j + 2, :] - ratio * beside))
        first = (one - beside * second) * over
        moved = table - left * first - right * second
        if full:
            table = jnp.where(rows == j, first, jnp.where(rows == j + 1, second, moved))
        else:
            table = jnp.where(rows > j + 1, moved, jnp.where(rows == j + 1, two, table))
    return table


def unit(order):
    return (
        lax.broadcasted_iota(jnp.int32, (order, order), 0) == lax.broadcasted_iota(jnp.int32, (order, order), 1)
    ).astype(f32)


def inverse(matrix):
    order = matrix.shape[0]
    return eliminate(jnp.concatenate([matrix, unit(order)], axis=1), True)[:, order:]


def cholesky_inverse(matrix):
    order = matrix.shape[0]
    done = eliminate(jnp.concatenate([matrix, unit(order)], axis=1), False)
    pivots = jnp.sum(done[:, :order] * unit(order), axis=1, keepdims=True)
    return done[:, order:] * (1.0 / jnp.sqrt(pivots))


def coefficients(table, gram, xp, pp, pax, pap_inverse, total_rows):
    n = gram.shape[0]
    waw, wap = table[0:n, :n], table[0:n, n:]
    wax, wx = table[n : 2 * n, :n], table[n : 2 * n, n:]
    wp, ww = table[2 * n : 3 * n, :n], table[2 * n : 3 * n, n:]
    waw = waw + waw.T
    first = nn(pap_inverse, wap.T)
    if pax is None:
        rhs = -wax
    else:
        second = nn(pap_inverse, pax)
        rhs = nn(wap, second) - wax
    schur = waw - nn(wap, first)
    zw = eliminate(jnp.concatenate([schur, rhs], axis=1), True)[:, n:]
    zp = -nn(first, zw)
    if pax is not None:
        zp = zp - second
    cross = nn(wx.T, zw) + nn(xp, zp)
    zwt, zpt = zw.T, zp.T
    inner = nn(zwt, nn(ww, zw) + nn(wp, zp)) + nn(zpt, nn(wp.T, zw) + nn(pp, zp))
    lengths = (gram + cross + cross.T + inner) / total_rows
    return zw, zp, zwt, zpt, cross, inner, wax, cholesky_inverse(lengths)


def prepare_kernel(groups, base, vals, faces, rows, cols, face_rows, face_src, stored, joined, diagonal, where):
    lb, kb = faces.shape[0], faces.shape[1]

    def twice(block):
        wide = block.astype(f32)
        return jnp.concatenate([wide, wide], axis=1).astype(bf16)

    for k in range(lb):
        diagonal[k] = twice(vals[k])
    for g in range(groups):
        half = (g % 2) * kb
        for m in range(lb):
            if g < groups - 1:
                k = (g + 1) * lb + m
                i, target, block = rows[k], cols[k], twice(vals[k])
            else:
                i, target, block = face_rows[m], base + face_src[m], twice(faces[m])
            stored[i, :, 2 * kb * g : 2 * kb * (g + 1)] = block
            joined[i, :, kb * g : kb * (g + 1)] = block[:, half : half + kb]
            where[i * groups + g] = target


def wire_kernel(vector, bnd, wire, edge):
    write_wire(vector, bnd, wire, edge)


def partial_kernel(n_row, n_z, merge, wire, joined, where, pos, *refs):
    refs = list(refs)
    parts = n_row + 2
    earlier = [refs.pop(0) for _ in range(parts)] if merge else []
    outs, acc = refs[:-1], refs[-1]
    own, core_keep, core_send, *row_outs = outs
    lb, kb = wire.shape[0], wire.shape[2] // 2
    ifr = core_keep.shape[0] // (n_z * (2 if merge else 1))
    groups = joined.shape[2] // kb
    low = lax.broadcasted_iota(jnp.int32, (kb, 2 * kb), 1) < kb
    core = pos[1] % 2
    for source, target in zip(earlier, outs):
        target[pl.ds(0, source.shape[0])] = source[...]
    row_base = lb if merge else 0
    edge_base = n_z * ifr if merge else 0
    acc[...] = jnp.zeros(acc.shape, f32)
    for i in range(lb):
        blocks = jnp.concatenate([joined[i], joined[i]], axis=0)
        out = jnp.dot(wire[i], blocks, preferred_element_type=f32)
        for t in range(groups // 2):
            tile = out[:, 2 * kb * t : 2 * kb * (t + 1)]
            one = where[i * groups + 2 * t]
            two = where[i * groups + 2 * t + 1]
            acc[one] = acc[one] + jnp.where(low, tile, 0.0)
            acc[two] = acc[two] + jnp.where(low, 0.0, tile)

    def folded(index):
        block = acc[index]
        return block[:, :kb] + block[:, kb:]

    for k in range(n_row):
        start = (pos[0] ^ k) * lb
        for i in range(lb):
            if k == 0:
                own[row_base + i] = folded(start + i)
            else:
                row_outs[k - 1][row_base + i] = two_parts(folded(start + i))
    for z in range(n_z):
        for q in range(ifr):
            spot = edge_base + z * ifr + q
            core_keep[spot] = folded(n_row * lb + (z * 2 + core) * ifr + q)
            core_send[spot] = two_parts(folded(n_row * lb + (z * 2 + 1 - core) * ifr + q))


def pair_kernel(n_z, count, keep, got, pos, own, *outs):
    ifr, kb = own.shape[0] // count, own.shape[2]
    for k in range(n_z):
        z = (pos[1] // 2) ^ k
        for v in range(count):
            for q in range(ifr):
                spot = (v * n_z + z) * ifr + q
                there = got[spot].astype(f32)
                total = keep[spot] + (there[:, :kb] + there[:, kb:])
                if k == 0:
                    own[v * ifr + q] = total
                else:
                    outs[k - 1][v * ifr + q] = two_parts(total)


def split_halo(refs, n_row, n_z):
    wires = [refs.pop(0) for _ in range(n_row)]
    same, other = refs.pop(0), refs.pop(0)
    ifr = same.shape[0] // n_z
    return wires, [((same, k * ifr, ifr), (other, k * ifr, ifr)) for k in range(n_z)]


def x_image_kernel(n_row, n_z, *refs):
    refs = list(refs)
    wires, edges = split_halo(refs, n_row, n_z)
    stored, diagonal, where, pos, x, p, half, diag, table, halo = refs
    n = x.shape[0]
    fill_halo(wires, edges, pos, halo)
    forward(halo, wires[0], stored, diagonal, where, half, diag)
    half[...] = half[...] + 0.5 * diag[...]
    table[0:n, :] = nt(x[...], jnp.concatenate([half[...], x[...]], axis=0))
    table[n : 2 * n, :] = nt(p[...], jnp.concatenate([x[...], p[...]], axis=0))


def p_image_kernel(n_row, n_z, *refs):
    refs = list(refs)
    wires, edges = split_halo(refs, n_row, n_z)
    stored, diagonal, where, pos, x, half_x, p, before, half, diag, keep, send, halo, table = refs
    n = x.shape[0]
    fill_halo(wires, edges, pos, halo)
    forward(halo, wires[0], stored, diagonal, where, half, diag)
    half[...] = half[...] + 0.5 * diag[...]
    table[0 : 2 * n, :] = before[...]
    table[2 * n : 3 * n, :] = nt(p[...], jnp.concatenate([half[...], half_x[...]], axis=0))
    table[2 * n : 3 * n, n:] = table[2 * n : 3 * n, n:] + nt(half[...], x[...])
    write_halves(table, pos, keep, send)


def take_returned(refs, n_row, n_z):
    own = refs.pop(0)
    rows = [refs.pop(0) for _ in range(n_row - 1)]
    edge_own = refs.pop(0)
    return own, rows, edge_own, [refs.pop(0) for _ in range(n_z - 1)]


def update_kernel(n_row, n_z, *refs):
    refs = list(refs)
    back_parts = take_returned(refs, n_row, n_z)
    mine, other, pos, bnd, x, half, diag, precond, table, ax, energy, w, wire, edge, back = refs
    n = x.shape[0]
    read_halves(mine, other, pos, table)
    returned(0, *back_parts, bnd, back)
    ax[...] = half[...] + 0.5 * diag[...]
    add_returned(back, ax)
    stored, gram = table[0:n, 0:n], table[0:n, n:]
    total = stored + stored.T
    energy[...] = total
    ritz = nn(total, inverse(0.5 * (gram + gram.T)))
    w[...] = precond[...] * (ax[...] - nn(ritz, x[...]))
    write_wire(w, bnd, wire, edge)


def inverse_kernel(table, solved):
    n = solved.shape[0]
    stored = table[2 * n : 3 * n, 0:n]
    solved[...] = inverse(stored + stored.T)


def update_image_kernel(n_row, n_z, first, *refs):
    refs = list(refs)
    wires, edges = split_halo(refs, n_row, n_z)
    stored, diagonal, where, pos, w, x, p, ax, ap, half, diag, keep, send, halo, table = refs
    n = w.shape[0]
    fill_halo(wires, edges, pos, halo)
    forward(halo, wires[0], stored, diagonal, where, half, diag)
    half[...] = half[...] + 0.5 * diag[...]
    here = w[...]
    table[0:n, :] = nt(here, jnp.concatenate([half[...], ap[...]], axis=0))
    table[n : 2 * n, :] = nt(here, jnp.concatenate([ax[...], x[...]], axis=0))
    table[2 * n : 3 * n, :] = nt(here, jnp.concatenate([p[...], here], axis=0))
    if first:
        table[0:n, n:] = table[0:n, n:] + nt(half[...], p[...])
    write_halves(table, pos, keep, send)


def move_kernel(n_row, n_z, total_rows, *refs):
    refs = list(refs)
    back_parts = take_returned(refs, n_row, n_z)
    mine, other, pos, bnd, start, energy, pap_inverse, x, p, ax, ap, ap_diag, w, aw, aw_diag, precond = refs[:16]
    x_out, ax_out, w_out, wire, edge, step_x, step_a, small, table, back = refs[16:]
    n = x.shape[0]
    read_halves(mine, other, pos, table)
    gram = start[0:n, n:]
    px, pp = start[n : 2 * n, 0:n], start[n : 2 * n, n:]
    pax = start[2 * n : 3 * n, n:]
    zw, zp, zwt, zpt, cross, inner, wax, scale = coefficients(
        table, 0.5 * (gram + gram.T), px.T, pp, pax, pap_inverse[...], total_rows
    )
    step_a[...] = nn(zpt, ap[...] + 0.5 * ap_diag[...]) + nn(zwt, aw[...] + 0.5 * aw_diag[...])
    returned(0, *back_parts, bnd, back)
    for i in range(0, back.shape[0], 2):
        pair = jnp.concatenate([back[i], back[i + 1]], axis=1)
        span = slice(i * back.shape[2], (i + 2) * back.shape[2])
        step_a[:, span] = step_a[:, span] + nn(zpt, pair)
    returned(1, *back_parts, bnd, back)
    for i in range(0, back.shape[0], 2):
        pair = jnp.concatenate([back[i], back[i + 1]], axis=1)
        span = slice(i * back.shape[2], (i + 2) * back.shape[2])
        step_a[:, span] = step_a[:, span] + nn(zwt, pair)
    step_x[...] = nn(zwt, w[...]) + nn(zpt, p[...])
    x_out[...] = nn(scale, x[...] + step_x[...])
    ax_out[...] = nn(scale, ax[...] + step_a[...])
    gain = nn(wax.T, zw) + nn(pax.T, zp)
    gain = 0.5 * (gain + gain.T)
    ritz = nn(scale, nn(energy[...] + gain, scale.T)) / total_rows
    w_out[...] = precond[...] * (ax_out[...] - nn(ritz, x_out[...]))
    write_wire(w_out, bnd, wire, edge)
    small[0:n, :] = -gain
    small[n : 2 * n, :] = cross + inner
    small[2 * n : 3 * n, :] = inner
    small[3 * n : 4 * n, :] = scale


def settle_kernel(small, step_x, step_a, p_out, ap_out, state):
    n = small.shape[1]
    scale = small[3 * n : 4 * n, :]
    scale_t = scale.T
    p_out[...] = nn(scale, step_x[...])
    ap_out[...] = nn(scale, step_a[...])
    state[0:n, :] = inverse(nn(scale, nn(small[0:n, :], scale_t)))
    state[n : 2 * n, :] = nn(scale, nn(small[n : 2 * n, :], scale_t))
    state[2 * n : 3 * n, :] = nn(scale, nn(small[2 * n : 3 * n, :], scale_t))


def finish_kernel(total_rows, mine, other, pos, state, x, p, w, x_out, p_out, table):
    n = x.shape[0]
    read_halves(mine, other, pos, table)
    zw, zp, zwt, zpt, _, _, _, scale = coefficients(
        table,
        unit(n) * total_rows,
        state[n : 2 * n, :],
        state[2 * n : 3 * n, :],
        None,
        state[0:n, :],
        total_rows,
    )
    step = nn(zwt, w[...]) + nn(zpt, p[...])
    x_out[...] = nn(scale, x[...] + step)
    p_out[...] = nn(scale, step)


def run(kernel, name, outs, ins, scratch=(), smem=(), smem_outs=(), flops=1000000):
    in_specs = [pl.BlockSpec(memory_space=SMEM if i in smem else VMEM) for i in range(len(ins))]
    out_specs = [pl.BlockSpec(memory_space=SMEM if i in smem_outs else VMEM) for i in range(len(outs))]
    moved = sum(a.size * a.dtype.itemsize for a in ins) + sum(o.size * o.dtype.itemsize for o in outs)
    return pl.pallas_call(
        kernel,
        name=name,
        out_shape=outs,
        in_specs=in_specs,
        out_specs=out_specs,
        scratch_shapes=list(scratch),
        compiler_params=pltpu.CompilerParams(vmem_limit_bytes=48 * 1024 * 1024),
        cost_estimate=pl.CostEstimate(flops=flops, bytes_accessed=moved, transcendentals=0),
    )(*ins)


def shaped(*shape, dtype=f32):
    return jax.ShapeDtypeStruct(shape, dtype)


def local(n_sub, n_row, modes, search, precond, in_row, in_col, in_val, bnd_rows, if_row, if_src, if_val):
    nin, kb = in_val.shape[2], in_val.shape[3]
    rows, n = modes.shape
    lb = rows // kb
    ifr = bnd_rows.shape[2]
    groups = nin // lb
    n_z = n_sub // 2
    total_rows = float(rows * n_sub * n_row)
    halo_blocks = n_row * lb + n_sub * ifr
    bnd = bnd_rows[0, 0]
    me_row, me_sub = lax.axis_index("row"), lax.axis_index("sub")
    pos = jnp.stack([me_row, me_sub]).astype(jnp.int32)
    after = lax.optimization_barrier

    def row_send(value, k):
        return lax.ppermute(value, "row", [(r, r ^ k) for r in range(n_row)])

    def sub_send(value, k):
        return lax.ppermute(value, "sub", [(s, s ^ k) for s in range(n_sub)])

    def wire(*shape):
        return shaped(*shape, n, 2 * kb, dtype=bf16)

    def halo_start(own, edge):
        rows_got = [row_send(own, k) for k in range(1, n_row)]
        return rows_got, [sub_send(edge, 2 * k) for k in range(1, n_z)]

    def halo_end(own, edge, rows_got, edges_got):
        same = jnp.concatenate([edge] + edges_got, axis=0)
        return [own] + rows_got + [same, sub_send(same, 1)]

    def halo_of(own, edge):
        return halo_end(own, edge, *halo_start(own, edge))

    def groups_of_four(value, size, send):
        base = 1
        while base < size:
            got = [value] + [send(value, base * m) for m in range(1, min(4, size // base))]
            while len(got) > 1:
                got = [got[i] + got[i + 1] for i in range(0, len(got), 2)]
            value = got[0]
            base *= 4
        return value

    def z_send(value, k):
        return sub_send(value, 2 * k)

    def sum_halves(keep, send):
        total = keep + sub_send(send, 1)
        total = groups_of_four(total, n_z, z_send)
        total = groups_of_four(total, n_row, row_send)
        return [total, sub_send(total, 1)]

    def partials(source, earlier=()):
        m = 2 if earlier else 1
        outs = [shaped(m * lb, n, kb), shaped(m * n_z * ifr, n, kb), wire(m * n_z * ifr)]
        outs += [wire(m * lb)] * (n_row - 1)
        return run(
            functools.partial(partial_kernel, n_row, n_z, m > 1),
            "partials",
            outs,
            [source, joined, where, pos] + list(earlier),
            [VMEM((halo_blocks, n, 2 * kb), f32)],
            smem=(2, 3),
        )

    def sum_with_partials(keep, send, parts, m, meanwhile=()):
        own, edge_keep, edge_send, *row_parts = parts
        total = keep + sub_send(send, 1)
        edge_got = sub_send(edge_send, 1)
        rows_got = [row_send(row_parts[k - 1], k) for k in range(1, n_row)]
        edge_own, *outs = run(
            functools.partial(pair_kernel, n_z, m),
            "pair",
            [shaped(m * ifr, n, kb)] + [wire(m * ifr)] * (n_z - 1),
            [edge_keep, edge_got, pos],
            smem=(2,),
        )
        total, *outs = after((total, *outs))
        edges_got = [z_send(outs[k - 1], k) for k in range(1, n_z)]
        total = groups_of_four(total, n_z, z_send)
        total, rows_got, edges_got, meanwhile = after((total, rows_got, edges_got, list(meanwhile)))
        total = groups_of_four(total, n_row, row_send)
        return [total, sub_send(total, 1)], [own] + rows_got + [edge_own] + edges_got, meanwhile

    x, p = modes.T, search.T
    scaling = precond.reshape(1, rows)
    wire_shapes = [wire(lb), wire(ifr)]
    x_wire, x_edge = run(wire_kernel, "wire", wire_shapes, [x, bnd], smem=(1,))
    x_rows, x_edges = halo_start(x_wire, x_edge)
    in_val, if_val, p, x_edges[0] = after((in_val, if_val, p, x_edges[0]))
    p_wire, p_edge = run(wire_kernel, "wire", wire_shapes, [p, bnd], smem=(1,))
    stored, joined, diagonal, where = run(
        functools.partial(prepare_kernel, groups, n_row * lb),
        "prepare",
        [
            shaped(lb, kb, groups * 2 * kb, dtype=bf16),
            shaped(lb, kb, groups * kb, dtype=bf16),
            shaped(lb, kb, 2 * kb, dtype=bf16),
            shaped(lb * groups, dtype=jnp.int32),
        ],
        [in_val[0, 0], if_val[0, 0], in_row[0, 0], in_col[0, 0], if_row[0, 0], if_src[0, 0]],
        smem=(2, 3, 4, 5),
        smem_outs=(3,),
    )
    stored, *x_edges = after((stored, *x_edges))
    x_halo = halo_end(x_wire, x_edge, x_rows, x_edges)
    x_parts = partials(x_wire)
    p_wire, p_edge, *x_parts = after((p_wire, p_edge, *x_parts))
    p_halo = halo_of(p_wire, p_edge)
    p_parts = partials(p_wire)
    blocks = [stored, diagonal, where, pos]
    halo_scratch = VMEM((halo_blocks, n, 2 * kb), bf16)
    back_scratch = VMEM((lb, n, kb), f32)
    whole = shaped(n, rows)

    count = len(x_halo)
    half_x, diag_x, table = run(
        functools.partial(x_image_kernel, n_row, n_z),
        "x_image",
        [whole, whole, shaped(2 * n, 2 * n)],
        x_halo + blocks + [x, p],
        [halo_scratch],
        smem=(count + 2, count + 3),
    )
    table_shape = shaped(3 * n, 2 * n)
    halves_shape = [shaped(3 * n // 2, 2 * n)] * 2
    table_scratch = VMEM((3 * n, 2 * n), f32)
    half_p, diag_p, keep, send = run(
        functools.partial(p_image_kernel, n_row, n_z),
        "p_image",
        [whole, whole] + halves_shape,
        p_halo + blocks + [x, half_x, p, table],
        [halo_scratch, table_scratch],
        smem=(count + 2, count + 3),
    )
    keep, send, x_parts, p_parts = after((keep, send, x_parts, p_parts))
    halves, x_back, _ = sum_with_partials(keep, send, x_parts, 1)
    count = len(x_back)
    table, ax, energy, w, w_wire, w_edge = run(
        functools.partial(update_kernel, n_row, n_z),
        "update",
        [table_shape, whole, shaped(n, n), whole] + wire_shapes,
        x_back + halves + [pos, bnd, x, half_x, diag_x, scaling],
        [back_scratch],
        smem=(count + 2, count + 3),
    )
    w_halo = halo_of(w_wire, w_edge)
    (pap_inverse,) = run(inverse_kernel, "pap_inverse", [shaped(n, n)], [table])
    w_parts = partials(w_wire, p_parts)

    def update_image(first, halo, w, x, p, ax, ap):
        count = len(halo)
        return run(
            functools.partial(update_image_kernel, n_row, n_z, first),
            "update_image",
            [whole, whole] + halves_shape,
            halo + blocks + [w, x, p, ax, ap],
            [halo_scratch, table_scratch],
            smem=(count + 2, count + 3),
        )

    half_w, diag_w, keep, send = update_image(True, w_halo, w, x, p, ax, half_p)
    keep, send, w_parts = after((keep, send, w_parts))
    halves, w_back, (pap_inverse,) = sum_with_partials(keep, send, w_parts, 2, [pap_inverse])
    count = len(w_back)
    x, ax, w, w_wire, w_edge, step_x, step_a, small = run(
        functools.partial(move_kernel, n_row, n_z, total_rows),
        "move",
        [whole] * 3 + wire_shapes + [whole, whole, shaped(4 * n, n)],
        w_back + halves + [pos, bnd, table, energy, pap_inverse, x, p, ax, half_p, diag_p, w, half_w, diag_w, scaling],
        [table_scratch, back_scratch],
        smem=(count + 2, count + 3),
    )
    w_halo = halo_of(w_wire, w_edge)
    p, ap, state = run(settle_kernel, "settle", [whole, whole, shaped(3 * n, n)], [small, step_x, step_a])
    _, _, keep, send = update_image(False, w_halo, w, x, p, ax, ap)
    halves = sum_halves(keep, send)
    x, p = run(
        functools.partial(finish_kernel, total_rows),
        "finish",
        [whole, whole],
        halves + [pos, state, x, p, w],
        [table_scratch],
        smem=(2,),
    )
    return (x.T, p.T)


def solution(mesh):
    return jax.shard_map(
        functools.partial(local, mesh.shape["sub"], mesh.shape["row"]),
        mesh=mesh,
        in_specs=(
            P(("sub", "row"), None),
            P(("sub", "row"), None),
            P(("sub", "row")),
            P("sub", "row", None),
            P("sub", "row", None),
            P("sub", "row", None, None, None),
            P("sub", "row", None),
            P("sub", "row", None),
            P("sub", "row", None),
            P("sub", "row", None, None, None),
        ),
        out_specs=(P(("sub", "row"), None), P(("sub", "row"), None)),
        check_vma=False,
    )
```

```python
import functools

import jax
import jax.numpy as jnp
from jax import lax
from jax.experimental import pallas as pl
from jax.experimental.pallas import tpu as pltpu
from jax.sharding import PartitionSpec as P

f32 = jnp.float32
bf16 = jnp.bfloat16
precise_mode = lax.Precision.HIGHEST
VMEM = pltpu.VMEM
SMEM = pltpu.SMEM


def nn(a, b):
    return lax.dot_general(a, b, (((1,), (0,)), ((), ())), precision=precise_mode, preferred_element_type=f32)


def nt(a, b):
    return lax.dot_general(a, b, (((1,), (1,)), ((), ())), precision=precise_mode, preferred_element_type=f32)


TOP = 32000.0
LOG_STEP = 0.08664339756999316


def low_half(shape):
    return lax.broadcasted_iota(jnp.int32, shape, 1) < shape[1] // 2


def swap(tile):
    return pltpu.roll(tile, tile.shape[1] // 2, 1)


def two_blocks(tile):
    low = low_half(tile.shape)
    high = tile.astype(bf16).astype(f32)
    rest = tile - high
    one = jnp.where(low, high, swap(rest))
    two = jnp.where(low, swap(high), rest)
    return one.astype(bf16), two.astype(bf16)


def code(tiles):
    most = jnp.abs(tiles[0])
    for tile in tiles[1:]:
        most = jnp.maximum(most, jnp.abs(tile))
    most = jnp.maximum(jnp.max(most, axis=1, keepdims=True), 1e-30)
    power = jnp.broadcast_to(jnp.ceil(jnp.log(most) * (1.0 / LOG_STEP)), tiles[0].shape)
    factor = TOP * jnp.exp(power * -LOG_STEP)
    return [jnp.floor(tile * factor + 0.5).astype(jnp.int32) for tile in tiles], power.astype(jnp.int32)


def step_of(power):
    return jnp.exp(power.astype(jnp.int32).astype(f32) * LOG_STEP) * (1.0 / TOP)


def decode(tile, step):
    return tile.astype(jnp.int32).astype(f32) * step


def edge_tiles(ifr):
    return ifr // 2 + 1


def code_edge(tiles, ifr):
    low = low_half(tiles[0].shape)
    tiles = list(tiles)
    tiles[-1] = jnp.where(low, tiles[-1], 0.0) if ifr % 2 else jnp.zeros_like(tiles[-1])
    coded, power = code(tiles)
    coded[-1] = jnp.where(low, coded[-1], power) if ifr % 2 else power
    return [tile.astype(jnp.int16) for tile in coded]


def decode_edge(ref, start, ifr):
    tiles = [ref[start + t].astype(jnp.int32) for t in range(edge_tiles(ifr))]
    low = low_half(tiles[-1].shape)
    power = jnp.where(low, swap(tiles[-1]), tiles[-1]) if ifr % 2 else tiles[-1]
    step = step_of(power)
    return [tile.astype(f32) * step for tile in tiles]


def write_wire(vector, bnd, wire, edge, place=0):
    ifr = bnd.shape[0]
    width = wire.shape[2]
    count = vector.shape[1] // width
    base = place * (count + 1)
    coded, power = code([vector[:, t * width : (t + 1) * width] for t in range(count)])
    for t in range(count):
        wire[base + t] = coded[t].astype(jnp.int16)
    wire[base + count] = power.astype(jnp.int16)
    low = low_half(power.shape)
    slots = []
    for q in range(ifr):
        tile = wire[base + bnd[q] // 2].astype(jnp.int32)
        side = jnp.broadcast_to(bnd[q] % 2, tile.shape)
        slots.append(jnp.where(side == q % 2, tile, swap(tile)))
    slots.append(power)
    if len(slots) % 2:
        slots.append(power)
    for t in range(edge_tiles(ifr)):
        edge[place * edge_tiles(ifr) + t] = jnp.where(low, slots[2 * t], slots[2 * t + 1]).astype(jnp.int16)


def fill_halo(vector, wires, edges, pos, halo, ifr, place=0, places=1):
    width = halo.shape[2]
    count = vector.shape[1] // width
    lb = 2 * count
    n_row = len(wires) + 1
    for t in range(count):
        one, two = two_blocks(vector[:, t * width : (t + 1) * width])
        halo[pos[0] * lb + 2 * t] = one
        halo[pos[0] * lb + 2 * t + 1] = two
    for k, wire in enumerate(wires):
        start = (pos[0] ^ (k + 1)) * lb
        base = place * (count + 1)
        step = step_of(wire[base + count])
        for t in range(count):
            one, two = two_blocks(decode(wire[base + t], step))
            halo[start + 2 * t] = one
            halo[start + 2 * t + 1] = two
    tiles = edge_tiles(ifr)
    for other, edge in enumerate(edges):
        for k in range(edge.shape[0] // (places * tiles)):
            start = n_row * lb + (((pos[1] // 2) ^ k) * 2 + ((pos[1] % 2) ^ other)) * ifr
            found = decode_edge(edge, (k * places + place) * tiles, ifr)
            for q in range(0, ifr, 2):
                blocks = two_blocks(found[q // 2])
                halo[start + q] = blocks[0]
                if q + 1 < ifr:
                    halo[start + q + 1] = blocks[1]


def write_halves(table, pos, keep, send):
    height = keep.shape[0]
    core = pos[1] % 2
    keep[...] = table[pl.ds(pl.multiple_of(core * height, 8), height), :]
    send[...] = table[pl.ds(pl.multiple_of((1 - core) * height, 8), height), :]


def read_halves(mine, other, pos, table):
    height = mine.shape[0]
    core = pos[1] % 2
    table[pl.ds(pl.multiple_of(core * height, 8), height), :] = mine[...]
    table[pl.ds(pl.multiple_of((1 - core) * height, 8), height), :] = other[...]


def forward(halo, pos, stored, diagonal, where, out, diag_out):
    lb, kb = stored.shape[0], stored.shape[1]
    own = pos[0] * lb
    groups = stored.shape[2] // (2 * kb)
    for i in range(0, lb, 2):
        sums, diags = [], []
        for m in (i, i + 1):
            row = jnp.concatenate([halo[where[m * groups + g]] for g in range(groups)], axis=1)
            sums.append(lax.dot_general(row, stored[m], (((1,), (1,)), ((), ())), preferred_element_type=f32))
            diags.append(lax.dot_general(halo[own + m], diagonal[m], (((1,), (1,)), ((), ())), preferred_element_type=f32))
        out[:, i * kb : (i + 2) * kb] = jnp.concatenate(sums, axis=1)
        diag_out[:, i * kb : (i + 2) * kb] = jnp.concatenate(diags, axis=1)


def returned(index, own, rows, edge_own, edges, bnd, back, target):
    count, _, width = back.shape
    ifr = bnd.shape[0]
    tiles = edge_tiles(ifr)
    n = target.shape[0]
    steps = [step_of(row[index * (count + 1) + count]) for row in rows]
    for t in range(count):
        total = own[index * n : (index + 1) * n, t * width : (t + 1) * width]
        for row, step in zip(rows, steps):
            total = total + decode(row[index * (count + 1) + t], step)
        back[t] = total
    found = [edge_own[index * tiles + t] for t in range(tiles)]
    for edge in edges:
        found = [a + b for a, b in zip(found, decode_edge(edge, index * tiles, ifr))]
    low = low_half(back.shape[1:])
    for q in range(ifr):
        side = jnp.broadcast_to(bnd[q] % 2, low.shape)
        block = jnp.where(side == q % 2, found[q // 2], swap(found[q // 2]))
        spot = bnd[q] // 2
        back[spot] = back[spot] + jnp.where(low == (side == 0), block, 0.0)
    for t in range(count):
        span = slice(t * width, (t + 1) * width)
        target[:, span] = target[:, span] + back[t]


def eliminate(table, full):
    order = table.shape[0]
    rows = lax.broadcasted_iota(jnp.int32, table.shape, 0)
    for j in range(0, order, 2):
        left = jnp.broadcast_to(table[:, j : j + 1], table.shape)
        right = jnp.broadcast_to(table[:, j + 1 : j + 2], table.shape)
        one, two = table[j : j + 1, :], table[j + 1 : j + 2, :]
        over = 1.0 / left[j : j + 1, :]
        ratio = left[j + 1 : j + 2, :] * over
        beside = right[j : j + 1, :]
        two = two - ratio * one
        second = two * (1.0 / (right[j + 1 : j + 2, :] - ratio * beside))
        first = (one - beside * second) * over
        moved = table - left * first - right * second
        if full:
            table = jnp.where(rows == j, first, jnp.where(rows == j + 1, second, moved))
        else:
            table = jnp.where(rows > j + 1, moved, jnp.where(rows == j + 1, two, table))
    return table


def unit(order):
    return (
        lax.broadcasted_iota(jnp.int32, (order, order), 0) == lax.broadcasted_iota(jnp.int32, (order, order), 1)
    ).astype(f32)


def inverse(matrix):
    order = matrix.shape[0]
    return eliminate(jnp.concatenate([matrix, unit(order)], axis=1), True)[:, order:]


def cholesky_inverse(matrix):
    order = matrix.shape[0]
    done = eliminate(jnp.concatenate([matrix, unit(order)], axis=1), False)
    pivots = jnp.sum(done[:, :order] * unit(order), axis=1, keepdims=True)
    return done[:, order:] * (1.0 / jnp.sqrt(pivots))


def coefficients(table, gram, xp, pp, pax, pap_inverse, total_rows):
    n = gram.shape[0]
    waw, wap = table[0:n, :n], table[0:n, n:]
    wax, wx = table[n : 2 * n, :n], table[n : 2 * n, n:]
    wp, ww = table[2 * n : 3 * n, :n], table[2 * n : 3 * n, n:]
    waw = waw + waw.T
    first = nn(pap_inverse, wap.T)
    if pax is None:
        rhs = -wax
    else:
        second = nn(pap_inverse, pax)
        rhs = nn(wap, second) - wax
    schur = waw - nn(wap, first)
    zw = eliminate(jnp.concatenate([schur, rhs], axis=1), True)[:, n:]
    zp = -nn(first, zw)
    if pax is not None:
        zp = zp - second
    cross = nn(wx.T, zw) + nn(xp, zp)
    zwt, zpt = zw.T, zp.T
    inner = nn(zwt, nn(ww, zw) + nn(wp, zp)) + nn(zpt, nn(wp.T, zw) + nn(pp, zp))
    lengths = (gram + cross + cross.T + inner) / total_rows
    return zw, zp, zwt, zpt, cross, inner, wax, cholesky_inverse(lengths)


def prepare_kernel(groups, base, vals, faces, rows, cols, face_rows, face_src, stored, joined, diagonal, where):
    lb, kb = faces.shape[0], faces.shape[1]

    def twice(block):
        wide = block.astype(f32)
        return jnp.concatenate([wide, wide], axis=1).astype(bf16)

    for k in range(lb):
        diagonal[k] = twice(vals[k])
    for g in range(groups):
        half = (g % 2) * kb
        for m in range(lb):
            if g < groups - 1:
                k = (g + 1) * lb + m
                i, target, block = rows[k], cols[k], twice(vals[k])
            else:
                i, target, block = face_rows[m], base + face_src[m], twice(faces[m])
            stored[i, :, 2 * kb * g : 2 * kb * (g + 1)] = block
            joined[i, :, kb * g : kb * (g + 1)] = block[:, half : half + kb]
            where[i * groups + g] = target


def wire_kernel(x, p, bnd, wire, edge):
    write_wire(x, bnd, wire, edge, 0)
    write_wire(p, bnd, wire, edge, 1)


def partial_kernel(n_row, n_z, merge, ifr, vector, joined, where, pos, *refs):
    refs = list(refs)
    parts = n_row + 2
    earlier = [refs.pop(0) for _ in range(parts)] if merge else []
    outs, acc = refs[:-1], refs[-1]
    own, core_keep, core_send, *row_outs = outs
    width = acc.shape[2]
    count = vector.shape[1] // width
    lb, kb, n = 2 * count, joined.shape[1], vector.shape[0]
    tiles = edge_tiles(ifr)
    groups = joined.shape[2] // kb
    low = low_half(acc.shape[1:])
    core = pos[1] % 2
    for source, target in zip(earlier, outs):
        target[pl.ds(0, source.shape[0])] = source[...]
    own_base = n if merge else 0
    row_base = count + 1 if merge else 0
    edge_base = n_z * tiles if merge else 0
    acc[...] = jnp.zeros(acc.shape, f32)
    for pair in range(count):
        both = two_blocks(vector[:, pair * width : (pair + 1) * width])
        for m in range(2):
            i = 2 * pair + m
            blocks = jnp.concatenate([joined[i], joined[i]], axis=0)
            out = jnp.dot(both[m], blocks, preferred_element_type=f32)
            for t in range(groups // 2):
                tile = out[:, width * t : width * (t + 1)]
                one = where[i * groups + 2 * t]
                two = where[i * groups + 2 * t + 1]
                acc[one] = acc[one] + jnp.where(low, tile, 0.0)
                acc[two] = acc[two] + jnp.where(low, 0.0, tile)

    def folded(one, two):
        return jnp.where(low, one, two) + swap(jnp.where(low, two, one))

    for k in range(n_row):
        start = (pos[0] ^ k) * lb
        found = [folded(acc[start + 2 * t], acc[start + 2 * t + 1]) for t in range(count)]
        if k == 0:
            for t in range(count):
                own[own_base : own_base + n, t * width : (t + 1) * width] = found[t]
        else:
            coded, power = code(found)
            for t in range(count):
                row_outs[k - 1][row_base + t] = coded[t].astype(jnp.int16)
            row_outs[k - 1][row_base + count] = power.astype(jnp.int16)
    for z in range(n_z):
        spot = edge_base + z * tiles
        for side in range(2):
            start = n_row * lb + (z * 2 + (core if side == 0 else 1 - core)) * ifr
            found = []
            for t in range(tiles):
                one = acc[start + 2 * t] if 2 * t < ifr else jnp.zeros(acc.shape[1:], f32)
                two = acc[start + 2 * t + 1] if 2 * t + 1 < ifr else jnp.zeros(acc.shape[1:], f32)
                found.append(folded(one, two))
            if side == 0:
                for t in range(tiles):
                    core_keep[spot + t] = found[t]
            else:
                for t, tile in enumerate(code_edge(found, ifr)):
                    core_send[spot + t] = tile


def pair_kernel(n_z, count, ifr, keep, got, pos, own, *outs):
    tiles = edge_tiles(ifr)
    for k in range(n_z):
        z = (pos[1] // 2) ^ k
        for v in range(count):
            spot = (v * n_z + z) * tiles
            there = decode_edge(got, spot, ifr)
            total = [keep[spot + t] + there[t] for t in range(tiles)]
            if k > 0:
                total = code_edge(total, ifr)
            target = own if k == 0 else outs[k - 1]
            for t in range(tiles):
                target[v * tiles + t] = total[t]


def split_halo(refs, n_row):
    wires = [refs.pop(0) for _ in range(n_row - 1)]
    return wires, [refs.pop(0), refs.pop(0)]


def start_image_kernel(n_row, ifr, *refs):
    refs = list(refs)
    wires, edges = split_halo(refs, n_row)
    stored, diagonal, where, pos, x, p, half_x, diag_x, half_p, diag_p, keep, send, halo_x, halo_p, table = refs
    n = x.shape[0]
    for place, (vector, half, diag, halo) in enumerate(((x, half_x, diag_x, halo_x), (p, half_p, diag_p, halo_p))):
        fill_halo(vector, wires, edges, pos, halo, ifr, place, 2)
        forward(halo, pos, stored, diagonal, where, half, diag)
        half[...] = half[...] + 0.5 * diag[...]
    table[0:n, :] = nt(x[...], jnp.concatenate([half_x[...], x[...]], axis=0))
    table[n : 2 * n, :] = nt(p[...], jnp.concatenate([x[...], p[...]], axis=0))
    table[2 * n : 3 * n, :] = nt(p[...], jnp.concatenate([half_p[...], half_x[...]], axis=0))
    table[2 * n : 3 * n, n:] = table[2 * n : 3 * n, n:] + nt(half_p[...], x[...])
    write_halves(table, pos, keep, send)


def take_returned(refs, n_row, n_z):
    own = refs.pop(0)
    rows = [refs.pop(0) for _ in range(n_row - 1)]
    edge_own = refs.pop(0)
    return own, rows, edge_own, [refs.pop(0) for _ in range(n_z - 1)]


def update_kernel(n_row, n_z, *refs):
    refs = list(refs)
    back_parts = take_returned(refs, n_row, n_z)
    mine, other, pos, bnd, x, half, diag, precond, table, ax, energy, w, wire, edge, back = refs
    n = x.shape[0]
    read_halves(mine, other, pos, table)
    ax[...] = half[...] + 0.5 * diag[...]
    returned(0, *back_parts, bnd, back, ax)
    stored, gram = table[0:n, 0:n], table[0:n, n:]
    total = stored + stored.T
    energy[...] = total
    ritz = nn(total, inverse(0.5 * (gram + gram.T)))
    w[...] = precond[...] * (ax[...] - nn(ritz, x[...]))
    write_wire(w, bnd, wire, edge)


def inverse_kernel(table, solved):
    n = solved.shape[0]
    stored = table[2 * n : 3 * n, 0:n]
    solved[...] = inverse(stored + stored.T)


def update_image_kernel(n_row, ifr, first, *refs):
    refs = list(refs)
    wires, edges = split_halo(refs, n_row)
    stored, diagonal, where, pos, w, x, p, ax, ap, half, diag, keep, send, halo, table = refs
    n = w.shape[0]
    fill_halo(w, wires, edges, pos, halo, ifr)
    forward(halo, pos, stored, diagonal, where, half, diag)
    half[...] = half[...] + 0.5 * diag[...]
    here = w[...]
    table[0:n, :] = nt(here, jnp.concatenate([half[...], ap[...]], axis=0))
    table[n : 2 * n, :] = nt(here, jnp.concatenate([ax[...], x[...]], axis=0))
    table[2 * n : 3 * n, :] = nt(here, jnp.concatenate([p[...], here], axis=0))
    if first:
        table[0:n, n:] = table[0:n, n:] + nt(half[...], p[...])
    write_halves(table, pos, keep, send)


def move_kernel(n_row, n_z, total_rows, *refs):
    refs = list(refs)
    back_parts = take_returned(refs, n_row, n_z)
    mine, other, pos, bnd, start, energy, pap_inverse, x, p, ax, ap, ap_diag, w, aw, aw_diag, precond = refs[:16]
    x_out, ax_out, w_out, wire, edge, step_x, step_a, small, table, back, ap_full, aw_full = refs[16:]
    n = x.shape[0]
    read_halves(mine, other, pos, table)
    gram = start[0:n, n:]
    px, pp = start[n : 2 * n, 0:n], start[n : 2 * n, n:]
    pax = start[2 * n : 3 * n, n:]
    zw, zp, zwt, zpt, cross, inner, wax, scale = coefficients(
        table, 0.5 * (gram + gram.T), px.T, pp, pax, pap_inverse[...], total_rows
    )
    ap_full[...] = ap[...] + 0.5 * ap_diag[...]
    returned(0, *back_parts, bnd, back, ap_full)
    aw_full[...] = aw[...] + 0.5 * aw_diag[...]
    returned(1, *back_parts, bnd, back, aw_full)
    step_a[...] = nn(zpt, ap_full[...]) + nn(zwt, aw_full[...])
    step_x[...] = nn(zwt, w[...]) + nn(zpt, p[...])
    x_out[...] = nn(scale, x[...] + step_x[...])
    ax_out[...] = nn(scale, ax[...] + step_a[...])
    gain = nn(wax.T, zw) + nn(pax.T, zp)
    gain = 0.5 * (gain + gain.T)
    ritz = nn(scale, nn(energy[...] + gain, scale.T)) / total_rows
    w_out[...] = precond[...] * (ax_out[...] - nn(ritz, x_out[...]))
    write_wire(w_out, bnd, wire, edge)
    small[0:n, :] = -gain
    small[n : 2 * n, :] = cross + inner
    small[2 * n : 3 * n, :] = inner
    small[3 * n : 4 * n, :] = scale


def settle_kernel(small, step_x, step_a, p_out, ap_out, state):
    n = small.shape[1]
    scale = small[3 * n : 4 * n, :]
    scale_t = scale.T
    p_out[...] = nn(scale, step_x[...])
    ap_out[...] = nn(scale, step_a[...])
    state[0:n, :] = inverse(nn(scale, nn(small[0:n, :], scale_t)))
    state[n : 2 * n, :] = nn(scale, nn(small[n : 2 * n, :], scale_t))
    state[2 * n : 3 * n, :] = nn(scale, nn(small[2 * n : 3 * n, :], scale_t))


def finish_kernel(total_rows, mine, other, pos, state, x, p, w, x_out, p_out, table):
    n = x.shape[0]
    read_halves(mine, other, pos, table)
    zw, zp, zwt, zpt, _, _, _, scale = coefficients(
        table,
        unit(n) * total_rows,
        state[n : 2 * n, :],
        state[2 * n : 3 * n, :],
        None,
        state[0:n, :],
        total_rows,
    )
    step = nn(zwt, w[...]) + nn(zpt, p[...])
    x_out[...] = nn(scale, x[...] + step)
    p_out[...] = nn(scale, step)


def run(kernel, name, outs, ins, scratch=(), smem=(), smem_outs=(), flops=1000000):
    in_specs = [pl.BlockSpec(memory_space=SMEM if i in smem else VMEM) for i in range(len(ins))]
    out_specs = [pl.BlockSpec(memory_space=SMEM if i in smem_outs else VMEM) for i in range(len(outs))]
    moved = sum(a.size * a.dtype.itemsize for a in ins) + sum(o.size * o.dtype.itemsize for o in outs)
    return pl.pallas_call(
        kernel,
        name=name,
        out_shape=outs,
        in_specs=in_specs,
        out_specs=out_specs,
        scratch_shapes=list(scratch),
        compiler_params=pltpu.CompilerParams(vmem_limit_bytes=48 * 1024 * 1024),
        cost_estimate=pl.CostEstimate(flops=flops, bytes_accessed=moved, transcendentals=0),
    )(*ins)


def shaped(*shape, dtype=f32):
    return jax.ShapeDtypeStruct(shape, dtype)


def local(n_sub, n_row, modes, search, precond, in_row, in_col, in_val, bnd_rows, if_row, if_src, if_val):
    nin, kb = in_val.shape[2], in_val.shape[3]
    rows, n = modes.shape
    lb = rows // kb
    ifr = bnd_rows.shape[2]
    groups = nin // lb
    n_z = n_sub // 2
    total_rows = float(rows * n_sub * n_row)
    halo_blocks = n_row * lb + n_sub * ifr
    bnd = bnd_rows[0, 0]
    me_row, me_sub = lax.axis_index("row"), lax.axis_index("sub")
    pos = jnp.stack([me_row, me_sub]).astype(jnp.int32)
    after = lax.optimization_barrier

    def row_send(value, k):
        return lax.ppermute(value, "row", [(r, r ^ k) for r in range(n_row)])

    def sub_send(value, k):
        return lax.ppermute(value, "sub", [(s, s ^ k) for s in range(n_sub)])

    tiles = lb // 2
    edges_in = edge_tiles(ifr)

    def coded(count):
        return shaped(count, n, 2 * kb, dtype=jnp.int16)

    def halo_start(own, edge):
        rows_got = [row_send(own, k) for k in range(1, n_row)]
        return rows_got, [sub_send(edge, 2 * k) for k in range(1, n_z)]

    def halo_end(edge, rows_got, edges_got):
        same = jnp.concatenate([edge] + edges_got, axis=0)
        return rows_got + [same, sub_send(same, 1)]

    def halo_of(own, edge):
        return halo_end(edge, *halo_start(own, edge))

    def groups_of_four(value, size, send):
        base = 1
        while base < size:
            got = [value] + [send(value, base * m) for m in range(1, min(4, size // base))]
            while len(got) > 1:
                got = [got[i] + got[i + 1] for i in range(0, len(got), 2)]
            value = got[0]
            base *= 4
        return value

    def z_send(value, k):
        return sub_send(value, 2 * k)

    def sum_halves(keep, send):
        total = keep + sub_send(send, 1)
        total = groups_of_four(total, n_z, z_send)
        total = groups_of_four(total, n_row, row_send)
        return [total, sub_send(total, 1)]

    def partials(source, earlier=()):
        m = 2 if earlier else 1
        outs = [shaped(m * n, rows), shaped(m * n_z * edges_in, n, 2 * kb), coded(m * n_z * edges_in)]
        outs += [coded(m * (tiles + 1))] * (n_row - 1)
        return run(
            functools.partial(partial_kernel, n_row, n_z, m > 1, ifr),
            "partials",
            outs,
            [source, joined, where, pos] + list(earlier),
            [VMEM((halo_blocks, n, 2 * kb), f32)],
            smem=(2, 3),
        )

    def sum_with_partials(keep, send, parts, m, meanwhile=()):
        own, edge_keep, edge_send, *row_parts = parts
        total = keep + sub_send(send, 1)
        edge_got = sub_send(edge_send, 1)
        rows_got = [row_send(row_parts[k - 1], k) for k in range(1, n_row)]
        edge_own, *outs = run(
            functools.partial(pair_kernel, n_z, m, ifr),
            "pair",
            [shaped(m * edges_in, n, 2 * kb)] + [coded(m * edges_in)] * (n_z - 1),
            [edge_keep, edge_got, pos],
            smem=(2,),
        )
        total, *outs = after((total, *outs))
        edges_got = [z_send(outs[k - 1], k) for k in range(1, n_z)]
        total = groups_of_four(total, n_z, z_send)
        total, rows_got, edges_got, meanwhile = after((total, rows_got, edges_got, list(meanwhile)))
        total = groups_of_four(total, n_row, row_send)
        return [total, sub_send(total, 1)], [own] + rows_got + [edge_own] + edges_got, meanwhile

    x, p = modes.T, search.T
    scaling = precond.reshape(1, rows)
    wire_shapes = [coded(tiles + 1), coded(edges_in)]
    wire, edge = run(wire_kernel, "wire", [coded(2 * (tiles + 1)), coded(2 * edges_in)], [x, p, bnd], smem=(2,))
    rows_got, edges_got = halo_start(wire, edge)
    in_val, if_val, edges_got[0] = after((in_val, if_val, edges_got[0]))
    stored, joined, diagonal, where = run(
        functools.partial(prepare_kernel, groups, n_row * lb),
        "prepare",
        [
            shaped(lb, kb, groups * 2 * kb, dtype=bf16),
            shaped(lb, kb, groups * kb, dtype=bf16),
            shaped(lb, kb, 2 * kb, dtype=bf16),
            shaped(lb * groups, dtype=jnp.int32),
        ],
        [in_val[0, 0], if_val[0, 0], in_row[0, 0], in_col[0, 0], if_row[0, 0], if_src[0, 0]],
        smem=(2, 3, 4, 5),
        smem_outs=(3,),
    )
    stored, *edges_got = after((stored, *edges_got))
    halo = halo_end(edge, rows_got, edges_got)
    x_parts = partials(x)
    p_parts = partials(p)
    blocks = [stored, diagonal, where, pos]
    halo_scratch = VMEM((halo_blocks, n, 2 * kb), bf16)
    back_scratch = VMEM((tiles, n, 2 * kb), f32)
    whole = shaped(n, rows)

    table_shape = shaped(3 * n, 2 * n)
    halves_shape = [shaped(3 * n // 2, 2 * n)] * 2
    table_scratch = VMEM((3 * n, 2 * n), f32)
    count = len(halo)
    half_x, diag_x, half_p, diag_p, keep, send = run(
        functools.partial(start_image_kernel, n_row, ifr),
        "start_image",
        [whole] * 4 + halves_shape,
        halo + blocks + [x, p],
        [halo_scratch, halo_scratch, table_scratch],
        smem=(count + 2, count + 3),
    )
    keep, send, x_parts, p_parts = after((keep, send, x_parts, p_parts))
    halves, x_back, _ = sum_with_partials(keep, send, x_parts, 1)
    count = len(x_back)
    table, ax, energy, w, w_wire, w_edge = run(
        functools.partial(update_kernel, n_row, n_z),
        "update",
        [table_shape, whole, shaped(n, n), whole] + wire_shapes,
        x_back + halves + [pos, bnd, x, half_x, diag_x, scaling],
        [back_scratch],
        smem=(count + 2, count + 3),
    )
    w_halo = halo_of(w_wire, w_edge)
    (pap_inverse,) = run(inverse_kernel, "pap_inverse", [shaped(n, n)], [table])
    w_parts = partials(w, p_parts)

    def update_image(first, halo, w, x, p, ax, ap):
        count = len(halo)
        return run(
            functools.partial(update_image_kernel, n_row, ifr, first),
            "update_image",
            [whole, whole] + halves_shape,
            halo + blocks + [w, x, p, ax, ap],
            [halo_scratch, table_scratch],
            smem=(count + 2, count + 3),
        )

    half_w, diag_w, keep, send = update_image(True, w_halo, w, x, p, ax, half_p)
    keep, send, w_parts = after((keep, send, w_parts))
    halves, w_back, (pap_inverse,) = sum_with_partials(keep, send, w_parts, 2, [pap_inverse])
    count = len(w_back)
    x, ax, w, w_wire, w_edge, step_x, step_a, small = run(
        functools.partial(move_kernel, n_row, n_z, total_rows),
        "move",
        [whole] * 3 + wire_shapes + [whole, whole, shaped(4 * n, n)],
        w_back + halves + [pos, bnd, table, energy, pap_inverse, x, p, ax, half_p, diag_p, w, half_w, diag_w, scaling],
        [table_scratch, back_scratch, VMEM((n, rows), f32), VMEM((n, rows), f32)],
        smem=(count + 2, count + 3),
    )
    w_halo = halo_of(w_wire, w_edge)
    p, ap, state = run(settle_kernel, "settle", [whole, whole, shaped(3 * n, n)], [small, step_x, step_a])
    _, _, keep, send = update_image(False, w_halo, w, x, p, ax, ap)
    halves = sum_halves(keep, send)
    x, p = run(
        functools.partial(finish_kernel, total_rows),
        "finish",
        [whole, whole],
        halves + [pos, state, x, p, w],
        [table_scratch],
        smem=(2,),
    )
    return (x.T, p.T)


def solution(mesh):
    return jax.shard_map(
        functools.partial(local, mesh.shape["sub"], mesh.shape["row"]),
        mesh=mesh,
        in_specs=(
            P(("sub", "row"), None),
            P(("sub", "row"), None),
            P(("sub", "row")),
            P("sub", "row", None),
            P("sub", "row", None),
            P("sub", "row", None, None, None),
            P("sub", "row", None),
            P("sub", "row", None),
            P("sub", "row", None),
            P("sub", "row", None, None, None),
        ),
        out_specs=(P(("sub", "row"), None), P(("sub", "row"), None)),
        check_vma=False,
    )
```

```python
import functools

import jax
import jax.numpy as jnp
from jax import lax
from jax.experimental import pallas as pl
from jax.experimental.pallas import tpu as pltpu
from jax.sharding import PartitionSpec as P

f32 = jnp.float32
bf16 = jnp.bfloat16
precise_mode = lax.Precision.HIGHEST
VMEM = pltpu.VMEM
SMEM = pltpu.SMEM


def nn(a, b):
    return lax.dot_general(a, b, (((1,), (0,)), ((), ())), precision=precise_mode, preferred_element_type=f32)


def nt(a, b):
    return lax.dot_general(a, b, (((1,), (1,)), ((), ())), precision=precise_mode, preferred_element_type=f32)


TOP = 32000.0
LOG_STEP = 0.08664339756999316


def low_half(shape):
    return lax.broadcasted_iota(jnp.int32, shape, 1) < shape[1] // 2


def swap(tile):
    return pltpu.roll(tile, tile.shape[1] // 2, 1)


def two_blocks(tile):
    low = low_half(tile.shape)
    high = tile.astype(bf16).astype(f32)
    rest = tile - high
    one = jnp.where(low, high, swap(rest))
    two = jnp.where(low, swap(high), rest)
    return one.astype(bf16), two.astype(bf16)


def code(tiles):
    most = jnp.abs(tiles[0])
    for tile in tiles[1:]:
        most = jnp.maximum(most, jnp.abs(tile))
    most = jnp.maximum(jnp.max(most, axis=1, keepdims=True), 1e-30)
    power = jnp.broadcast_to(jnp.ceil(jnp.log(most) * (1.0 / LOG_STEP)), tiles[0].shape)
    factor = TOP * jnp.exp(power * -LOG_STEP)
    return [jnp.floor(tile * factor + 0.5).astype(jnp.int32) for tile in tiles], power.astype(jnp.int32)


def step_of(power):
    return jnp.exp(power.astype(jnp.int32).astype(f32) * LOG_STEP) * (1.0 / TOP)


def decode(tile, step):
    return tile.astype(jnp.int32).astype(f32) * step


def edge_tiles(ifr):
    return ifr // 2 + 1


def code_edge(tiles, ifr):
    low = low_half(tiles[0].shape)
    tiles = list(tiles)
    tiles[-1] = jnp.where(low, tiles[-1], 0.0) if ifr % 2 else jnp.zeros_like(tiles[-1])
    coded, power = code(tiles)
    coded[-1] = jnp.where(low, coded[-1], power) if ifr % 2 else power
    return [tile.astype(jnp.int16) for tile in coded]


def decode_edge(ref, start, ifr):
    tiles = [ref[start + t].astype(jnp.int32) for t in range(edge_tiles(ifr))]
    low = low_half(tiles[-1].shape)
    power = jnp.where(low, swap(tiles[-1]), tiles[-1]) if ifr % 2 else tiles[-1]
    step = step_of(power)
    return [tile.astype(f32) * step for tile in tiles]


def write_wire(vector, bnd, wire, edge, place=0):
    ifr = bnd.shape[0]
    width = wire.shape[2]
    count = vector.shape[1] // width
    base = place * (count + 1)
    coded, power = code([vector[:, t * width : (t + 1) * width] for t in range(count)])
    for t in range(count):
        wire[base + t] = coded[t].astype(jnp.int16)
    wire[base + count] = power.astype(jnp.int16)
    low = low_half(power.shape)
    slots = []
    for q in range(ifr):
        tile = wire[base + bnd[q] // 2].astype(jnp.int32)
        side = jnp.broadcast_to(bnd[q] % 2, tile.shape)
        slots.append(jnp.where(side == q % 2, tile, swap(tile)))
    slots.append(power)
    if len(slots) % 2:
        slots.append(power)
    for t in range(edge_tiles(ifr)):
        edge[place * edge_tiles(ifr) + t] = jnp.where(low, slots[2 * t], slots[2 * t + 1]).astype(jnp.int16)


def fill_halo(vector, wires, edges, pos, halo, ifr, place=0, places=1):
    width = halo.shape[2]
    count = vector.shape[1] // width
    lb = 2 * count
    n_row = len(wires) + 1
    for t in range(count):
        one, two = two_blocks(vector[:, t * width : (t + 1) * width])
        halo[pos[0] * lb + 2 * t] = one
        halo[pos[0] * lb + 2 * t + 1] = two
    for k, wire in enumerate(wires):
        start = (pos[0] ^ (k + 1)) * lb
        base = place * (count + 1)
        step = step_of(wire[base + count])
        for t in range(count):
            one, two = two_blocks(decode(wire[base + t], step))
            halo[start + 2 * t] = one
            halo[start + 2 * t + 1] = two
    tiles = edge_tiles(ifr)
    for k, edge in enumerate(edges):
        for other in range(2):
            start = n_row * lb + (((pos[1] // 2) ^ k) * 2 + ((pos[1] % 2) ^ other)) * ifr
            found = decode_edge(edge, (other * places + place) * tiles, ifr)
            for q in range(0, ifr, 2):
                blocks = two_blocks(found[q // 2])
                halo[start + q] = blocks[0]
                if q + 1 < ifr:
                    halo[start + q + 1] = blocks[1]


def write_halves(table, pos, keep, send):
    height = keep.shape[0]
    core = pos[1] % 2
    keep[...] = table[pl.ds(pl.multiple_of(core * height, 8), height), :]
    send[...] = table[pl.ds(pl.multiple_of((1 - core) * height, 8), height), :]


def read_halves(mine, other, pos, table):
    height = mine.shape[0]
    core = pos[1] % 2
    table[pl.ds(pl.multiple_of(core * height, 8), height), :] = mine[...]
    table[pl.ds(pl.multiple_of((1 - core) * height, 8), height), :] = other[...]


def forward(halo, pos, stored, diagonal, where, out, diag_out):
    lb, kb = stored.shape[0], stored.shape[1]
    own = pos[0] * lb
    groups = stored.shape[2] // (2 * kb)
    for i in range(0, lb, 2):
        sums, diags = [], []
        for m in (i, i + 1):
            row = jnp.concatenate([halo[where[m * groups + g]] for g in range(groups)], axis=1)
            sums.append(lax.dot_general(row, stored[m], (((1,), (1,)), ((), ())), preferred_element_type=f32))
            diags.append(lax.dot_general(halo[own + m], diagonal[m], (((1,), (1,)), ((), ())), preferred_element_type=f32))
        out[:, i * kb : (i + 2) * kb] = jnp.concatenate(sums, axis=1)
        diag_out[:, i * kb : (i + 2) * kb] = jnp.concatenate(diags, axis=1)


def returned(index, own, rows, edge_own, edges, bnd, back, target):
    count, _, width = back.shape
    ifr = bnd.shape[0]
    tiles = edge_tiles(ifr)
    n = target.shape[0]
    steps = [step_of(row[index * (count + 1) + count]) for row in rows]
    for t in range(count):
        total = own[index * n : (index + 1) * n, t * width : (t + 1) * width]
        for row, step in zip(rows, steps):
            total = total + decode(row[index * (count + 1) + t], step)
        back[t] = total
    found = [edge_own[index * tiles + t] for t in range(tiles)]
    for edge in edges:
        found = [a + b for a, b in zip(found, decode_edge(edge, index * tiles, ifr))]
    low = low_half(back.shape[1:])
    for q in range(ifr):
        side = jnp.broadcast_to(bnd[q] % 2, low.shape)
        block = jnp.where(side == q % 2, found[q // 2], swap(found[q // 2]))
        spot = bnd[q] // 2
        back[spot] = back[spot] + jnp.where(low == (side == 0), block, 0.0)
    for t in range(count):
        span = slice(t * width, (t + 1) * width)
        target[:, span] = target[:, span] + back[t]


def eliminate(table, full):
    order = table.shape[0]
    rows = lax.broadcasted_iota(jnp.int32, table.shape, 0)
    for j in range(0, order, 2):
        left = jnp.broadcast_to(table[:, j : j + 1], table.shape)
        right = jnp.broadcast_to(table[:, j + 1 : j + 2], table.shape)
        one, two = table[j : j + 1, :], table[j + 1 : j + 2, :]
        over = 1.0 / left[j : j + 1, :]
        ratio = left[j + 1 : j + 2, :] * over
        beside = right[j : j + 1, :]
        two = two - ratio * one
        second = two * (1.0 / (right[j + 1 : j + 2, :] - ratio * beside))
        first = (one - beside * second) * over
        moved = table - left * first - right * second
        if full:
            table = jnp.where(rows == j, first, jnp.where(rows == j + 1, second, moved))
        else:
            table = jnp.where(rows > j + 1, moved, jnp.where(rows == j + 1, two, table))
    return table


def unit(order):
    return (
        lax.broadcasted_iota(jnp.int32, (order, order), 0) == lax.broadcasted_iota(jnp.int32, (order, order), 1)
    ).astype(f32)


def inverse(matrix):
    order = matrix.shape[0]
    return eliminate(jnp.concatenate([matrix, unit(order)], axis=1), True)[:, order:]


def cholesky_inverse(matrix):
    order = matrix.shape[0]
    done = eliminate(jnp.concatenate([matrix, unit(order)], axis=1), False)
    pivots = jnp.sum(done[:, :order] * unit(order), axis=1, keepdims=True)
    return done[:, order:] * (1.0 / jnp.sqrt(pivots))


def coefficients(table, gram, xp, pp, pax, pap_inverse, total_rows):
    n = gram.shape[0]
    waw, wap = table[0:n, :n], table[0:n, n:]
    wax, wx = table[n : 2 * n, :n], table[n : 2 * n, n:]
    wp, ww = table[2 * n : 3 * n, :n], table[2 * n : 3 * n, n:]
    waw = waw + waw.T
    first = nn(pap_inverse, wap.T)
    if pax is None:
        rhs = -wax
    else:
        second = nn(pap_inverse, pax)
        rhs = nn(wap, second) - wax
    schur = waw - nn(wap, first)
    zw = eliminate(jnp.concatenate([schur, rhs], axis=1), True)[:, n:]
    zp = -nn(first, zw)
    if pax is not None:
        zp = zp - second
    cross = nn(wx.T, zw) + nn(xp, zp)
    zwt, zpt = zw.T, zp.T
    inner = nn(zwt, nn(ww, zw) + nn(wp, zp)) + nn(zpt, nn(wp.T, zw) + nn(pp, zp))
    lengths = (gram + cross + cross.T + inner) / total_rows
    return zw, zp, zwt, zpt, cross, inner, wax, cholesky_inverse(lengths)


def prepare_kernel(groups, base, vals, faces, rows, cols, face_rows, face_src, stored, joined, diagonal, where):
    lb, kb = faces.shape[0], faces.shape[1]

    def twice(block):
        wide = block.astype(f32)
        return jnp.concatenate([wide, wide], axis=1).astype(bf16)

    for k in range(lb):
        diagonal[k] = twice(vals[k])
    for g in range(groups):
        half = (g % 2) * kb
        for m in range(lb):
            if g < groups - 1:
                k = (g + 1) * lb + m
                i, target, block = rows[k], cols[k], twice(vals[k])
            else:
                i, target, block = face_rows[m], base + face_src[m], twice(faces[m])
            stored[i, :, 2 * kb * g : 2 * kb * (g + 1)] = block
            joined[i, :, kb * g : kb * (g + 1)] = block[:, half : half + kb]
            where[i * groups + g] = target


def wire_kernel(x, p, bnd, wire, edge):
    write_wire(x, bnd, wire, edge, 0)
    write_wire(p, bnd, wire, edge, 1)


def partial_kernel(n_row, n_z, merge, ifr, vector, joined, where, pos, *refs):
    refs = list(refs)
    parts = n_row + 2
    earlier = [refs.pop(0) for _ in range(parts)] if merge else []
    outs, acc = refs[:-1], refs[-1]
    own, core_keep, core_send, *row_outs = outs
    width = acc.shape[2]
    count = vector.shape[1] // width
    lb, kb, n = 2 * count, joined.shape[1], vector.shape[0]
    tiles = edge_tiles(ifr)
    groups = joined.shape[2] // kb
    low = low_half(acc.shape[1:])
    core = pos[1] % 2
    for source, target in zip(earlier, outs):
        target[pl.ds(0, source.shape[0])] = source[...]
    own_base = n if merge else 0
    row_base = count + 1 if merge else 0
    edge_base = n_z * tiles if merge else 0
    acc[...] = jnp.zeros(acc.shape, f32)
    for pair in range(count):
        both = two_blocks(vector[:, pair * width : (pair + 1) * width])
        for m in range(2):
            i = 2 * pair + m
            blocks = jnp.concatenate([joined[i], joined[i]], axis=0)
            out = jnp.dot(both[m], blocks, preferred_element_type=f32)
            for t in range(groups // 2):
                tile = out[:, width * t : width * (t + 1)]
                one = where[i * groups + 2 * t]
                two = where[i * groups + 2 * t + 1]
                acc[one] = acc[one] + jnp.where(low, tile, 0.0)
                acc[two] = acc[two] + jnp.where(low, 0.0, tile)

    def folded(one, two):
        return jnp.where(low, one, two) + swap(jnp.where(low, two, one))

    for k in range(n_row):
        start = (pos[0] ^ k) * lb
        found = [folded(acc[start + 2 * t], acc[start + 2 * t + 1]) for t in range(count)]
        if k == 0:
            for t in range(count):
                own[own_base : own_base + n, t * width : (t + 1) * width] = found[t]
        else:
            coded, power = code(found)
            for t in range(count):
                row_outs[k - 1][row_base + t] = coded[t].astype(jnp.int16)
            row_outs[k - 1][row_base + count] = power.astype(jnp.int16)
    for z in range(n_z):
        spot = edge_base + z * tiles
        for side in range(2):
            start = n_row * lb + (z * 2 + (core if side == 0 else 1 - core)) * ifr
            found = []
            for t in range(tiles):
                one = acc[start + 2 * t] if 2 * t < ifr else jnp.zeros(acc.shape[1:], f32)
                two = acc[start + 2 * t + 1] if 2 * t + 1 < ifr else jnp.zeros(acc.shape[1:], f32)
                found.append(folded(one, two))
            if side == 0:
                for t in range(tiles):
                    core_keep[spot + t] = found[t]
            else:
                for t, tile in enumerate(code_edge(found, ifr)):
                    core_send[spot + t] = tile


def pair_kernel(n_z, count, ifr, keep, got, pos, own, *outs):
    tiles = edge_tiles(ifr)
    for k in range(n_z):
        z = (pos[1] // 2) ^ k
        for v in range(count):
            spot = (v * n_z + z) * tiles
            there = decode_edge(got, spot, ifr)
            total = [keep[spot + t] + there[t] for t in range(tiles)]
            if k > 0:
                total = code_edge(total, ifr)
            target = own if k == 0 else outs[k - 1]
            for t in range(tiles):
                target[v * tiles + t] = total[t]


def split_halo(refs, n_row, n_z):
    return [refs.pop(0) for _ in range(n_row - 1)], [refs.pop(0) for _ in range(n_z)]


def start_image_kernel(n_row, n_z, ifr, *refs):
    refs = list(refs)
    wires, edges = split_halo(refs, n_row, n_z)
    stored, diagonal, where, pos, x, p, half_x, diag_x, half_p, diag_p, keep, send, halo_x, halo_p, table = refs
    n = x.shape[0]
    for place, (vector, half, diag, halo) in enumerate(((x, half_x, diag_x, halo_x), (p, half_p, diag_p, halo_p))):
        fill_halo(vector, wires, edges, pos, halo, ifr, place, 2)
        forward(halo, pos, stored, diagonal, where, half, diag)
        half[...] = half[...] + 0.5 * diag[...]
    table[0:n, :] = nt(x[...], jnp.concatenate([half_x[...], x[...]], axis=0))
    table[n : 2 * n, :] = nt(p[...], jnp.concatenate([x[...], p[...]], axis=0))
    table[2 * n : 3 * n, :] = nt(p[...], jnp.concatenate([half_p[...], half_x[...]], axis=0))
    table[2 * n : 3 * n, n:] = table[2 * n : 3 * n, n:] + nt(half_p[...], x[...])
    write_halves(table, pos, keep, send)


def take_returned(refs, n_row, n_z):
    own = refs.pop(0)
    rows = [refs.pop(0) for _ in range(n_row - 1)]
    edge_own = refs.pop(0)
    return own, rows, edge_own, [refs.pop(0) for _ in range(n_z - 1)]


def update_kernel(n_row, n_z, *refs):
    refs = list(refs)
    back_parts = take_returned(refs, n_row, n_z)
    mine, other, pos, bnd, x, half, diag, precond, table, ax, energy, w, wire, edge, back = refs
    n = x.shape[0]
    read_halves(mine, other, pos, table)
    ax[...] = half[...] + 0.5 * diag[...]
    returned(0, *back_parts, bnd, back, ax)
    stored, gram = table[0:n, 0:n], table[0:n, n:]
    total = stored + stored.T
    energy[...] = total
    ritz = nn(total, inverse(0.5 * (gram + gram.T)))
    w[...] = precond[...] * (ax[...] - nn(ritz, x[...]))
    write_wire(w, bnd, wire, edge)


def inverse_kernel(table, solved):
    n = solved.shape[0]
    stored = table[2 * n : 3 * n, 0:n]
    solved[...] = inverse(stored + stored.T)


def update_image_kernel(n_row, n_z, ifr, first, *refs):
    refs = list(refs)
    wires, edges = split_halo(refs, n_row, n_z)
    stored, diagonal, where, pos, w, x, p, ax, ap, half, diag, keep, send, halo, table = refs
    n = w.shape[0]
    fill_halo(w, wires, edges, pos, halo, ifr)
    forward(halo, pos, stored, diagonal, where, half, diag)
    half[...] = half[...] + 0.5 * diag[...]
    here = w[...]
    table[0:n, :] = nt(here, jnp.concatenate([half[...], ap[...]], axis=0))
    table[n : 2 * n, :] = nt(here, jnp.concatenate([ax[...], x[...]], axis=0))
    table[2 * n : 3 * n, :] = nt(here, jnp.concatenate([p[...], here], axis=0))
    if first:
        table[0:n, n:] = table[0:n, n:] + nt(half[...], p[...])
    write_halves(table, pos, keep, send)


def move_kernel(n_row, n_z, total_rows, *refs):
    refs = list(refs)
    start_parts = take_returned(refs, n_row, n_z)
    back_parts = take_returned(refs, n_row, n_z)
    mine, other, pos, bnd, start, energy, pap_inverse, x, p, ax, ap, ap_diag, w, aw, aw_diag, precond = refs[:16]
    x_out, ax_out, w_out, wire, edge, step_x, step_a, small, table, back, ap_full, aw_full = refs[16:]
    n = x.shape[0]
    read_halves(mine, other, pos, table)
    gram = start[0:n, n:]
    px, pp = start[n : 2 * n, 0:n], start[n : 2 * n, n:]
    pax = start[2 * n : 3 * n, n:]
    zw, zp, zwt, zpt, cross, inner, wax, scale = coefficients(
        table, 0.5 * (gram + gram.T), px.T, pp, pax, pap_inverse[...], total_rows
    )
    ap_full[...] = ap[...] + 0.5 * ap_diag[...]
    returned(1, *start_parts, bnd, back, ap_full)
    aw_full[...] = aw[...] + 0.5 * aw_diag[...]
    returned(0, *back_parts, bnd, back, aw_full)
    step_a[...] = nn(zpt, ap_full[...]) + nn(zwt, aw_full[...])
    step_x[...] = nn(zwt, w[...]) + nn(zpt, p[...])
    x_out[...] = nn(scale, x[...] + step_x[...])
    ax_out[...] = nn(scale, ax[...] + step_a[...])
    gain = nn(wax.T, zw) + nn(pax.T, zp)
    gain = 0.5 * (gain + gain.T)
    ritz = nn(scale, nn(energy[...] + gain, scale.T)) / total_rows
    w_out[...] = precond[...] * (ax_out[...] - nn(ritz, x_out[...]))
    write_wire(w_out, bnd, wire, edge)
    small[0:n, :] = -gain
    small[n : 2 * n, :] = cross + inner
    small[2 * n : 3 * n, :] = inner
    small[3 * n : 4 * n, :] = scale


def settle_kernel(small, step_x, step_a, p_out, ap_out, state):
    n = small.shape[1]
    scale = small[3 * n : 4 * n, :]
    scale_t = scale.T
    p_out[...] = nn(scale, step_x[...])
    ap_out[...] = nn(scale, step_a[...])
    state[0:n, :] = inverse(nn(scale, nn(small[0:n, :], scale_t)))
    state[n : 2 * n, :] = nn(scale, nn(small[n : 2 * n, :], scale_t))
    state[2 * n : 3 * n, :] = nn(scale, nn(small[2 * n : 3 * n, :], scale_t))


def finish_kernel(total_rows, mine, other, pos, state, x, p, w, x_out, p_out, table):
    n = x.shape[0]
    read_halves(mine, other, pos, table)
    zw, zp, zwt, zpt, _, _, _, scale = coefficients(
        table,
        unit(n) * total_rows,
        state[n : 2 * n, :],
        state[2 * n : 3 * n, :],
        None,
        state[0:n, :],
        total_rows,
    )
    step = nn(zwt, w[...]) + nn(zpt, p[...])
    x_out[...] = nn(scale, x[...] + step)
    p_out[...] = nn(scale, step)


def run(kernel, name, outs, ins, scratch=(), smem=(), smem_outs=(), flops=1000000):
    in_specs = [pl.BlockSpec(memory_space=SMEM if i in smem else VMEM) for i in range(len(ins))]
    out_specs = [pl.BlockSpec(memory_space=SMEM if i in smem_outs else VMEM) for i in range(len(outs))]
    moved = sum(a.size * a.dtype.itemsize for a in ins) + sum(o.size * o.dtype.itemsize for o in outs)
    return pl.pallas_call(
        kernel,
        name=name,
        out_shape=outs,
        in_specs=in_specs,
        out_specs=out_specs,
        scratch_shapes=list(scratch),
        compiler_params=pltpu.CompilerParams(vmem_limit_bytes=48 * 1024 * 1024),
        cost_estimate=pl.CostEstimate(flops=flops, bytes_accessed=moved, transcendentals=0),
    )(*ins)


def shaped(*shape, dtype=f32):
    return jax.ShapeDtypeStruct(shape, dtype)


def local(n_sub, n_row, modes, search, precond, in_row, in_col, in_val, bnd_rows, if_row, if_src, if_val):
    nin, kb = in_val.shape[2], in_val.shape[3]
    rows, n = modes.shape
    lb = rows // kb
    ifr = bnd_rows.shape[2]
    groups = nin // lb
    n_z = n_sub // 2
    total_rows = float(rows * n_sub * n_row)
    halo_blocks = n_row * lb + n_sub * ifr
    bnd = bnd_rows[0, 0]
    me_row, me_sub = lax.axis_index("row"), lax.axis_index("sub")
    pos = jnp.stack([me_row, me_sub]).astype(jnp.int32)
    after = lax.optimization_barrier

    def row_send(value, k):
        return lax.ppermute(value, "row", [(r, r ^ k) for r in range(n_row)])

    def sub_send(value, k):
        return lax.ppermute(value, "sub", [(s, s ^ k) for s in range(n_sub)])

    tiles = lb // 2
    edges_in = edge_tiles(ifr)

    def coded(count):
        return shaped(count, n, 2 * kb, dtype=jnp.int16)

    def halo_of(own, edge):
        rows_got = [row_send(own, k) for k in range(1, n_row)]
        pair = jnp.concatenate([edge, sub_send(edge, 1)], axis=0)
        return rows_got + [pair] + [sub_send(pair, 2 * k) for k in range(1, n_z)]

    def groups_of_four(value, size, send):
        base = 1
        while base < size:
            got = [value] + [send(value, base * m) for m in range(1, min(4, size // base))]
            while len(got) > 1:
                got = [got[i] + got[i + 1] for i in range(0, len(got), 2)]
            value = got[0]
            base *= 4
        return value

    def z_send(value, k):
        return sub_send(value, 2 * k)

    def sum_halves(keep, send, meanwhile=()):
        total = keep + sub_send(send, 1)
        total = groups_of_four(total, n_z, z_send)
        total, *meanwhile = after((total, *meanwhile))
        total = groups_of_four(total, n_row, row_send)
        return [total, sub_send(total, 1)], meanwhile

    def partials(source, earlier=()):
        m = 2 if earlier else 1
        outs = [shaped(m * n, rows), shaped(m * n_z * edges_in, n, 2 * kb), coded(m * n_z * edges_in)]
        outs += [coded(m * (tiles + 1))] * (n_row - 1)
        return run(
            functools.partial(partial_kernel, n_row, n_z, m > 1, ifr),
            "partials",
            outs,
            [source, joined, where, pos] + list(earlier),
            [VMEM((halo_blocks, n, 2 * kb), f32)],
            smem=(2, 3),
        )

    def send_partials(parts, m):
        own, edge_keep, edge_send, *row_parts = parts
        edge_got = sub_send(edge_send, 1)
        rows_got = [row_send(row_parts[k - 1], k) for k in range(1, n_row)]
        edge_own, *outs = run(
            functools.partial(pair_kernel, n_z, m, ifr),
            "pair",
            [shaped(m * edges_in, n, 2 * kb)] + [coded(m * edges_in)] * (n_z - 1),
            [edge_keep, edge_got, pos],
            smem=(2,),
        )
        return [own] + rows_got + [edge_own] + [z_send(outs[k - 1], k) for k in range(1, n_z)]

    x, p = modes.T, search.T
    scaling = precond.reshape(1, rows)
    wire_shapes = [coded(tiles + 1), coded(edges_in)]
    wire, edge = run(wire_kernel, "wire", [coded(2 * (tiles + 1)), coded(2 * edges_in)], [x, p, bnd], smem=(2,))
    halo = halo_of(wire, edge)
    in_val, if_val, halo[0], halo[-1] = after((in_val, if_val, halo[0], halo[-1]))
    stored, joined, diagonal, where = run(
        functools.partial(prepare_kernel, groups, n_row * lb),
        "prepare",
        [
            shaped(lb, kb, groups * 2 * kb, dtype=bf16),
            shaped(lb, kb, groups * kb, dtype=bf16),
            shaped(lb, kb, 2 * kb, dtype=bf16),
            shaped(lb * groups, dtype=jnp.int32),
        ],
        [in_val[0, 0], if_val[0, 0], in_row[0, 0], in_col[0, 0], if_row[0, 0], if_src[0, 0]],
        smem=(2, 3, 4, 5),
        smem_outs=(3,),
    )
    parts = partials(p, partials(x))
    blocks = [stored, diagonal, where, pos]
    halo_scratch = VMEM((halo_blocks, n, 2 * kb), bf16)
    back_scratch = VMEM((tiles, n, 2 * kb), f32)
    whole = shaped(n, rows)

    table_shape = shaped(3 * n, 2 * n)
    halves_shape = [shaped(3 * n // 2, 2 * n)] * 2
    table_scratch = VMEM((3 * n, 2 * n), f32)
    count = len(halo)
    half_x, diag_x, half_p, diag_p, keep, send = run(
        functools.partial(start_image_kernel, n_row, n_z, ifr),
        "start_image",
        [whole] * 4 + halves_shape,
        halo + blocks + [x, p],
        [halo_scratch, halo_scratch, table_scratch],
        smem=(count + 2, count + 3),
    )
    start_back = send_partials(parts, 2)
    keep, send, *start_back = after((keep, send, *start_back))
    halves, _ = sum_halves(keep, send)
    count = len(start_back)
    table, ax, energy, w, w_wire, w_edge = run(
        functools.partial(update_kernel, n_row, n_z),
        "update",
        [table_shape, whole, shaped(n, n), whole] + wire_shapes,
        start_back + halves + [pos, bnd, x, half_x, diag_x, scaling],
        [back_scratch],
        smem=(count + 2, count + 3),
    )
    w_halo = halo_of(w_wire, w_edge)
    (pap_inverse,) = run(inverse_kernel, "pap_inverse", [shaped(n, n)], [table])
    w_back = send_partials(partials(w), 1)

    def update_image(first, halo, w, x, p, ax, ap):
        count = len(halo)
        return run(
            functools.partial(update_image_kernel, n_row, n_z, ifr, first),
            "update_image",
            [whole, whole] + halves_shape,
            halo + blocks + [w, x, p, ax, ap],
            [halo_scratch, table_scratch],
            smem=(count + 2, count + 3),
        )

    half_w, diag_w, keep, send = update_image(True, w_halo, w, x, p, ax, half_p)
    keep, send, *w_back = after((keep, send, *w_back))
    halves, (pap_inverse,) = sum_halves(keep, send, [pap_inverse])
    count = len(start_back) + len(w_back)
    x, ax, w, w_wire, w_edge, step_x, step_a, small = run(
        functools.partial(move_kernel, n_row, n_z, total_rows),
        "move",
        [whole] * 3 + wire_shapes + [whole, whole, shaped(4 * n, n)],
        start_back + w_back + halves + [pos, bnd, table, energy, pap_inverse, x, p, ax, half_p, diag_p, w, half_w, diag_w, scaling],
        [table_scratch, back_scratch, VMEM((n, rows), f32), VMEM((n, rows), f32)],
        smem=(count + 2, count + 3),
    )
    w_halo = halo_of(w_wire, w_edge)
    p, ap, state = run(settle_kernel, "settle", [whole, whole, shaped(3 * n, n)], [small, step_x, step_a])
    _, _, keep, send = update_image(False, w_halo, w, x, p, ax, ap)
    halves, _ = sum_halves(keep, send)
    x, p = run(
        functools.partial(finish_kernel, total_rows),
        "finish",
        [whole, whole],
        halves + [pos, state, x, p, w],
        [table_scratch],
        smem=(2,),
    )
    return (x.T, p.T)


def solution(mesh):
    return jax.shard_map(
        functools.partial(local, mesh.shape["sub"], mesh.shape["row"]),
        mesh=mesh,
        in_specs=(
            P(("sub", "row"), None),
            P(("sub", "row"), None),
            P(("sub", "row")),
            P("sub", "row", None),
            P("sub", "row", None),
            P("sub", "row", None, None, None),
            P("sub", "row", None),
            P("sub", "row", None),
            P("sub", "row", None),
            P("sub", "row", None, None, None),
        ),
        out_specs=(P(("sub", "row"), None), P(("sub", "row"), None)),
        check_vma=False,
    )
```

```python
import functools

import jax
import jax.numpy as jnp
from jax import lax
from jax.experimental import pallas as pl
from jax.experimental.pallas import tpu as pltpu
from jax.sharding import PartitionSpec as P

f32 = jnp.float32
bf16 = jnp.bfloat16
precise_mode = lax.Precision.HIGHEST
VMEM = pltpu.VMEM
SMEM = pltpu.SMEM


def nn(a, b):
    return lax.dot_general(a, b, (((1,), (0,)), ((), ())), precision=precise_mode, preferred_element_type=f32)


def nt(a, b):
    return lax.dot_general(a, b, (((1,), (1,)), ((), ())), precision=precise_mode, preferred_element_type=f32)


TOP = 32000.0
LOG_STEP = 0.08664339756999316


def low_half(shape):
    return lax.broadcasted_iota(jnp.int32, shape, 1) < shape[1] // 2


def swap(tile):
    return pltpu.roll(tile, tile.shape[1] // 2, 1)


def two_blocks(tile):
    low = low_half(tile.shape)
    high = tile.astype(bf16).astype(f32)
    rest = tile - high
    one = jnp.where(low, high, swap(rest))
    two = jnp.where(low, swap(high), rest)
    return one.astype(bf16), two.astype(bf16)


def code(tiles):
    most = jnp.abs(tiles[0])
    for tile in tiles[1:]:
        most = jnp.maximum(most, jnp.abs(tile))
    most = jnp.maximum(jnp.max(most, axis=1, keepdims=True), 1e-30)
    power = jnp.broadcast_to(jnp.ceil(jnp.log(most) * (1.0 / LOG_STEP)), tiles[0].shape)
    factor = TOP * jnp.exp(power * -LOG_STEP)
    return [jnp.floor(tile * factor + 0.5).astype(jnp.int32) for tile in tiles], power.astype(jnp.int32)


def step_of(power):
    return jnp.exp(power.astype(jnp.int32).astype(f32) * LOG_STEP) * (1.0 / TOP)


def decode(tile, step):
    return tile.astype(jnp.int32).astype(f32) * step


def edge_tiles(ifr):
    return ifr // 2 + 1


def code_edge(tiles, ifr):
    low = low_half(tiles[0].shape)
    tiles = list(tiles)
    tiles[-1] = jnp.where(low, tiles[-1], 0.0) if ifr % 2 else jnp.zeros_like(tiles[-1])
    coded, power = code(tiles)
    coded[-1] = jnp.where(low, coded[-1], power) if ifr % 2 else power
    return [tile.astype(jnp.int16) for tile in coded]


def decode_edge(ref, start, ifr):
    tiles = [ref[start + t].astype(jnp.int32) for t in range(edge_tiles(ifr))]
    low = low_half(tiles[-1].shape)
    power = jnp.where(low, swap(tiles[-1]), tiles[-1]) if ifr % 2 else tiles[-1]
    step = step_of(power)
    return [tile.astype(f32) * step for tile in tiles]


def write_wire(vector, bnd, wire, edge, place=0):
    ifr = bnd.shape[0]
    width = wire.shape[2]
    count = vector.shape[1] // width
    base = place * (count + 1)
    coded, power = code([vector[:, t * width : (t + 1) * width] for t in range(count)])
    for t in range(count):
        wire[base + t] = coded[t].astype(jnp.int16)
    wire[base + count] = power.astype(jnp.int16)
    low = low_half(power.shape)
    slots = []
    for q in range(ifr):
        tile = wire[base + bnd[q] // 2].astype(jnp.int32)
        side = jnp.broadcast_to(bnd[q] % 2, tile.shape)
        slots.append(jnp.where(side == q % 2, tile, swap(tile)))
    slots.append(power)
    if len(slots) % 2:
        slots.append(power)
    for t in range(edge_tiles(ifr)):
        edge[place * edge_tiles(ifr) + t] = jnp.where(low, slots[2 * t], slots[2 * t + 1]).astype(jnp.int16)


def fill_halo(vector, wires, edges, pos, halo, ifr, place=0, base=0):
    width = halo.shape[2]
    count = vector.shape[1] // width
    lb = 2 * count
    n_row = len(wires) + 1
    for t in range(count):
        one, two = two_blocks(vector[:, t * width : (t + 1) * width])
        halo[pos[0] * lb + 2 * t] = one
        halo[pos[0] * lb + 2 * t + 1] = two
    for k, wire in enumerate(wires):
        start = (pos[0] ^ (k + 1)) * lb
        spot = base + place * (count + 1)
        step = step_of(wire[spot + count])
        for t in range(count):
            one, two = two_blocks(decode(wire[spot + t], step))
            halo[start + 2 * t] = one
            halo[start + 2 * t + 1] = two
    tiles = edge_tiles(ifr)
    for k, pair in enumerate(edges):
        for other, (edge, spot) in enumerate(pair):
            start = n_row * lb + (((pos[1] // 2) ^ k) * 2 + ((pos[1] % 2) ^ other)) * ifr
            found = decode_edge(edge, spot + place * tiles, ifr)
            for q in range(0, ifr, 2):
                blocks = two_blocks(found[q // 2])
                halo[start + q] = blocks[0]
                if q + 1 < ifr:
                    halo[start + q + 1] = blocks[1]


def write_halves(table, pos, keep, send):
    height = keep.shape[0]
    core = pos[1] % 2
    keep[...] = table[pl.ds(pl.multiple_of(core * height, 8), height), :]
    send[...] = table[pl.ds(pl.multiple_of((1 - core) * height, 8), height), :]


def read_halves(mine, other, pos, table):
    height = mine.shape[0]
    core = pos[1] % 2
    table[pl.ds(pl.multiple_of(core * height, 8), height), :] = mine[...]
    table[pl.ds(pl.multiple_of((1 - core) * height, 8), height), :] = other[...]


def forward(halo, pos, stored, diagonal, where, out, diag_out):
    lb, kb = stored.shape[0], stored.shape[1]
    own = pos[0] * lb
    groups = stored.shape[2] // (2 * kb)
    for i in range(0, lb, 2):
        sums, diags = [], []
        for m in (i, i + 1):
            row = jnp.concatenate([halo[where[m * groups + g]] for g in range(groups)], axis=1)
            sums.append(lax.dot_general(row, stored[m], (((1,), (1,)), ((), ())), preferred_element_type=f32))
            diags.append(lax.dot_general(halo[own + m], diagonal[m], (((1,), (1,)), ((), ())), preferred_element_type=f32))
        out[:, i * kb : (i + 2) * kb] = jnp.concatenate(sums, axis=1)
        diag_out[:, i * kb : (i + 2) * kb] = jnp.concatenate(diags, axis=1)


def returned(index, own, rows, edge_own, edges, bnd, back, target):
    count, _, width = back.shape
    ifr = bnd.shape[0]
    tiles = edge_tiles(ifr)
    n = target.shape[0]
    steps = [step_of(row[index * (count + 1) + count]) for row in rows]
    for t in range(count):
        total = own[index * n : (index + 1) * n, t * width : (t + 1) * width]
        for row, step in zip(rows, steps):
            total = total + decode(row[index * (count + 1) + t], step)
        back[t] = total
    found = [edge_own[index * tiles + t] for t in range(tiles)]
    for edge in edges:
        found = [a + b for a, b in zip(found, decode_edge(edge, index * tiles, ifr))]
    low = low_half(back.shape[1:])
    for q in range(ifr):
        side = jnp.broadcast_to(bnd[q] % 2, low.shape)
        block = jnp.where(side == q % 2, found[q // 2], swap(found[q // 2]))
        spot = bnd[q] // 2
        back[spot] = back[spot] + jnp.where(low == (side == 0), block, 0.0)
    for t in range(count):
        span = slice(t * width, (t + 1) * width)
        target[:, span] = target[:, span] + back[t]


def eliminate(table, full):
    order = table.shape[0]
    rows = lax.broadcasted_iota(jnp.int32, table.shape, 0)
    for j in range(0, order, 2):
        left = jnp.broadcast_to(table[:, j : j + 1], table.shape)
        right = jnp.broadcast_to(table[:, j + 1 : j + 2], table.shape)
        one, two = table[j : j + 1, :], table[j + 1 : j + 2, :]
        over = 1.0 / left[j : j + 1, :]
        ratio = left[j + 1 : j + 2, :] * over
        beside = right[j : j + 1, :]
        two = two - ratio * one
        second = two * (1.0 / (right[j + 1 : j + 2, :] - ratio * beside))
        first = (one - beside * second) * over
        moved = table - left * first - right * second
        if full:
            table = jnp.where(rows == j, first, jnp.where(rows == j + 1, second, moved))
        else:
            table = jnp.where(rows > j + 1, moved, jnp.where(rows == j + 1, two, table))
    return table


def unit(order):
    return (
        lax.broadcasted_iota(jnp.int32, (order, order), 0) == lax.broadcasted_iota(jnp.int32, (order, order), 1)
    ).astype(f32)


def inverse(matrix):
    order = matrix.shape[0]
    return eliminate(jnp.concatenate([matrix, unit(order)], axis=1), True)[:, order:]


def cholesky_inverse(matrix):
    order = matrix.shape[0]
    done = eliminate(jnp.concatenate([matrix, unit(order)], axis=1), False)
    pivots = jnp.sum(done[:, :order] * unit(order), axis=1, keepdims=True)
    return done[:, order:] * (1.0 / jnp.sqrt(pivots))


def coefficients(table, gram, xp, pp, pax, pap_inverse, total_rows):
    n = gram.shape[0]
    waw, wap = table[0:n, :n], table[0:n, n:]
    wax, wx = table[n : 2 * n, :n], table[n : 2 * n, n:]
    wp, ww = table[2 * n : 3 * n, :n], table[2 * n : 3 * n, n:]
    waw = waw + waw.T
    first = nn(pap_inverse, wap.T)
    if pax is None:
        rhs = -wax
    else:
        second = nn(pap_inverse, pax)
        rhs = nn(wap, second) - wax
    schur = waw - nn(wap, first)
    zw = eliminate(jnp.concatenate([schur, rhs], axis=1), True)[:, n:]
    zp = -nn(first, zw)
    if pax is not None:
        zp = zp - second
    cross = nn(wx.T, zw) + nn(xp, zp)
    zwt, zpt = zw.T, zp.T
    inner = nn(zwt, nn(ww, zw) + nn(wp, zp)) + nn(zpt, nn(wp.T, zw) + nn(pp, zp))
    lengths = (gram + cross + cross.T + inner) / total_rows
    return zw, zp, zwt, zpt, cross, inner, wax, cholesky_inverse(lengths)


def prepare_kernel(groups, base, vals, faces, rows, cols, face_rows, face_src, stored, joined, diagonal, where):
    lb, kb = faces.shape[0], faces.shape[1]

    def twice(block):
        wide = block.astype(f32)
        return jnp.concatenate([wide, wide], axis=1).astype(bf16)

    for k in range(lb):
        diagonal[k] = twice(vals[k])
    for g in range(groups):
        half = (g % 2) * kb
        for m in range(lb):
            if g < groups - 1:
                k = (g + 1) * lb + m
                i, target, block = rows[k], cols[k], twice(vals[k])
            else:
                i, target, block = face_rows[m], base + face_src[m], twice(faces[m])
            stored[i, :, 2 * kb * g : 2 * kb * (g + 1)] = block
            joined[i, :, kb * g : kb * (g + 1)] = block[:, half : half + kb]
            where[i * groups + g] = target


def wire_kernel(x, p, bnd, wire, edge):
    write_wire(x, bnd, wire, edge, 0)
    write_wire(p, bnd, wire, edge, 1)


def partial_kernel(n_row, n_z, merge, extra, ifr, vector, joined, where, pos, *refs):
    refs = list(refs)
    parts = n_row + 2
    earlier = [refs.pop(0) for _ in range(parts)] if merge else []
    more = [refs.pop(0) for _ in range(2)] if extra else []
    outs, acc = refs[:-1], refs[-1]
    own, core_keep, core_send, *row_outs = outs
    width = acc.shape[2]
    count = vector.shape[1] // width
    lb, kb, n = 2 * count, joined.shape[1], vector.shape[0]
    tiles = edge_tiles(ifr)
    groups = joined.shape[2] // kb
    low = low_half(acc.shape[1:])
    core = pos[1] % 2
    for source, target in zip(earlier, outs):
        target[pl.ds(0, source.shape[0])] = source[...]
    own_base = n if merge else 0
    row_base = count + 1 if merge else 0
    edge_base = n_z * tiles if merge else 0
    acc[...] = jnp.zeros(acc.shape, f32)
    for pair in range(count):
        both = two_blocks(vector[:, pair * width : (pair + 1) * width])
        for m in range(2):
            i = 2 * pair + m
            blocks = jnp.concatenate([joined[i], joined[i]], axis=0)
            out = jnp.dot(both[m], blocks, preferred_element_type=f32)
            for t in range(groups // 2):
                tile = out[:, width * t : width * (t + 1)]
                one = where[i * groups + 2 * t]
                two = where[i * groups + 2 * t + 1]
                acc[one] = acc[one] + jnp.where(low, tile, 0.0)
                acc[two] = acc[two] + jnp.where(low, 0.0, tile)

    def folded(one, two):
        return jnp.where(low, one, two) + swap(jnp.where(low, two, one))

    for k in range(n_row):
        start = (pos[0] ^ k) * lb
        found = [folded(acc[start + 2 * t], acc[start + 2 * t + 1]) for t in range(count)]
        if k == 0:
            for t in range(count):
                own[own_base : own_base + n, t * width : (t + 1) * width] = found[t]
        else:
            coded, power = code(found)
            for t in range(count):
                row_outs[k - 1][row_base + t] = coded[t].astype(jnp.int16)
            row_outs[k - 1][row_base + count] = power.astype(jnp.int16)
    for z in range(n_z):
        spot = edge_base + z * tiles
        for side in range(2):
            start = n_row * lb + (z * 2 + (core if side == 0 else 1 - core)) * ifr
            found = []
            for t in range(tiles):
                one = acc[start + 2 * t] if 2 * t < ifr else jnp.zeros(acc.shape[1:], f32)
                two = acc[start + 2 * t + 1] if 2 * t + 1 < ifr else jnp.zeros(acc.shape[1:], f32)
                found.append(folded(one, two))
            if side == 0:
                for t in range(tiles):
                    core_keep[spot + t] = found[t]
            else:
                for t, tile in enumerate(code_edge(found, ifr)):
                    core_send[spot + t] = tile
    if extra:
        for row_out in row_outs:
            row_out[pl.ds(count + 1, count + 1)] = more[0][...]
        core_send[pl.ds(n_z * tiles, tiles)] = more[1][...]


def pair_kernel(n_z, count, extra, ifr, keep, got, pos, *refs):
    refs = list(refs)
    more = refs.pop(0) if extra else None
    own, outs = refs[0], refs[1:]
    tiles = edge_tiles(ifr)
    for k in range(n_z):
        if extra and k > 0:
            outs[k - 1][pl.ds(count * tiles, tiles)] = more[...]
            outs[k - 1][pl.ds((count + 1) * tiles, tiles)] = got[pl.ds(count * n_z * tiles, tiles)]
        z = (pos[1] // 2) ^ k
        for v in range(count):
            spot = (v * n_z + z) * tiles
            there = decode_edge(got, spot, ifr)
            total = [keep[spot + t] + there[t] for t in range(tiles)]
            if k > 0:
                total = code_edge(total, ifr)
            target = own if k == 0 else outs[k - 1]
            for t in range(tiles):
                target[v * tiles + t] = total[t]


def split_halo(refs, n_row, n_z):
    wires = [refs.pop(0) for _ in range(n_row - 1)]
    edges = [refs.pop(0) for _ in range(n_z)]
    return wires, [((edge, 0), (edge, edge.shape[0] // 2)) for edge in edges]


def split_merged(refs, n_row, n_z, ifr):
    wires = [refs.pop(0) for _ in range(n_row - 1)]
    edge, core_got = refs.pop(0), refs.pop(0)
    tiles = edge_tiles(ifr)
    edges = [((edge, 0), (core_got, n_z * tiles))]
    for _ in range(n_z - 1):
        got = refs.pop(0)
        edges.append(((got, tiles), (got, 2 * tiles)))
    return wires, edges


def start_image_kernel(n_row, n_z, ifr, *refs):
    refs = list(refs)
    wires, edges = split_halo(refs, n_row, n_z)
    stored, diagonal, where, pos, x, p, half_x, diag_x, half_p, diag_p, keep, send, halo_x, halo_p, table = refs
    n = x.shape[0]
    for place, (vector, half, diag, halo) in enumerate(((x, half_x, diag_x, halo_x), (p, half_p, diag_p, halo_p))):
        fill_halo(vector, wires, edges, pos, halo, ifr, place)
        forward(halo, pos, stored, diagonal, where, half, diag)
        half[...] = half[...] + 0.5 * diag[...]
    table[0:n, :] = nt(x[...], jnp.concatenate([half_x[...], x[...]], axis=0))
    table[n : 2 * n, :] = nt(p[...], jnp.concatenate([x[...], p[...]], axis=0))
    table[2 * n : 3 * n, :] = nt(p[...], jnp.concatenate([half_p[...], half_x[...]], axis=0))
    table[2 * n : 3 * n, n:] = table[2 * n : 3 * n, n:] + nt(half_p[...], x[...])
    write_halves(table, pos, keep, send)


def take_returned(refs, n_row, n_z):
    own = refs.pop(0)
    rows = [refs.pop(0) for _ in range(n_row - 1)]
    edge_own = refs.pop(0)
    return own, rows, edge_own, [refs.pop(0) for _ in range(n_z - 1)]


def update_kernel(n_row, n_z, *refs):
    refs = list(refs)
    back_parts = take_returned(refs, n_row, n_z)
    mine, other, pos, bnd, x, half, diag, precond, table, ax, energy, w, wire, edge, back = refs
    n = x.shape[0]
    read_halves(mine, other, pos, table)
    ax[...] = half[...] + 0.5 * diag[...]
    returned(0, *back_parts, bnd, back, ax)
    stored, gram = table[0:n, 0:n], table[0:n, n:]
    total = stored + stored.T
    energy[...] = total
    ritz = nn(total, inverse(0.5 * (gram + gram.T)))
    w[...] = precond[...] * (ax[...] - nn(ritz, x[...]))
    write_wire(w, bnd, wire, edge)


def inverse_kernel(table, solved):
    n = solved.shape[0]
    stored = table[2 * n : 3 * n, 0:n]
    solved[...] = inverse(stored + stored.T)


def update_image_kernel(n_row, n_z, ifr, first, *refs):
    refs = list(refs)
    wires, edges = split_merged(refs, n_row, n_z, ifr) if first else split_halo(refs, n_row, n_z)
    stored, diagonal, where, pos, w, x, p, ax, ap, half, diag, keep, send, halo, table = refs
    n = w.shape[0]
    fill_halo(w, wires, edges, pos, halo, ifr, 0, w.shape[1] // halo.shape[2] + 1 if first else 0)
    forward(halo, pos, stored, diagonal, where, half, diag)
    half[...] = half[...] + 0.5 * diag[...]
    here = w[...]
    table[0:n, :] = nt(here, jnp.concatenate([half[...], ap[...]], axis=0))
    table[n : 2 * n, :] = nt(here, jnp.concatenate([ax[...], x[...]], axis=0))
    table[2 * n : 3 * n, :] = nt(here, jnp.concatenate([p[...], here], axis=0))
    if first:
        table[0:n, n:] = table[0:n, n:] + nt(half[...], p[...])
    write_halves(table, pos, keep, send)


def move_kernel(n_row, n_z, total_rows, *refs):
    refs = list(refs)
    start_parts = take_returned(refs, n_row, n_z)
    back_parts = take_returned(refs, n_row, n_z)
    mine, other, pos, bnd, start, energy, pap_inverse, x, p, ax, ap, ap_diag, w, aw, aw_diag, precond = refs[:16]
    x_out, ax_out, w_out, wire, edge, step_x, step_a, small, table, back, ap_full, aw_full = refs[16:]
    n = x.shape[0]
    read_halves(mine, other, pos, table)
    gram = start[0:n, n:]
    px, pp = start[n : 2 * n, 0:n], start[n : 2 * n, n:]
    pax = start[2 * n : 3 * n, n:]
    zw, zp, zwt, zpt, cross, inner, wax, scale = coefficients(
        table, 0.5 * (gram + gram.T), px.T, pp, pax, pap_inverse[...], total_rows
    )
    ap_full[...] = ap[...] + 0.5 * ap_diag[...]
    returned(1, *start_parts, bnd, back, ap_full)
    aw_full[...] = aw[...] + 0.5 * aw_diag[...]
    returned(0, *back_parts, bnd, back, aw_full)
    step_a[...] = nn(zpt, ap_full[...]) + nn(zwt, aw_full[...])
    step_x[...] = nn(zwt, w[...]) + nn(zpt, p[...])
    x_out[...] = nn(scale, x[...] + step_x[...])
    ax_out[...] = nn(scale, ax[...] + step_a[...])
    gain = nn(wax.T, zw) + nn(pax.T, zp)
    gain = 0.5 * (gain + gain.T)
    ritz = nn(scale, nn(energy[...] + gain, scale.T)) / total_rows
    w_out[...] = precond[...] * (ax_out[...] - nn(ritz, x_out[...]))
    write_wire(w_out, bnd, wire, edge)
    small[0:n, :] = -gain
    small[n : 2 * n, :] = cross + inner
    small[2 * n : 3 * n, :] = inner
    small[3 * n : 4 * n, :] = scale


def settle_kernel(small, step_x, step_a, p_out, ap_out, state):
    n = small.shape[1]
    scale = small[3 * n : 4 * n, :]
    scale_t = scale.T
    p_out[...] = nn(scale, step_x[...])
    ap_out[...] = nn(scale, step_a[...])
    state[0:n, :] = inverse(nn(scale, nn(small[0:n, :], scale_t)))
    state[n : 2 * n, :] = nn(scale, nn(small[n : 2 * n, :], scale_t))
    state[2 * n : 3 * n, :] = nn(scale, nn(small[2 * n : 3 * n, :], scale_t))


def finish_kernel(total_rows, mine, other, pos, state, x, p, w, x_out, p_out, table):
    n = x.shape[0]
    read_halves(mine, other, pos, table)
    zw, zp, zwt, zpt, _, _, _, scale = coefficients(
        table,
        unit(n) * total_rows,
        state[n : 2 * n, :],
        state[2 * n : 3 * n, :],
        None,
        state[0:n, :],
        total_rows,
    )
    step = nn(zwt, w[...]) + nn(zpt, p[...])
    x_out[...] = nn(scale, x[...] + step)
    p_out[...] = nn(scale, step)


def run(kernel, name, outs, ins, scratch=(), smem=(), smem_outs=(), flops=1000000):
    in_specs = [pl.BlockSpec(memory_space=SMEM if i in smem else VMEM) for i in range(len(ins))]
    out_specs = [pl.BlockSpec(memory_space=SMEM if i in smem_outs else VMEM) for i in range(len(outs))]
    moved = sum(a.size * a.dtype.itemsize for a in ins) + sum(o.size * o.dtype.itemsize for o in outs)
    return pl.pallas_call(
        kernel,
        name=name,
        out_shape=outs,
        in_specs=in_specs,
        out_specs=out_specs,
        scratch_shapes=list(scratch),
        compiler_params=pltpu.CompilerParams(vmem_limit_bytes=48 * 1024 * 1024),
        cost_estimate=pl.CostEstimate(flops=flops, bytes_accessed=moved, transcendentals=0),
    )(*ins)


def shaped(*shape, dtype=f32):
    return jax.ShapeDtypeStruct(shape, dtype)


def local(n_sub, n_row, modes, search, precond, in_row, in_col, in_val, bnd_rows, if_row, if_src, if_val):
    nin, kb = in_val.shape[2], in_val.shape[3]
    rows, n = modes.shape
    lb = rows // kb
    ifr = bnd_rows.shape[2]
    groups = nin // lb
    n_z = n_sub // 2
    total_rows = float(rows * n_sub * n_row)
    halo_blocks = n_row * lb + n_sub * ifr
    bnd = bnd_rows[0, 0]
    me_row, me_sub = lax.axis_index("row"), lax.axis_index("sub")
    pos = jnp.stack([me_row, me_sub]).astype(jnp.int32)
    after = lax.optimization_barrier

    def row_send(value, k):
        return lax.ppermute(value, "row", [(r, r ^ k) for r in range(n_row)])

    def sub_send(value, k):
        return lax.ppermute(value, "sub", [(s, s ^ k) for s in range(n_sub)])

    tiles = lb // 2
    edges_in = edge_tiles(ifr)

    def coded(count):
        return shaped(count, n, 2 * kb, dtype=jnp.int16)

    def halo_of(own, edge):
        rows_got = [row_send(own, k) for k in range(1, n_row)]
        pair = jnp.concatenate([edge, sub_send(edge, 1)], axis=0)
        return rows_got + [pair] + [sub_send(pair, 2 * k) for k in range(1, n_z)]

    def groups_of_four(value, size, send):
        base = 1
        while base < size:
            got = [value] + [send(value, base * m) for m in range(1, min(4, size // base))]
            while len(got) > 1:
                got = [got[i] + got[i + 1] for i in range(0, len(got), 2)]
            value = got[0]
            base *= 4
        return value

    def z_send(value, k):
        return sub_send(value, 2 * k)

    def sum_halves(keep, send, meanwhile=()):
        total = keep + sub_send(send, 1)
        total = groups_of_four(total, n_z, z_send)
        total, *meanwhile = after((total, *meanwhile))
        total = groups_of_four(total, n_row, row_send)
        return [total, sub_send(total, 1)], meanwhile

    def partials(source, earlier=(), more=()):
        m = 2 if earlier else 1
        e = 1 if more else 0
        outs = [shaped(m * n, rows), shaped(m * n_z * edges_in, n, 2 * kb), coded((m * n_z + e) * edges_in)]
        outs += [coded((m + e) * (tiles + 1))] * (n_row - 1)
        return run(
            functools.partial(partial_kernel, n_row, n_z, m > 1, e > 0, ifr),
            "partials",
            outs,
            [source, joined, where, pos] + list(earlier) + list(more),
            [VMEM((halo_blocks, n, 2 * kb), f32)],
            smem=(2, 3),
        )

    def send_partials(parts, m, more=()):
        own, edge_keep, edge_send, *row_parts = parts
        e = 1 if more else 0
        edge_got = sub_send(edge_send, 1)
        rows_got = [row_send(row_parts[k - 1], k) for k in range(1, n_row)]
        edge_own, *outs = run(
            functools.partial(pair_kernel, n_z, m, e > 0, ifr),
            "pair",
            [shaped(m * edges_in, n, 2 * kb)] + [coded((m + 2 * e) * edges_in)] * (n_z - 1),
            [edge_keep, edge_got, pos] + list(more),
            smem=(2,),
        )
        return [own] + rows_got + [edge_own] + [z_send(outs[k - 1], k) for k in range(1, n_z)], edge_got

    x, p = modes.T, search.T
    scaling = precond.reshape(1, rows)
    wire_shapes = [coded(tiles + 1), coded(edges_in)]
    wire, edge = run(wire_kernel, "wire", [coded(2 * (tiles + 1)), coded(2 * edges_in)], [x, p, bnd], smem=(2,))
    halo = halo_of(wire, edge)
    in_val, if_val, halo[0], halo[-1] = after((in_val, if_val, halo[0], halo[-1]))
    stored, joined, diagonal, where = run(
        functools.partial(prepare_kernel, groups, n_row * lb),
        "prepare",
        [
            shaped(lb, kb, groups * 2 * kb, dtype=bf16),
            shaped(lb, kb, groups * kb, dtype=bf16),
            shaped(lb, kb, 2 * kb, dtype=bf16),
            shaped(lb * groups, dtype=jnp.int32),
        ],
        [in_val[0, 0], if_val[0, 0], in_row[0, 0], in_col[0, 0], if_row[0, 0], if_src[0, 0]],
        smem=(2, 3, 4, 5),
        smem_outs=(3,),
    )
    joined, *halo = after((joined, *halo))
    parts = partials(p, partials(x))
    blocks = [stored, diagonal, where, pos]
    halo_scratch = VMEM((halo_blocks, n, 2 * kb), bf16)
    back_scratch = VMEM((tiles, n, 2 * kb), f32)
    whole = shaped(n, rows)

    table_shape = shaped(3 * n, 2 * n)
    halves_shape = [shaped(3 * n // 2, 2 * n)] * 2
    table_scratch = VMEM((3 * n, 2 * n), f32)
    count = len(halo)
    half_x, diag_x, half_p, diag_p, keep, send = run(
        functools.partial(start_image_kernel, n_row, n_z, ifr),
        "start_image",
        [whole] * 4 + halves_shape,
        halo + blocks + [x, p],
        [halo_scratch, halo_scratch, table_scratch],
        smem=(count + 2, count + 3),
    )
    start_back, _ = send_partials(parts, 2)
    keep, send, *start_back = after((keep, send, *start_back))
    halves, _ = sum_halves(keep, send)
    count = len(start_back)
    table, ax, energy, w, w_wire, w_edge = run(
        functools.partial(update_kernel, n_row, n_z),
        "update",
        [table_shape, whole, shaped(n, n), whole] + wire_shapes,
        start_back + halves + [pos, bnd, x, half_x, diag_x, scaling],
        [back_scratch],
        smem=(count + 2, count + 3),
    )
    (pap_inverse,) = run(inverse_kernel, "pap_inverse", [shaped(n, n)], [table])
    w_back, core_got = send_partials(partials(w, more=[w_wire, w_edge]), 1, [w_edge])
    w_halo = w_back[1:n_row] + [w_edge, core_got] + w_back[n_row + 1 :]

    def update_image(first, halo, w, x, p, ax, ap):
        count = len(halo)
        return run(
            functools.partial(update_image_kernel, n_row, n_z, ifr, first),
            "update_image",
            [whole, whole] + halves_shape,
            halo + blocks + [w, x, p, ax, ap],
            [halo_scratch, table_scratch],
            smem=(count + 2, count + 3),
        )

    half_w, diag_w, keep, send = update_image(True, w_halo, w, x, p, ax, half_p)
    halves, (pap_inverse,) = sum_halves(keep, send, [pap_inverse])
    count = len(start_back) + len(w_back)
    x, ax, w, w_wire, w_edge, step_x, step_a, small = run(
        functools.partial(move_kernel, n_row, n_z, total_rows),
        "move",
        [whole] * 3 + wire_shapes + [whole, whole, shaped(4 * n, n)],
        start_back + w_back + halves + [pos, bnd, table, energy, pap_inverse, x, p, ax, half_p, diag_p, w, half_w, diag_w, scaling],
        [table_scratch, back_scratch, VMEM((n, rows), f32), VMEM((n, rows), f32)],
        smem=(count + 2, count + 3),
    )
    w_halo = halo_of(w_wire, w_edge)
    p, ap, state = run(settle_kernel, "settle", [whole, whole, shaped(3 * n, n)], [small, step_x, step_a])
    _, _, keep, send = update_image(False, w_halo, w, x, p, ax, ap)
    halves, _ = sum_halves(keep, send)
    x, p = run(
        functools.partial(finish_kernel, total_rows),
        "finish",
        [whole, whole],
        halves + [pos, state, x, p, w],
        [table_scratch],
        smem=(2,),
    )
    return (x.T, p.T)


def solution(mesh):
    return jax.shard_map(
        functools.partial(local, mesh.shape["sub"], mesh.shape["row"]),
        mesh=mesh,
        in_specs=(
            P(("sub", "row"), None),
            P(("sub", "row"), None),
            P(("sub", "row")),
            P("sub", "row", None),
            P("sub", "row", None),
            P("sub", "row", None, None, None),
            P("sub", "row", None),
            P("sub", "row", None),
            P("sub", "row", None),
            P("sub", "row", None, None, None),
        ),
        out_specs=(P(("sub", "row"), None), P(("sub", "row"), None)),
        check_vma=False,
    )
```

```python
import functools

import jax
import jax.numpy as jnp
from jax import lax
from jax.experimental import pallas as pl
from jax.experimental.pallas import tpu as pltpu
from jax.sharding import PartitionSpec as P

f32 = jnp.float32
bf16 = jnp.bfloat16
precise_mode = lax.Precision.HIGHEST
VMEM = pltpu.VMEM
SMEM = pltpu.SMEM


def nn(a, b):
    return lax.dot_general(a, b, (((1,), (0,)), ((), ())), precision=precise_mode, preferred_element_type=f32)


def nt(a, b):
    return lax.dot_general(a, b, (((1,), (1,)), ((), ())), precision=precise_mode, preferred_element_type=f32)


TOP = 32000.0
LOG_STEP = 0.08664339756999316


def low_half(shape):
    return lax.broadcasted_iota(jnp.int32, shape, 1) < shape[1] // 2


def swap(tile):
    return pltpu.roll(tile, tile.shape[1] // 2, 1)


def two_blocks(tile):
    low = low_half(tile.shape)
    high = tile.astype(bf16).astype(f32)
    rest = tile - high
    one = jnp.where(low, high, swap(rest))
    two = jnp.where(low, swap(high), rest)
    return one.astype(bf16), two.astype(bf16)


def code(tiles):
    most = jnp.abs(tiles[0])
    for tile in tiles[1:]:
        most = jnp.maximum(most, jnp.abs(tile))
    most = jnp.maximum(jnp.max(most, axis=1, keepdims=True), 1e-30)
    power = jnp.broadcast_to(jnp.ceil(jnp.log(most) * (1.0 / LOG_STEP)), tiles[0].shape)
    factor = TOP * jnp.exp(power * -LOG_STEP)
    return [jnp.floor(tile * factor + 0.5).astype(jnp.int32) for tile in tiles], power.astype(jnp.int32)


def step_of(power):
    return jnp.exp(power.astype(jnp.int32).astype(f32) * LOG_STEP) * (1.0 / TOP)


def decode(tile, step):
    return tile.astype(jnp.int32).astype(f32) * step


def edge_tiles(ifr):
    return ifr // 2 + 1


def code_edge(tiles, ifr):
    low = low_half(tiles[0].shape)
    tiles = list(tiles)
    tiles[-1] = jnp.where(low, tiles[-1], 0.0) if ifr % 2 else jnp.zeros_like(tiles[-1])
    coded, power = code(tiles)
    coded[-1] = jnp.where(low, coded[-1], power) if ifr % 2 else power
    return [tile.astype(jnp.int16) for tile in coded]


def decode_edge(ref, start, ifr):
    tiles = [ref[start + t].astype(jnp.int32) for t in range(edge_tiles(ifr))]
    low = low_half(tiles[-1].shape)
    power = jnp.where(low, swap(tiles[-1]), tiles[-1]) if ifr % 2 else tiles[-1]
    step = step_of(power)
    return [tile.astype(f32) * step for tile in tiles]


def write_wire(vector, bnd, wire, edge, place=0):
    ifr = bnd.shape[0]
    width = wire.shape[2]
    count = vector.shape[1] // width
    base = place * (count + 1)
    coded, power = code([vector[:, t * width : (t + 1) * width] for t in range(count)])
    for t in range(count):
        wire[base + t] = coded[t].astype(jnp.int16)
    wire[base + count] = power.astype(jnp.int16)
    low = low_half(power.shape)
    slots = []
    for q in range(ifr):
        tile = wire[base + bnd[q] // 2].astype(jnp.int32)
        side = jnp.broadcast_to(bnd[q] % 2, tile.shape)
        slots.append(jnp.where(side == q % 2, tile, swap(tile)))
    slots.append(power)
    if len(slots) % 2:
        slots.append(power)
    for t in range(edge_tiles(ifr)):
        edge[place * edge_tiles(ifr) + t] = jnp.where(low, slots[2 * t], slots[2 * t + 1]).astype(jnp.int16)


def fill_halo(vector, wires, edges, pos, halo, ifr, place=0, base=0):
    width = halo.shape[2]
    count = vector.shape[1] // width
    lb = 2 * count
    n_row = len(wires) + 1
    for t in range(count):
        one, two = two_blocks(vector[:, t * width : (t + 1) * width])
        halo[pos[0] * lb + 2 * t] = one
        halo[pos[0] * lb + 2 * t + 1] = two
    for k, wire in enumerate(wires):
        start = (pos[0] ^ (k + 1)) * lb
        spot = base + place * (count + 1)
        step = step_of(wire[spot + count])
        for t in range(count):
            one, two = two_blocks(decode(wire[spot + t], step))
            halo[start + 2 * t] = one
            halo[start + 2 * t + 1] = two
    tiles = edge_tiles(ifr)
    for k, pair in enumerate(edges):
        for other, (edge, spot) in enumerate(pair):
            start = n_row * lb + (((pos[1] // 2) ^ k) * 2 + ((pos[1] % 2) ^ other)) * ifr
            found = decode_edge(edge, spot + place * tiles, ifr)
            for q in range(0, ifr, 2):
                blocks = two_blocks(found[q // 2])
                halo[start + q] = blocks[0]
                if q + 1 < ifr:
                    halo[start + q + 1] = blocks[1]


def write_halves(table, pos, keep, send):
    height = keep.shape[0]
    core = pos[1] % 2
    keep[...] = table[pl.ds(pl.multiple_of(core * height, 8), height), :]
    send[...] = table[pl.ds(pl.multiple_of((1 - core) * height, 8), height), :]


def read_halves(mine, other, pos, table):
    height = mine.shape[0]
    core = pos[1] % 2
    table[pl.ds(pl.multiple_of(core * height, 8), height), :] = mine[...]
    table[pl.ds(pl.multiple_of((1 - core) * height, 8), height), :] = other[...]


def forward(halo, pos, stored, diagonal, where, out, diag_out):
    lb, kb = stored.shape[0], stored.shape[1]
    own = pos[0] * lb
    groups = stored.shape[2] // (2 * kb)
    for i in range(0, lb, 2):
        sums, diags = [], []
        for m in (i, i + 1):
            row = jnp.concatenate([halo[where[m * groups + g]] for g in range(groups)], axis=1)
            sums.append(lax.dot_general(row, stored[m], (((1,), (1,)), ((), ())), preferred_element_type=f32))
            diags.append(lax.dot_general(halo[own + m], diagonal[m], (((1,), (1,)), ((), ())), preferred_element_type=f32))
        out[:, i * kb : (i + 2) * kb] = jnp.concatenate(sums, axis=1)
        diag_out[:, i * kb : (i + 2) * kb] = jnp.concatenate(diags, axis=1)


def returned(index, own, rows, edge_own, edges, bnd, back, target):
    count, _, width = back.shape
    ifr = bnd.shape[0]
    tiles = edge_tiles(ifr)
    n = target.shape[0]
    steps = [step_of(row[index * (count + 1) + count]) for row in rows]
    for t in range(count):
        total = own[index * n : (index + 1) * n, t * width : (t + 1) * width]
        for row, step in zip(rows, steps):
            total = total + decode(row[index * (count + 1) + t], step)
        back[t] = total
    found = [edge_own[index * tiles + t] for t in range(tiles)]
    for edge in edges:
        found = [a + b for a, b in zip(found, decode_edge(edge, index * tiles, ifr))]
    low = low_half(back.shape[1:])
    for q in range(ifr):
        side = jnp.broadcast_to(bnd[q] % 2, low.shape)
        block = jnp.where(side == q % 2, found[q // 2], swap(found[q // 2]))
        spot = bnd[q] // 2
        back[spot] = back[spot] + jnp.where(low == (side == 0), block, 0.0)
    for t in range(count):
        span = slice(t * width, (t + 1) * width)
        target[:, span] = target[:, span] + back[t]


def unit(order):
    return (
        lax.broadcasted_iota(jnp.int32, (order, order), 0) == lax.broadcasted_iota(jnp.int32, (order, order), 1)
    ).astype(f32)


def eliminate(matrix, right, full):
    order = matrix.shape[0]
    held = matrix * unit(order)
    down = 1.0 / jnp.sqrt(jnp.sum(held, axis=1, keepdims=True))
    across = 1.0 / jnp.sqrt(jnp.sum(held, axis=0, keepdims=True))
    table = jnp.concatenate([matrix * across, right], axis=1) * down
    rows = lax.broadcasted_iota(jnp.int32, table.shape, 0)
    for j in range(0, order, 2):
        left = jnp.broadcast_to(table[:, j : j + 1], table.shape)
        beside = jnp.broadcast_to(table[:, j + 1 : j + 2], table.shape)
        one, two = table[j : j + 1, :], table[j + 1 : j + 2, :]
        a, b = left[j : j + 1, :], beside[j : j + 1, :]
        c, d = left[j + 1 : j + 2, :], beside[j + 1 : j + 2, :]
        scale = 1.0 / (a * d - b * c)
        first = (d * one - b * two) * scale
        second = (a * two - c * one) * scale
        moved = table - left * first - beside * second
        if full:
            table = jnp.where(rows == j, first, jnp.where(rows == j + 1, second, moved))
        else:
            table = jnp.where(rows > j + 1, moved, jnp.where(rows == j + 1, two - (c / a) * one, table))
    if full:
        return table[:, order:] * down
    pivots = jnp.sum(table[:, :order] * unit(order), axis=1, keepdims=True)
    return table[:, order:] * (1.0 / jnp.sqrt(pivots))


def inverse(matrix):
    return eliminate(matrix, unit(matrix.shape[0]), True)


def cholesky_inverse(matrix):
    return eliminate(matrix, unit(matrix.shape[0]), False)


def coefficients(table, gram, xp, pp, pax, pap_inverse, total_rows):
    n = gram.shape[0]
    waw, wap = table[0:n, :n], table[0:n, n:]
    wax, wx = table[n : 2 * n, :n], table[n : 2 * n, n:]
    wp, ww = table[2 * n : 3 * n, :n], table[2 * n : 3 * n, n:]
    waw = waw + waw.T
    first = nn(pap_inverse, wap.T)
    if pax is None:
        rhs = -wax
    else:
        second = nn(pap_inverse, pax)
        rhs = nn(wap, second) - wax
    schur = waw - nn(wap, first)
    zw = eliminate(schur, rhs, True)
    zp = -nn(first, zw)
    if pax is not None:
        zp = zp - second
    cross = nn(wx.T, zw) + nn(xp, zp)
    zwt, zpt = zw.T, zp.T
    inner = nn(zwt, nn(ww, zw) + nn(wp, zp)) + nn(zpt, nn(wp.T, zw) + nn(pp, zp))
    lengths = (gram + cross + cross.T + inner) / total_rows
    return zw, zp, zwt, zpt, cross, inner, wax, cholesky_inverse(lengths)


def prepare_kernel(groups, base, vals, faces, rows, cols, face_rows, face_src, stored, joined, diagonal, where):
    lb, kb = faces.shape[0], faces.shape[1]

    def twice(block):
        wide = block.astype(f32)
        return jnp.concatenate([wide, wide], axis=1).astype(bf16)

    for k in range(lb):
        diagonal[k] = twice(vals[k])
    for g in range(groups):
        half = (g % 2) * kb
        for m in range(lb):
            if g < groups - 1:
                k = (g + 1) * lb + m
                i, target, block = rows[k], cols[k], twice(vals[k])
            else:
                i, target, block = face_rows[m], base + face_src[m], twice(faces[m])
            stored[i, :, 2 * kb * g : 2 * kb * (g + 1)] = block
            joined[i, :, kb * g : kb * (g + 1)] = block[:, half : half + kb]
            where[i * groups + g] = target


def wire_kernel(x, p, bnd, wire, edge):
    write_wire(x, bnd, wire, edge, 0)
    write_wire(p, bnd, wire, edge, 1)


def partial_kernel(n_row, n_z, merge, extra, ifr, vector, joined, where, pos, *refs):
    refs = list(refs)
    parts = n_row + 2
    earlier = [refs.pop(0) for _ in range(parts)] if merge else []
    more = [refs.pop(0) for _ in range(2)] if extra else []
    outs, acc = refs[:-1], refs[-1]
    own, core_keep, core_send, *row_outs = outs
    width = acc.shape[2]
    count = vector.shape[1] // width
    lb, kb, n = 2 * count, joined.shape[1], vector.shape[0]
    tiles = edge_tiles(ifr)
    groups = joined.shape[2] // kb
    low = low_half(acc.shape[1:])
    core = pos[1] % 2
    for source, target in zip(earlier, outs):
        target[pl.ds(0, source.shape[0])] = source[...]
    own_base = n if merge else 0
    row_base = count + 1 if merge else 0
    edge_base = n_z * tiles if merge else 0
    acc[...] = jnp.zeros(acc.shape, f32)
    for pair in range(count):
        both = two_blocks(vector[:, pair * width : (pair + 1) * width])
        for m in range(2):
            i = 2 * pair + m
            blocks = jnp.concatenate([joined[i], joined[i]], axis=0)
            out = jnp.dot(both[m], blocks, preferred_element_type=f32)
            for t in range(groups // 2):
                tile = out[:, width * t : width * (t + 1)]
                one = where[i * groups + 2 * t]
                two = where[i * groups + 2 * t + 1]
                acc[one] = acc[one] + jnp.where(low, tile, 0.0)
                acc[two] = acc[two] + jnp.where(low, 0.0, tile)

    def folded(one, two):
        return jnp.where(low, one, two) + swap(jnp.where(low, two, one))

    for k in range(n_row):
        start = (pos[0] ^ k) * lb
        found = [folded(acc[start + 2 * t], acc[start + 2 * t + 1]) for t in range(count)]
        if k == 0:
            for t in range(count):
                own[own_base : own_base + n, t * width : (t + 1) * width] = found[t]
        else:
            coded, power = code(found)
            for t in range(count):
                row_outs[k - 1][row_base + t] = coded[t].astype(jnp.int16)
            row_outs[k - 1][row_base + count] = power.astype(jnp.int16)
    for z in range(n_z):
        spot = edge_base + z * tiles
        for side in range(2):
            start = n_row * lb + (z * 2 + (core if side == 0 else 1 - core)) * ifr
            found = []
            for t in range(tiles):
                one = acc[start + 2 * t] if 2 * t < ifr else jnp.zeros(acc.shape[1:], f32)
                two = acc[start + 2 * t + 1] if 2 * t + 1 < ifr else jnp.zeros(acc.shape[1:], f32)
                found.append(folded(one, two))
            if side == 0:
                for t in range(tiles):
                    core_keep[spot + t] = found[t]
            else:
                for t, tile in enumerate(code_edge(found, ifr)):
                    core_send[spot + t] = tile
    if extra:
        for row_out in row_outs:
            row_out[pl.ds(count + 1, count + 1)] = more[0][...]
        core_send[pl.ds(n_z * tiles, tiles)] = more[1][...]


def pair_kernel(n_z, count, extra, ifr, keep, got, pos, *refs):
    refs = list(refs)
    more = refs.pop(0) if extra else None
    own, outs = refs[0], refs[1:]
    tiles = edge_tiles(ifr)
    for k in range(n_z):
        if extra and k > 0:
            outs[k - 1][pl.ds(count * tiles, tiles)] = more[...]
            outs[k - 1][pl.ds((count + 1) * tiles, tiles)] = got[pl.ds(count * n_z * tiles, tiles)]
        z = (pos[1] // 2) ^ k
        for v in range(count):
            spot = (v * n_z + z) * tiles
            there = decode_edge(got, spot, ifr)
            total = [keep[spot + t] + there[t] for t in range(tiles)]
            if k > 0:
                total = code_edge(total, ifr)
            target = own if k == 0 else outs[k - 1]
            for t in range(tiles):
                target[v * tiles + t] = total[t]


def split_halo(refs, n_row, n_z):
    wires = [refs.pop(0) for _ in range(n_row - 1)]
    edges = [refs.pop(0) for _ in range(n_z)]
    return wires, [((edge, 0), (edge, edge.shape[0] // 2)) for edge in edges]


def split_merged(refs, n_row, n_z, ifr):
    wires = [refs.pop(0) for _ in range(n_row - 1)]
    edge, core_got = refs.pop(0), refs.pop(0)
    tiles = edge_tiles(ifr)
    edges = [((edge, 0), (core_got, n_z * tiles))]
    for _ in range(n_z - 1):
        got = refs.pop(0)
        edges.append(((got, tiles), (got, 2 * tiles)))
    return wires, edges


def start_image_kernel(n_row, n_z, ifr, *refs):
    refs = list(refs)
    wires, edges = split_halo(refs, n_row, n_z)
    stored, diagonal, where, pos, x, p, half_x, diag_x, half_p, diag_p, keep, send, halo_x, halo_p, table = refs
    n = x.shape[0]
    for place, (vector, half, diag, halo) in enumerate(((x, half_x, diag_x, halo_x), (p, half_p, diag_p, halo_p))):
        fill_halo(vector, wires, edges, pos, halo, ifr, place)
        forward(halo, pos, stored, diagonal, where, half, diag)
        half[...] = half[...] + 0.5 * diag[...]
    table[0:n, :] = nt(x[...], jnp.concatenate([half_x[...], x[...]], axis=0))
    table[n : 2 * n, :] = nt(p[...], jnp.concatenate([x[...], p[...]], axis=0))
    table[2 * n : 3 * n, :] = nt(p[...], jnp.concatenate([half_p[...], half_x[...]], axis=0))
    table[2 * n : 3 * n, n:] = table[2 * n : 3 * n, n:] + nt(half_p[...], x[...])
    write_halves(table, pos, keep, send)


def take_returned(refs, n_row, n_z):
    own = refs.pop(0)
    rows = [refs.pop(0) for _ in range(n_row - 1)]
    edge_own = refs.pop(0)
    return own, rows, edge_own, [refs.pop(0) for _ in range(n_z - 1)]


def update_kernel(n_row, n_z, *refs):
    refs = list(refs)
    back_parts = take_returned(refs, n_row, n_z)
    mine, other, pos, bnd, x, half, diag, precond, table, ax, energy, w, wire, edge, back = refs
    n = x.shape[0]
    read_halves(mine, other, pos, table)
    ax[...] = half[...] + 0.5 * diag[...]
    returned(0, *back_parts, bnd, back, ax)
    stored, gram = table[0:n, 0:n], table[0:n, n:]
    total = stored + stored.T
    energy[...] = total
    ritz = nn(total, inverse(0.5 * (gram + gram.T)))
    w[...] = precond[...] * (ax[...] - nn(ritz, x[...]))
    write_wire(w, bnd, wire, edge)


def inverse_kernel(table, solved):
    n = solved.shape[0]
    stored = table[2 * n : 3 * n, 0:n]
    solved[...] = inverse(stored + stored.T)


def update_image_kernel(n_row, n_z, ifr, first, *refs):
    refs = list(refs)
    wires, edges = split_merged(refs, n_row, n_z, ifr) if first else split_halo(refs, n_row, n_z)
    stored, diagonal, where, pos, w, x, p, ax, ap, half, diag, keep, send, halo, table = refs
    n = w.shape[0]
    fill_halo(w, wires, edges, pos, halo, ifr, 0, w.shape[1] // halo.shape[2] + 1 if first else 0)
    forward(halo, pos, stored, diagonal, where, half, diag)
    half[...] = half[...] + 0.5 * diag[...]
    here = w[...]
    table[0:n, :] = nt(here, jnp.concatenate([half[...], ap[...]], axis=0))
    table[n : 2 * n, :] = nt(here, jnp.concatenate([ax[...], x[...]], axis=0))
    table[2 * n : 3 * n, :] = nt(here, jnp.concatenate([p[...], here], axis=0))
    if first:
        table[0:n, n:] = table[0:n, n:] + nt(half[...], p[...])
    write_halves(table, pos, keep, send)


def move_kernel(n_row, n_z, total_rows, *refs):
    refs = list(refs)
    start_parts = take_returned(refs, n_row, n_z)
    back_parts = take_returned(refs, n_row, n_z)
    mine, other, pos, bnd, start, energy, pap_inverse, x, p, ax, ap, ap_diag, w, aw, aw_diag, precond = refs[:16]
    x_out, ax_out, w_out, wire, edge, step_x, step_a, small, table, back, ap_full, aw_full = refs[16:]
    n = x.shape[0]
    read_halves(mine, other, pos, table)
    gram = start[0:n, n:]
    px, pp = start[n : 2 * n, 0:n], start[n : 2 * n, n:]
    pax = start[2 * n : 3 * n, n:]
    zw, zp, zwt, zpt, cross, inner, wax, scale = coefficients(
        table, 0.5 * (gram + gram.T), px.T, pp, pax, pap_inverse[...], total_rows
    )
    ap_full[...] = ap[...] + 0.5 * ap_diag[...]
    returned(1, *start_parts, bnd, back, ap_full)
    aw_full[...] = aw[...] + 0.5 * aw_diag[...]
    returned(0, *back_parts, bnd, back, aw_full)
    step_a[...] = nn(zpt, ap_full[...]) + nn(zwt, aw_full[...])
    step_x[...] = nn(zwt, w[...]) + nn(zpt, p[...])
    x_out[...] = nn(scale, x[...] + step_x[...])
    ax_out[...] = nn(scale, ax[...] + step_a[...])
    gain = nn(wax.T, zw) + nn(pax.T, zp)
    gain = 0.5 * (gain + gain.T)
    ritz = nn(scale, nn(energy[...] + gain, scale.T)) / total_rows
    w_out[...] = precond[...] * (ax_out[...] - nn(ritz, x_out[...]))
    write_wire(w_out, bnd, wire, edge)
    small[0:n, :] = -gain
    small[n : 2 * n, :] = cross + inner
    small[2 * n : 3 * n, :] = inner
    small[3 * n : 4 * n, :] = scale


def settle_kernel(small, step_x, step_a, p_out, ap_out, state):
    n = small.shape[1]
    scale = small[3 * n : 4 * n, :]
    scale_t = scale.T
    p_out[...] = nn(scale, step_x[...])
    ap_out[...] = nn(scale, step_a[...])
    state[0:n, :] = inverse(nn(scale, nn(small[0:n, :], scale_t)))
    state[n : 2 * n, :] = nn(scale, nn(small[n : 2 * n, :], scale_t))
    state[2 * n : 3 * n, :] = nn(scale, nn(small[2 * n : 3 * n, :], scale_t))


def finish_kernel(total_rows, mine, other, pos, state, x, p, w, x_out, p_out, table):
    n = x.shape[0]
    read_halves(mine, other, pos, table)
    zw, zp, zwt, zpt, _, _, _, scale = coefficients(
        table,
        unit(n) * total_rows,
        state[n : 2 * n, :],
        state[2 * n : 3 * n, :],
        None,
        state[0:n, :],
        total_rows,
    )
    step = nn(zwt, w[...]) + nn(zpt, p[...])
    x_out[...] = nn(scale, x[...] + step)
    p_out[...] = nn(scale, step)


def run(kernel, name, outs, ins, scratch=(), smem=(), smem_outs=(), flops=1000000):
    in_specs = [pl.BlockSpec(memory_space=SMEM if i in smem else VMEM) for i in range(len(ins))]
    out_specs = [pl.BlockSpec(memory_space=SMEM if i in smem_outs else VMEM) for i in range(len(outs))]
    moved = sum(a.size * a.dtype.itemsize for a in ins) + sum(o.size * o.dtype.itemsize for o in outs)
    return pl.pallas_call(
        kernel,
        name=name,
        out_shape=outs,
        in_specs=in_specs,
        out_specs=out_specs,
        scratch_shapes=list(scratch),
        compiler_params=pltpu.CompilerParams(vmem_limit_bytes=48 * 1024 * 1024),
        cost_estimate=pl.CostEstimate(flops=flops, bytes_accessed=moved, transcendentals=0),
    )(*ins)


def shaped(*shape, dtype=f32):
    return jax.ShapeDtypeStruct(shape, dtype)


def local(n_sub, n_row, modes, search, precond, in_row, in_col, in_val, bnd_rows, if_row, if_src, if_val):
    nin, kb = in_val.shape[2], in_val.shape[3]
    rows, n = modes.shape
    lb = rows // kb
    ifr = bnd_rows.shape[2]
    groups = nin // lb
    n_z = n_sub // 2
    total_rows = float(rows * n_sub * n_row)
    halo_blocks = n_row * lb + n_sub * ifr
    bnd = bnd_rows[0, 0]
    me_row, me_sub = lax.axis_index("row"), lax.axis_index("sub")
    pos = jnp.stack([me_row, me_sub]).astype(jnp.int32)
    after = lax.optimization_barrier

    def row_send(value, k):
        return lax.ppermute(value, "row", [(r, r ^ k) for r in range(n_row)])

    def sub_send(value, k):
        return lax.ppermute(value, "sub", [(s, s ^ k) for s in range(n_sub)])

    tiles = lb // 2
    edges_in = edge_tiles(ifr)

    def coded(count):
        return shaped(count, n, 2 * kb, dtype=jnp.int16)

    def halo_of(own, edge):
        rows_got = [row_send(own, k) for k in range(1, n_row)]
        pair = jnp.concatenate([edge, sub_send(edge, 1)], axis=0)
        return rows_got + [pair] + [sub_send(pair, 2 * k) for k in range(1, n_z)]

    def groups_of_four(value, size, send):
        base = 1
        while base < size:
            got = [value] + [send(value, base * m) for m in range(1, min(4, size // base))]
            while len(got) > 1:
                got = [got[i] + got[i + 1] for i in range(0, len(got), 2)]
            value = got[0]
            base *= 4
        return value

    def z_send(value, k):
        return sub_send(value, 2 * k)

    def sum_halves(keep, send, meanwhile=()):
        total = keep + sub_send(send, 1)
        total = groups_of_four(total, n_z, z_send)
        total, *meanwhile = after((total, *meanwhile))
        total = groups_of_four(total, n_row, row_send)
        return [total, sub_send(total, 1)], meanwhile

    def partials(source, earlier=(), more=()):
        m = 2 if earlier else 1
        e = 1 if more else 0
        outs = [shaped(m * n, rows), shaped(m * n_z * edges_in, n, 2 * kb), coded((m * n_z + e) * edges_in)]
        outs += [coded((m + e) * (tiles + 1))] * (n_row - 1)
        return run(
            functools.partial(partial_kernel, n_row, n_z, m > 1, e > 0, ifr),
            "partials",
            outs,
            [source, joined, where, pos] + list(earlier) + list(more),
            [VMEM((halo_blocks, n, 2 * kb), f32)],
            smem=(2, 3),
        )

    def send_partials(parts, m, more=()):
        own, edge_keep, edge_send, *row_parts = parts
        e = 1 if more else 0
        edge_got = sub_send(edge_send, 1)
        rows_got = [row_send(row_parts[k - 1], k) for k in range(1, n_row)]
        edge_own, *outs = run(
            functools.partial(pair_kernel, n_z, m, e > 0, ifr),
            "pair",
            [shaped(m * edges_in, n, 2 * kb)] + [coded((m + 2 * e) * edges_in)] * (n_z - 1),
            [edge_keep, edge_got, pos] + list(more),
            smem=(2,),
        )
        return [own] + rows_got + [edge_own] + [z_send(outs[k - 1], k) for k in range(1, n_z)], edge_got

    x, p = modes.T, search.T
    scaling = precond.reshape(1, rows)
    wire_shapes = [coded(tiles + 1), coded(edges_in)]
    wire, edge = run(wire_kernel, "wire", [coded(2 * (tiles + 1)), coded(2 * edges_in)], [x, p, bnd], smem=(2,))
    halo = halo_of(wire, edge)
    in_val, if_val, halo[0], halo[-1] = after((in_val, if_val, halo[0], halo[-1]))
    stored, joined, diagonal, where = run(
        functools.partial(prepare_kernel, groups, n_row * lb),
        "prepare",
        [
            shaped(lb, kb, groups * 2 * kb, dtype=bf16),
            shaped(lb, kb, groups * kb, dtype=bf16),
            shaped(lb, kb, 2 * kb, dtype=bf16),
            shaped(lb * groups, dtype=jnp.int32),
        ],
        [in_val[0, 0], if_val[0, 0], in_row[0, 0], in_col[0, 0], if_row[0, 0], if_src[0, 0]],
        smem=(2, 3, 4, 5),
        smem_outs=(3,),
    )
    joined, *halo = after((joined, *halo))
    parts = partials(p, partials(x))
    blocks = [stored, diagonal, where, pos]
    halo_scratch = VMEM((halo_blocks, n, 2 * kb), bf16)
    back_scratch = VMEM((tiles, n, 2 * kb), f32)
    whole = shaped(n, rows)

    table_shape = shaped(3 * n, 2 * n)
    halves_shape = [shaped(3 * n // 2, 2 * n)] * 2
    table_scratch = VMEM((3 * n, 2 * n), f32)
    count = len(halo)
    half_x, diag_x, half_p, diag_p, keep, send = run(
        functools.partial(start_image_kernel, n_row, n_z, ifr),
        "start_image",
        [whole] * 4 + halves_shape,
        halo + blocks + [x, p],
        [halo_scratch, halo_scratch, table_scratch],
        smem=(count + 2, count + 3),
    )
    start_back, _ = send_partials(parts, 2)
    keep, send, *start_back = after((keep, send, *start_back))
    halves, _ = sum_halves(keep, send)
    count = len(start_back)
    table, ax, energy, w, w_wire, w_edge = run(
        functools.partial(update_kernel, n_row, n_z),
        "update",
        [table_shape, whole, shaped(n, n), whole] + wire_shapes,
        start_back + halves + [pos, bnd, x, half_x, diag_x, scaling],
        [back_scratch],
        smem=(count + 2, count + 3),
    )
    (pap_inverse,) = run(inverse_kernel, "pap_inverse", [shaped(n, n)], [table])
    w_back, core_got = send_partials(partials(w, more=[w_wire, w_edge]), 1, [w_edge])
    w_halo = w_back[1:n_row] + [w_edge, core_got] + w_back[n_row + 1 :]

    def update_image(first, halo, w, x, p, ax, ap):
        count = len(halo)
        return run(
            functools.partial(update_image_kernel, n_row, n_z, ifr, first),
            "update_image",
            [whole, whole] + halves_shape,
            halo + blocks + [w, x, p, ax, ap],
            [halo_scratch, table_scratch],
            smem=(count + 2, count + 3),
        )

    half_w, diag_w, keep, send = update_image(True, w_halo, w, x, p, ax, half_p)
    halves, (pap_inverse,) = sum_halves(keep, send, [pap_inverse])
    count = len(start_back) + len(w_back)
    x, ax, w, w_wire, w_edge, step_x, step_a, small = run(
        functools.partial(move_kernel, n_row, n_z, total_rows),
        "move",
        [whole] * 3 + wire_shapes + [whole, whole, shaped(4 * n, n)],
        start_back + w_back + halves + [pos, bnd, table, energy, pap_inverse, x, p, ax, half_p, diag_p, w, half_w, diag_w, scaling],
        [table_scratch, back_scratch, VMEM((n, rows), f32), VMEM((n, rows), f32)],
        smem=(count + 2, count + 3),
    )
    w_halo = halo_of(w_wire, w_edge)
    p, ap, state = run(settle_kernel, "settle", [whole, whole, shaped(3 * n, n)], [small, step_x, step_a])
    _, _, keep, send = update_image(False, w_halo, w, x, p, ax, ap)
    halves, _ = sum_halves(keep, send)
    x, p = run(
        functools.partial(finish_kernel, total_rows),
        "finish",
        [whole, whole],
        halves + [pos, state, x, p, w],
        [table_scratch],
        smem=(2,),
    )
    return (x.T, p.T)


def solution(mesh):
    return jax.shard_map(
        functools.partial(local, mesh.shape["sub"], mesh.shape["row"]),
        mesh=mesh,
        in_specs=(
            P(("sub", "row"), None),
            P(("sub", "row"), None),
            P(("sub", "row")),
            P("sub", "row", None),
            P("sub", "row", None),
            P("sub", "row", None, None, None),
            P("sub", "row", None),
            P("sub", "row", None),
            P("sub", "row", None),
            P("sub", "row", None, None, None),
        ),
        out_specs=(P(("sub", "row"), None), P(("sub", "row"), None)),
        check_vma=False,
    )
```
